32 devices in a mesh: grp: 2 (over y), orb: 4 (over z), row: 4 (over x, core).
Axes of the slice: x: 2, y: 2, z: 4, core: 2. Of those that a mesh axis runs over, the one named last changes fastest.
Arguments:
- half_tensor: bfloat16 [512, 64, 2048], P(('grp', 'orb'), 'row'), parts along dimension 0, may hold values from -0.75 to 0.75
- batch_owner: int32 [128, 1], P(('grp', 'row')), parts along dimension 0, may hold values from 0 to 3; in each aligned block of 16 rows (0 to 15, 16 to 31, ...) at most 8 rows name the same one
- pair_list: int32 [8, 64], P(('grp', 'orb')), parts along dimension 0, may hold values from 0 to 135, as said below
- live_pairs: int32 [8], P(('grp', 'orb')), parts along dimension 0, may hold values from 32 to 64, as said below
Outputs:
- exchange_blocks: bfloat16 [8, 64, 128, 128], P(('grp', 'orb'), 'row'), parts along dimension 0
The draws below stay inside these ranges and needn't reach their ends.
There are 2 independent parts, one for each index of `grp`. The reference program is written for one: setup_inputs(seed, part) draws one part's arguments, and reference() takes and returns one part's arrays. A program takes and returns all parts, laid end to end along the dimension named above; each array names one. Nothing has to cross between parts.
Inputs may be any that keep to these rules, and one draw needn't show every extreme that they name: `batch_owner`: among the 16 orbitals of one index of row, no batch holds more than 8. `pair_list`: each batch lists 64 distinct pair codes. Only the first live_pairs[b] codes of batch b are used; some batch uses all 64.
All inputs are finite; a program needn't handle non-finite values.
Results may differ from the reference program's by a relative error of at most 0.008.
Values may be sent and summed in bfloat16 or wider, within the bound.
No kernel may reach another device: no remote copies, remote signals or barrier semaphores. Data moves between devices by JAX's collectives and lax.ppermute only.
A program may use at most 64 MiB of HBM per device.

```python
import math
import jax
import jax.numpy as jnp
import numpy as np
from jax import lax

AUX = 256
TILE = 128
DB = 16
CAP = 8
NPAIR = 64
NBATCH = 4
NOCC = 64
OCC_R = 16
DOM = 2048
N_ROW = 4


def draw_pair_list(key, part):
    key = jax.random.fold_in(key, 11)
    batch_keys = jax.random.split(key, NBATCH)
    orders = jax.vmap(lambda each_key: jax.random.permutation(each_key, DB * (DB + 1) // 2))(batch_keys)
    return orders[:, :NPAIR].astype(jnp.int32)


def draw_live_pairs(key, part):
    key = jax.random.fold_in(key, 23)
    count_key, full_key = jax.random.split(key)
    counts = jax.random.randint(count_key, (NBATCH,), NPAIR // 2, NPAIR + 1)
    full_batch = jax.random.randint(full_key, (), 0, NBATCH)
    batch_ids = jnp.arange(NBATCH, dtype=jnp.int32)
    return jnp.where(batch_ids == full_batch, NPAIR, counts).astype(jnp.int32)


def levels(key, shape, cuts, least, top_value):
    factor_of, own = 1.0, jax.random.fold_in(key, 6)
    for axis_at, parts in cuts:
        steps = jnp.exp(jax.random.uniform(jax.random.fold_in(own, axis_at), (parts,), jnp.float32, least / len(cuts), top_value / len(cuts)))
        factor_of = factor_of * jnp.repeat(steps, shape[axis_at] // parts).reshape([-1 if axis == axis_at else 1 for axis in range(len(shape))])
    return factor_of


def deal_out(rng, own, number, rows, number_of, top, bound, slope):
    order = jax.random.permutation(rng, number_of)
    packed, ordinary = shares(number_of, rows * top, bound, slope, True), shares(number_of, rows * top, bound, slope, False)
    places = jnp.arange(number_of)

    def named(lengths, rotation):
        used = int((lengths > 0).sum())
        fixed = max(1, used // 4)
        moved = fixed + (places - fixed + rotation * (used - fixed)) % max(1, number_of - fixed)
        return jnp.zeros((number_of,), jnp.int32).at[order[jnp.where(places < fixed, places, moved)]].set(jnp.asarray(lengths, jnp.int32))

    lengths = jnp.where(number % 4 == 0, named(packed, number // 4), named(ordinary, number - number // 4 - 1))
    mixed = jax.random.permutation(jax.random.fold_in(own, 3), number_of)
    source_of, taker = mixed[0:number_of // 2 * 2:2], mixed[1:number_of // 2 * 2:2]
    slack = jnp.minimum(lengths[source_of] - 1, bound - lengths[taker]) // 2
    slack = jnp.where((source_of == order[0]) | (taker == order[0]) | (lengths[taker] == 0), 0, jnp.maximum(slack, 0))
    moved = jax.random.randint(jax.random.fold_in(own, 4), (number_of // 2,), 0, 1 << 20) % (slack + 1)
    lengths = lengths.at[source_of].add(-moved).at[taker].add(moved)
    items = jnp.searchsorted(jnp.cumsum(lengths), jnp.arange(rows * top), side="right").astype(jnp.int32)
    listing = items.reshape(top, rows).T
    listing = listing[jax.random.permutation(jax.random.fold_in(own, 1), rows)]
    rotation = jax.random.randint(jax.random.fold_in(own, 2), (rows, 1), 0, top)
    return jnp.take_along_axis(listing, (jnp.arange(top)[None, :] + rotation) % top, axis=1)


def shares(amount, total, most, lean, full):
    loads = [(1 << 20) // math.isqrt(standing ** lean) + 1 for standing in range(1, amount + 1)]
    largest = most if full else min(most, max(-(-total // amount), total * loads[0] // sum(loads)))
    least = 1 if total - largest >= amount - 1 else 0
    given, rest = [largest] + [least] * (amount - 1), total - largest - least * (amount - 1)
    while rest > 0:
        movable = [i for i in range(1, amount) if given[i] < largest] or [i for i in range(1, amount) if given[i] < most]
        pool, left = sum([loads[i] for i in movable]), rest
        for i in movable:
            more = min(most - given[i], max(1, left * loads[i] // pool), rest)
            given[i] = given[i] + more
            rest = rest - more
    return np.array(given)


def noise(stream_key, shape, scale, most, cuts=(), kind=jnp.bfloat16):
    factor_of = levels(stream_key, shape, cuts, -0.22, 0.18) if cuts else 1.0
    drawn = jax.random.normal(stream_key, shape, jnp.float32) * scale * factor_of
    return jnp.minimum(jnp.maximum(drawn, -most), most).astype(kind)


def setup_inputs(seed: int = 0, part: int = 0) -> dict:
    arg_keys = jax.random.split(jax.random.key(seed), 5)
    part_keys = jax.random.split(jax.random.fold_in(arg_keys[4], part), 5)
    half_tensor = noise(part_keys[0], (AUX, NOCC, DOM), 0.125, 0.75, ((0, 4), (1, 4)))
    batch_owner_keys = jax.random.split(jax.random.fold_in(part_keys[1], 1), NOCC // OCC_R)
    batch_owner_turns = jax.random.permutation(jax.random.fold_in(part_keys[1], 3), NOCC // OCC_R)
    batch_owner = jax.vmap(lambda own, number: deal_out(jax.random.fold_in(part_keys[1], 2), own, number, OCC_R, NBATCH, 1, CAP, 2))(batch_owner_keys, batch_owner_turns).reshape((NOCC, 1))
    pair_list = draw_pair_list(jax.random.fold_in(jax.random.fold_in(arg_keys[4], part), 71), part)
    live_pairs = draw_live_pairs(jax.random.fold_in(jax.random.fold_in(arg_keys[4], part), 71), part)
    return dict(half_tensor=half_tensor, batch_owner=batch_owner, pair_list=pair_list, live_pairs=live_pairs)


def block_pairs(pair_codes, blocks):
    row_grid = lax.broadcasted_iota(jnp.int32, (blocks, blocks), 0)
    col_grid = lax.broadcasted_iota(jnp.int32, (blocks, blocks), 1)
    code_grid = row_grid * blocks - (row_grid * (row_grid - 1)) // 2 + (col_grid - row_grid)
    upper_part = col_grid >= row_grid
    matches = (code_grid[None, :, :] == pair_codes[:, None, None]) & upper_part[None, :, :]
    first_blocks = jnp.sum(jnp.where(matches, row_grid[None], 0), axis=(1, 2)).astype(jnp.int32)
    second_blocks = jnp.sum(jnp.where(matches, col_grid[None], 0), axis=(1, 2)).astype(jnp.int32)
    return first_blocks, second_blocks


def slot_sources(owner_local, batches, capacity):
    local_count = owner_local.shape[0]
    batch_ids = lax.broadcasted_iota(jnp.int32, (local_count, batches), 1)
    onehot = (owner_local[:, None] == batch_ids).astype(jnp.int32)
    ranking = jnp.cumsum(onehot, axis=0) - 1
    slot_of = jnp.sum(ranking * onehot, axis=1)
    target = owner_local * capacity + slot_of
    slot_ids = lax.broadcasted_iota(jnp.int32, (local_count, batches * capacity), 1)
    orbital_ids = lax.broadcasted_iota(jnp.int32, (local_count, batches * capacity), 0)
    slot_hits = target[:, None] == slot_ids
    source_row = jnp.sum(jnp.where(slot_hits, orbital_ids, 0), axis=0)
    filled = jnp.any(slot_hits, axis=0)
    return jnp.where(filled, source_row, local_count).astype(jnp.int32)


def reference(half_tensor, batch_owner, pair_list, live_pairs):
    owners = batch_owner[:, 0].reshape(N_ROW, OCC_R)
    sources = jax.vmap(lambda owner_row: slot_sources(owner_row, NBATCH, CAP))(owners)
    offsets = lax.broadcasted_iota(jnp.int32, sources.shape, 0) * OCC_R
    global_rows = jnp.where(sources < OCC_R, sources + offsets, NOCC).astype(jnp.int32)

    def per_batch(batch):
        first_blocks, second_blocks = block_pairs(pair_list[batch], DB)
        keep_mask = jnp.arange(NPAIR, dtype=jnp.int32) < live_pairs[batch]

        def per_group(group):
            chosen = lax.dynamic_slice_in_dim(global_rows[group], (batch * CAP).astype(jnp.int32), CAP)
            picked = jnp.take(half_tensor, chosen, axis=1, mode="fill", fill_value=0)
            stacked_rows = picked.reshape(AUX * CAP, DB, TILE)
            left_part = jnp.take(stacked_rows, first_blocks, axis=1).astype(jnp.float32)
            right_part = jnp.take(stacked_rows, second_blocks, axis=1).astype(jnp.float32)
            tile_block = jnp.einsum("mga,mgb->gab", left_part, right_part)
            tile_block = jnp.where(keep_mask[:, None, None], tile_block, jnp.float32(0.0))
            rounded = lax.optimization_barrier(tile_block.astype(jnp.bfloat16))
            return rounded.astype(jnp.float32)

        partial_tiles = lax.map(per_group, jnp.arange(N_ROW, dtype=jnp.int32))
        return jnp.sum(partial_tiles, axis=0).astype(jnp.bfloat16)

    return lax.map(per_batch, jnp.arange(NBATCH, dtype=jnp.int32))
```

```python
import functools
import math

import jax
import jax.numpy as jnp
from jax import lax
from jax.experimental import pallas as pl
from jax.experimental.pallas import tpu as pltpu
from jax.sharding import PartitionSpec as P

TILE = 128
CAP = 8
GROUP = 256


def block_pairs(pair_codes, blocks):
    row_grid = lax.broadcasted_iota(jnp.int32, (blocks, blocks), 0)
    col_grid = lax.broadcasted_iota(jnp.int32, (blocks, blocks), 1)
    code_grid = row_grid * blocks - row_grid * (row_grid - 1) // 2 + (col_grid - row_grid)
    upper_part = col_grid >= row_grid
    matches = (code_grid[None, :, :] == pair_codes[:, None, None]) & upper_part[None, :, :]
    first_blocks = jnp.sum(jnp.where(matches, row_grid[None], 0), axis=(1, 2))
    second_blocks = jnp.sum(jnp.where(matches, col_grid[None], 0), axis=(1, 2))
    return (first_blocks, second_blocks)


def slot_sources(owner_local, batches, capacity):
    local_count = owner_local.shape[0]
    batch_ids = lax.broadcasted_iota(jnp.int32, (local_count, batches), 1)
    onehot = (owner_local[:, None] == batch_ids).astype(jnp.int32)
    ranking = jnp.cumsum(onehot, axis=0) - 1
    slot_of = jnp.sum(ranking * onehot, axis=1)
    target = owner_local * capacity + slot_of
    slot_ids = lax.broadcasted_iota(jnp.int32, (local_count, batches * capacity), 1)
    orbital_ids = lax.broadcasted_iota(jnp.int32, (local_count, batches * capacity), 0)
    slot_hits = target[:, None] == slot_ids
    source_row = jnp.sum(jnp.where(slot_hits, orbital_ids, 0), axis=0)
    filled = jnp.any(slot_hits, axis=0)
    return jnp.where(filled, source_row, local_count)


def slab_plan(half_tensor, batch_owner, pair_list, live_pairs):
    batches = lax.axis_size("orb")
    aux_local, occ_local, domain = half_tensor.shape
    blocks = domain // TILE
    sources = slot_sources(batch_owner[:, 0], batches, CAP)
    block_major = half_tensor.reshape(aux_local, occ_local, blocks, TILE).transpose(2, 1, 0, 3)
    outgoing = jnp.take(block_major, sources, axis=1, mode="fill", fill_value=0)
    arrived = lax.all_to_all(outgoing, "orb", split_axis=1, concat_axis=2, tiled=True)
    stacked_rows = arrived.reshape(blocks, -1, TILE)
    first_blocks, second_blocks = block_pairs(pair_list[0], blocks)
    live_count = live_pairs[0]
    pair_total = pair_list.shape[1]
    contract = (((0,), (0,)), ((), ()))
    group_size = math.gcd(4, pair_total)

    def one_group(group_index):
        pair_start = group_index * group_size
        tiles = []
        for offset in range(group_size):
            left = lax.dynamic_index_in_dim(
                stacked_rows, first_blocks[pair_start + offset], 0, keepdims=False
            )
            right = lax.dynamic_index_in_dim(
                stacked_rows, second_blocks[pair_start + offset], 0, keepdims=False
            )
            tiles.append(
                lax.dot_general(left, right, contract, preferred_element_type=jnp.float32)
            )
        keep_mask = pair_start + lax.iota(jnp.int32, group_size) < live_count
        return jnp.where(keep_mask[:, None, None], jnp.stack(tiles, axis=0), jnp.float32(0.0))

    grouped = lax.map(one_group, jnp.arange(pair_total // group_size, dtype=jnp.int32))
    terms = grouped.reshape(pair_total, TILE, TILE)
    mine = lax.psum_scatter(terms.astype(jnp.bfloat16), "row", scatter_dimension=0, tiled=True)
    return mine[None]


def chunk_kernel(
    blocks, share, occ_local, place, pairs, own_row, own_col, other_row, other_col,
    own_rows, other_rows, send_ref, keep_ref, rows_scratch, turned_scratch,
):
    step = pl.program_id(0)
    half_steps = pl.num_programs(0) // 2
    batch = place[0]
    kept = GROUP // occ_local * CAP

    def compact(row_ref, col_ref, data_ref):
        owner_row = row_ref[...]
        earlier = lax.broadcasted_iota(jnp.int32, (occ_local, GROUP), 0)
        lane = lax.broadcasted_iota(jnp.int32, (occ_local, GROUP), 1)
        before = (col_ref[...] == owner_row) & (earlier < lane % occ_local)
        rank = jnp.sum(before.astype(jnp.int32), axis=0, keepdims=True)
        lane_row = lax.broadcasted_iota(jnp.int32, (1, GROUP), 1)
        target = jnp.where(owner_row == batch, lane_row // occ_local * CAP + rank, -1)
        slot = lax.broadcasted_iota(jnp.int32, (kept, GROUP), 0)
        pick = (slot == target).astype(jnp.bfloat16)
        packed = jnp.dot(pick, data_ref[...], preferred_element_type=jnp.float32)
        packed = packed.astype(jnp.bfloat16)
        start = pl.multiple_of(step * kept, kept)
        rows_scratch[pl.ds(start, kept), :] = packed
        turned_scratch[:, pl.ds(start, kept)] = packed.T

    @pl.when(step < half_steps)
    def _():
        compact(own_row, own_col, own_rows)

    @pl.when(step >= half_steps)
    def _():
        compact(other_row, other_col, other_rows)

    @pl.when(step == pl.num_programs(0) - 1)
    def _():
        def tile(pair):
            code = pairs[batch, pair]
            known = jnp.maximum(code, 0)
            left = pl.multiple_of(known // blocks * TILE, TILE)
            right = pl.multiple_of(known % blocks * TILE, TILE)
            product = jnp.dot(
                turned_scratch[pl.ds(left, TILE), :],
                rows_scratch[:, pl.ds(right, TILE)],
                preferred_element_type=jnp.float32,
            )
            return jnp.where(code >= 0, product, jnp.float32(0.0))

        width = math.gcd(4, share)

        def several(turn, carry):
            for offset in range(width):
                at = turn * width + offset
                send_ref[at] = tile(place[1] + at).astype(jnp.bfloat16)
                keep_ref[at] = tile(place[2] + at)
            return carry

        lax.fori_loop(0, share // width, several, 0)


def tile_chunk(place, pairs, owners, own_rows, other_rows, share, occ_local):
    rows_total, domain = own_rows.shape
    half_steps = rows_total // GROUP
    kept = GROUP // occ_local * CAP
    depth = 2 * half_steps * kept
    whole = lambda shape: pl.BlockSpec(shape, lambda step, *_: (0,) * len(shape))
    return pl.pallas_call(
        functools.partial(chunk_kernel, domain // TILE, share, occ_local),
        grid_spec=pltpu.PrefetchScalarGridSpec(
            num_scalar_prefetch=2,
            grid=(2 * half_steps,),
            in_specs=[
                whole((1, GROUP)),
                whole((occ_local, 1)),
                whole((1, GROUP)),
                whole((occ_local, 1)),
                pl.BlockSpec(
                    (GROUP, domain), lambda step, *_: (jnp.minimum(step, half_steps - 1), 0)
                ),
                pl.BlockSpec(
                    (GROUP, domain), lambda step, *_: (jnp.maximum(step - half_steps, 0), 0)
                ),
            ],
            out_specs=[whole((share, TILE, TILE)), whole((share, TILE, TILE))],
            scratch_shapes=[
                pltpu.VMEM((depth, domain), jnp.bfloat16),
                pltpu.VMEM((domain, depth), jnp.bfloat16),
            ],
        ),
        out_shape=[
            jax.ShapeDtypeStruct((share, TILE, TILE), jnp.bfloat16),
            jax.ShapeDtypeStruct((share, TILE, TILE), jnp.float32),
        ],
        compiler_params=pltpu.CompilerParams(vmem_limit_bytes=48 * 1024 * 1024),
        cost_estimate=pl.CostEstimate(
            flops=4 * share * TILE * TILE * depth + 2 * depth * GROUP * domain,
            bytes_accessed=4 * rows_total * domain + 6 * share * TILE * TILE,
            transcendentals=0,
        ),
        name="tile_chunk",
    )(place, pairs, *owners, own_rows, other_rows)


def tile_plan(half_tensor, batch_owner, pair_list, live_pairs):
    batches = lax.axis_size("orb")
    rows = lax.axis_size("row")
    aux_local, occ_local, domain = half_tensor.shape
    pair_total = pair_list.shape[1]
    share = pair_total // rows
    blocks = domain // TILE
    row_at = lax.axis_index("row")
    orb_at = lax.axis_index("orb")
    swap_core = [(i, i ^ 1) for i in range(rows)]
    swap_x = [(i, i ^ 2) for i in range(rows)]

    own_rows = half_tensor.reshape(aux_local * occ_local, domain)
    other_rows = lax.ppermute(own_rows, "row", swap_core)
    other_owner = lax.ppermute(batch_owner, "row", swap_core)
    first_blocks, second_blocks = block_pairs(pair_list[0], blocks)
    live = lax.iota(jnp.int32, pair_total) < live_pairs[0]
    own_pairs = jnp.where(live, first_blocks * blocks + second_blocks, -1)
    pairs = lax.all_gather(own_pairs, "orb")

    def lanes(owner):
        return jnp.tile(owner[:, 0], GROUP // occ_local)[None]

    owners = (lanes(batch_owner), batch_owner, lanes(other_owner), other_owner)
    shifts = sorted(range(1, batches), key=lambda s: -min(s, batches - s)) + [0]
    total = None
    for shift in shifts:
        batch = (orb_at + shift) % batches
        place = jnp.stack([batch, (row_at ^ 2) * share, row_at * share]).astype(jnp.int32)
        send, keep = tile_chunk(place, pairs, owners, own_rows, other_rows, share, occ_local)
        term = keep + lax.ppermute(send, "row", swap_x).astype(jnp.float32)
        if shift:
            onward = [(i, (i + shift) % batches) for i in range(batches)]
            term = lax.ppermute(term.astype(jnp.bfloat16), "orb", onward).astype(jnp.float32)
        total = term if total is None else total + term
    return total.astype(jnp.bfloat16)[None]


def per_device(half_tensor, batch_owner, pair_list, live_pairs):
    batches = lax.axis_size("orb")
    rows = lax.axis_size("row")
    aux_local, occ_local, domain = half_tensor.shape
    pair_total = pair_list.shape[1]
    tile_elements = batches * pair_total * TILE * TILE
    slab_elements = batches * CAP * aux_local * domain
    fits = (
        rows == 4
        and pair_total % rows == 0
        and GROUP % occ_local == 0
        and aux_local * occ_local % GROUP == 0
        and tile_elements <= slab_elements
    )
    plan = tile_plan if fits else slab_plan
    return plan(half_tensor, batch_owner, pair_list, live_pairs)


def solution(mesh):
    return jax.shard_map(
        per_device,
        mesh=mesh,
        in_specs=(
            P(("grp", "orb"), "row", None),
            P(("grp", "row"), None),
            P(("grp", "orb"), None),
            P(("grp", "orb")),
        ),
        out_specs=P(("grp", "orb"), "row", None, None),
        check_vma=False,
    )
```

```python
import functools
import math

import jax
import jax.numpy as jnp
from jax import lax
from jax.experimental import pallas as pl
from jax.experimental.pallas import tpu as pltpu
from jax.sharding import PartitionSpec as P

TILE = 128
CAP = 8
GROUP = 256


def block_pairs(pair_codes, blocks):
    row_grid = lax.broadcasted_iota(jnp.int32, (blocks, blocks), 0)
    col_grid = lax.broadcasted_iota(jnp.int32, (blocks, blocks), 1)
    code_grid = row_grid * blocks - row_grid * (row_grid - 1) // 2 + (col_grid - row_grid)
    upper_part = col_grid >= row_grid
    matches = (code_grid[None, :, :] == pair_codes[:, None, None]) & upper_part[None, :, :]
    first_blocks = jnp.sum(jnp.where(matches, row_grid[None], 0), axis=(1, 2))
    second_blocks = jnp.sum(jnp.where(matches, col_grid[None], 0), axis=(1, 2))
    return (first_blocks, second_blocks)


def slot_sources(owner_local, batches, capacity):
    local_count = owner_local.shape[0]
    batch_ids = lax.broadcasted_iota(jnp.int32, (local_count, batches), 1)
    onehot = (owner_local[:, None] == batch_ids).astype(jnp.int32)
    ranking = jnp.cumsum(onehot, axis=0) - 1
    slot_of = jnp.sum(ranking * onehot, axis=1)
    target = owner_local * capacity + slot_of
    slot_ids = lax.broadcasted_iota(jnp.int32, (local_count, batches * capacity), 1)
    orbital_ids = lax.broadcasted_iota(jnp.int32, (local_count, batches * capacity), 0)
    slot_hits = target[:, None] == slot_ids
    source_row = jnp.sum(jnp.where(slot_hits, orbital_ids, 0), axis=0)
    filled = jnp.any(slot_hits, axis=0)
    return jnp.where(filled, source_row, local_count)


def slab_plan(half_tensor, batch_owner, pair_list, live_pairs):
    batches = lax.axis_size("orb")
    aux_local, occ_local, domain = half_tensor.shape
    blocks = domain // TILE
    sources = slot_sources(batch_owner[:, 0], batches, CAP)
    block_major = half_tensor.reshape(aux_local, occ_local, blocks, TILE).transpose(2, 1, 0, 3)
    outgoing = jnp.take(block_major, sources, axis=1, mode="fill", fill_value=0)
    arrived = lax.all_to_all(outgoing, "orb", split_axis=1, concat_axis=2, tiled=True)
    stacked_rows = arrived.reshape(blocks, -1, TILE)
    first_blocks, second_blocks = block_pairs(pair_list[0], blocks)
    live_count = live_pairs[0]
    pair_total = pair_list.shape[1]
    contract = (((0,), (0,)), ((), ()))
    group_size = math.gcd(4, pair_total)

    def one_group(group_index):
        pair_start = group_index * group_size
        tiles = []
        for offset in range(group_size):
            left = lax.dynamic_index_in_dim(
                stacked_rows, first_blocks[pair_start + offset], 0, keepdims=False
            )
            right = lax.dynamic_index_in_dim(
                stacked_rows, second_blocks[pair_start + offset], 0, keepdims=False
            )
            tiles.append(
                lax.dot_general(left, right, contract, preferred_element_type=jnp.float32)
            )
        keep_mask = pair_start + lax.iota(jnp.int32, group_size) < live_count
        return jnp.where(keep_mask[:, None, None], jnp.stack(tiles, axis=0), jnp.float32(0.0))

    grouped = lax.map(one_group, jnp.arange(pair_total // group_size, dtype=jnp.int32))
    terms = grouped.reshape(pair_total, TILE, TILE)
    mine = lax.psum_scatter(terms.astype(jnp.bfloat16), "row", scatter_dimension=0, tiled=True)
    return mine[None]


def chunk_kernel(sources, started, occ_local, place, pairs, table, *refs):
    owners, refs = refs[:sources], refs[sources:]
    slabs, refs = refs[:sources], refs[sources:]
    before, refs = (refs[:2], refs[2:]) if started else (None, refs)
    send_ref, keep_ref, packed_rows, turned = refs
    step = pl.program_id(0)
    groups = pl.num_programs(0) // sources
    batch = place[0]
    share = send_ref.shape[0]
    live = pairs[pairs.shape[0] - 1]
    per_group = GROUP // occ_local
    held = per_group * CAP

    def count(owner):
        number = jnp.int32(0)
        for orbital in range(occ_local):
            number = number + (owner[orbital] == batch).astype(jnp.int32)
        return number

    counts = [count(owner) for owner in owners]

    def pack(owner, number, slab, first, group):
        lane = lax.broadcasted_iota(jnp.int32, (1, GROUP), 1)
        rank = jnp.int32(0)
        target = jnp.full((1, GROUP), -1, jnp.int32)
        for orbital in range(occ_local):
            mine = owner[orbital] == batch
            row = jnp.where(mine, lane // occ_local * number + rank, -1)
            target = jnp.where(lane % occ_local == orbital, row, target)
            rank = rank + mine.astype(jnp.int32)
        slot = lax.broadcasted_iota(jnp.int32, (held, GROUP), 0)
        pick = (slot == target).astype(jnp.bfloat16)
        packed = jnp.dot(pick, slab[...], preferred_element_type=jnp.float32)
        start = pl.multiple_of((first + group * number) * per_group, per_group)
        packed_rows[pl.ds(start, held), :] = packed.astype(jnp.bfloat16)

    first = jnp.int32(0)
    for source in range(sources):
        @pl.when((step >= source * groups) & (step < (source + 1) * groups))
        def _(source=source, first=first):
            pack(owners[source], counts[source], slabs[source], first, step - source * groups)

        first = first + groups * counts[source]

    @pl.when(step == pl.num_programs(0) - 1)
    def _():
        filled = pl.multiple_of(first * per_group, per_group)
        domain = packed_rows.shape[1]
        packed_rows[pl.ds(filled, GROUP), :] = jnp.zeros((GROUP, domain), jnp.bfloat16)
        parts = (filled + GROUP - 1) // GROUP

        def turn(part, carry):
            at = pl.multiple_of(part * GROUP, GROUP)
            for block in range(domain // TILE):
                columns = slice(block * TILE, (block + 1) * TILE)
                turned[columns, pl.ds(at, GROUP)] = packed_rows[pl.ds(at, GROUP), columns].T
            return carry

        lax.fori_loop(0, parts, turn, 0)

        def tiles(depth):
            def tile(pair, out, at, start):
                value = jnp.zeros((TILE, TILE), jnp.float32)
                if depth:
                    code = pairs[pair]
                    left = pl.multiple_of(table[2 * code], TILE)
                    right = pl.multiple_of(table[2 * code + 1], TILE)
                    product = jnp.dot(
                        turned[pl.ds(left, TILE), :depth],
                        packed_rows[:depth, pl.ds(right, TILE)],
                        preferred_element_type=jnp.float32,
                    )
                    value = jnp.where(pair < live, product, value)
                if start is not None:
                    value = value + start[at]
                out[at] = value.astype(out.dtype)

            width = math.gcd(4, share)

            def several(turn_at, carry):
                for offset in range(width):
                    at = turn_at * width + offset
                    tile(place[1] + at, send_ref, at, before and before[0])
                    tile(place[2] + at, keep_ref, at, before and before[1])
                return carry

            lax.fori_loop(0, share // width, several, 0)

        for part_count in range(turned.shape[1] // GROUP + 1):
            pl.when(parts == part_count)(functools.partial(tiles, part_count * GROUP))


def tile_chunk(place, pairs, table, owners, slabs, share, send_type, before=()):
    sources = len(slabs)
    occ_local, = owners[0].shape
    rows_total, domain = slabs[0].shape
    groups = rows_total // GROUP
    depth = sources * groups * GROUP // occ_local * CAP
    depth = -(-depth // GROUP) * GROUP
    tiles = (share, TILE, TILE)
    whole = pl.BlockSpec(tiles, lambda step, *_: (0, 0, 0))

    def slab_spec(source):
        def block(step, *_):
            return (jnp.clip(step - source * groups, 0, groups - 1), 0)

        return pl.BlockSpec((GROUP, domain), block)

    return pl.pallas_call(
        functools.partial(chunk_kernel, sources, bool(before), occ_local),
        grid_spec=pltpu.PrefetchScalarGridSpec(
            num_scalar_prefetch=3 + sources,
            grid=(sources * groups,),
            in_specs=[slab_spec(source) for source in range(sources)] + [whole] * len(before),
            out_specs=[whole, whole],
            scratch_shapes=[
                pltpu.VMEM((depth + GROUP, domain), jnp.bfloat16),
                pltpu.VMEM((domain, depth), jnp.bfloat16),
            ],
        ),
        out_shape=[
            jax.ShapeDtypeStruct(tiles, send_type),
            jax.ShapeDtypeStruct(tiles, jnp.float32),
        ],
        compiler_params=pltpu.CompilerParams(vmem_limit_bytes=56 * 1024 * 1024),
        cost_estimate=pl.CostEstimate(
            flops=4 * share * TILE * TILE * depth + 2 * depth * GROUP * domain,
            bytes_accessed=2 * sources * rows_total * domain + 6 * share * TILE * TILE,
            transcendentals=0,
        ),
        name="tile_chunk",
    )(place, pairs, table, *owners, *slabs, *before)


def pair_table(blocks):
    return jnp.asarray(
        [TILE * block for left in range(blocks) for right in range(left, blocks)
         for block in (left, right)],
        jnp.int32,
    )


def tile_plan(half_tensor, batch_owner, pair_list, live_pairs):
    batches = lax.axis_size("orb")
    rows = lax.axis_size("row")
    aux_local, occ_local, domain = half_tensor.shape
    share = pair_list.shape[1] // rows
    row_at = lax.axis_index("row")
    orb_at = lax.axis_index("orb")

    def exchange(array, axis, bits):
        size = lax.axis_size(axis)
        return lax.ppermute(array, axis, [(i, i ^ bits) for i in range(size)])

    own_rows = half_tensor.reshape(aux_local * occ_local, domain)
    other_rows = exchange(own_rows, "row", 1)
    own_owner = batch_owner[:, 0]
    other_owner = exchange(own_owner, "row", 1)
    own_pairs = jnp.concatenate([pair_list[0], live_pairs])
    pairs = [own_pairs] + [exchange(own_pairs, "orb", bits) for bits in range(1, batches)]
    table = pair_table(domain // TILE)

    def place_of(bits):
        return jnp.stack([orb_at ^ bits, (row_at ^ 2) * share, row_at * share]).astype(jnp.int32)

    def chunk(bits, place):
        both = (own_owner, other_owner), (own_rows, other_rows)
        return tile_chunk(place, pairs[bits], table, *both, share, jnp.bfloat16)

    def over_x(send, keep):
        return keep + exchange(send, "row", 2).astype(jnp.float32)

    def after(array, earlier):
        return lax.optimization_barrier((array, earlier))

    place = place_of(3)
    started = tile_chunk(
        place, pairs[3], table, (own_owner,), (own_rows,), share, jnp.float32
    )
    send_3, keep_3 = tile_chunk(
        place, pairs[3], table, (other_owner,), (other_rows,), share, jnp.bfloat16, started
    )
    send_2, keep_2 = chunk(2, place_of(2))
    far = over_x(send_3, keep_3).astype(jnp.bfloat16)
    place, far = after(place_of(1), far)
    far = exchange(far, "orb", 1)
    send_1, keep_1 = chunk(1, place)
    term_2 = over_x(send_2, keep_2)
    place, term_2 = after(place_of(0), term_2)
    across = exchange((term_2 + far.astype(jnp.float32)).astype(jnp.bfloat16), "orb", 2)
    send_0, keep_0 = chunk(0, place)
    near = exchange(over_x(send_1, keep_1).astype(jnp.bfloat16), "orb", 1)
    total = over_x(send_0, keep_0) + near.astype(jnp.float32) + across.astype(jnp.float32)
    return total.astype(jnp.bfloat16)[None]


def per_device(half_tensor, batch_owner, pair_list, live_pairs):
    batches = lax.axis_size("orb")
    rows = lax.axis_size("row")
    aux_local, occ_local, domain = half_tensor.shape
    pair_total = pair_list.shape[1]
    tile_elements = batches * pair_total * TILE * TILE
    slab_elements = batches * CAP * aux_local * domain
    fits = (
        rows == 4
        and batches == 4
        and pair_total % rows == 0
        and GROUP % occ_local == 0
        and aux_local * occ_local % GROUP == 0
        and tile_elements <= slab_elements
    )
    plan = tile_plan if fits else slab_plan
    return plan(half_tensor, batch_owner, pair_list, live_pairs)


def solution(mesh):
    return jax.shard_map(
        per_device,
        mesh=mesh,
        in_specs=(
            P(("grp", "orb"), "row", None),
            P(("grp", "row"), None),
            P(("grp", "orb"), None),
            P(("grp", "orb")),
        ),
        out_specs=P(("grp", "orb"), "row", None, None),
        check_vma=False,
    )
```

```python
import functools
import math

import jax
import jax.numpy as jnp
from jax import lax
from jax.experimental import pallas as pl
from jax.experimental.pallas import tpu as pltpu
from jax.sharding import PartitionSpec as P

TILE = 128
CAP = 8
GROUP = 256
ROWS = 4


def block_pairs(pair_codes, blocks):
    row_grid = lax.broadcasted_iota(jnp.int32, (blocks, blocks), 0)
    col_grid = lax.broadcasted_iota(jnp.int32, (blocks, blocks), 1)
    code_grid = row_grid * blocks - row_grid * (row_grid - 1) // 2 + (col_grid - row_grid)
    upper_part = col_grid >= row_grid
    matches = (code_grid[None, :, :] == pair_codes[:, None, None]) & upper_part[None, :, :]
    first_blocks = jnp.sum(jnp.where(matches, row_grid[None], 0), axis=(1, 2))
    second_blocks = jnp.sum(jnp.where(matches, col_grid[None], 0), axis=(1, 2))
    return (first_blocks, second_blocks)


def slot_sources(owner_local, batches, capacity):
    local_count = owner_local.shape[0]
    batch_ids = lax.broadcasted_iota(jnp.int32, (local_count, batches), 1)
    onehot = (owner_local[:, None] == batch_ids).astype(jnp.int32)
    ranking = jnp.cumsum(onehot, axis=0) - 1
    slot_of = jnp.sum(ranking * onehot, axis=1)
    target = owner_local * capacity + slot_of
    slot_ids = lax.broadcasted_iota(jnp.int32, (local_count, batches * capacity), 1)
    orbital_ids = lax.broadcasted_iota(jnp.int32, (local_count, batches * capacity), 0)
    slot_hits = target[:, None] == slot_ids
    source_row = jnp.sum(jnp.where(slot_hits, orbital_ids, 0), axis=0)
    filled = jnp.any(slot_hits, axis=0)
    return jnp.where(filled, source_row, local_count)


def slab_plan(half_tensor, batch_owner, pair_list, live_pairs):
    batches = lax.axis_size("orb")
    aux_local, occ_local, domain = half_tensor.shape
    blocks = domain // TILE
    sources = slot_sources(batch_owner[:, 0], batches, CAP)
    block_major = half_tensor.reshape(aux_local, occ_local, blocks, TILE).transpose(2, 1, 0, 3)
    outgoing = jnp.take(block_major, sources, axis=1, mode="fill", fill_value=0)
    arrived = lax.all_to_all(outgoing, "orb", split_axis=1, concat_axis=2, tiled=True)
    stacked_rows = arrived.reshape(blocks, -1, TILE)
    first_blocks, second_blocks = block_pairs(pair_list[0], blocks)
    live_count = live_pairs[0]
    pair_total = pair_list.shape[1]
    contract = (((0,), (0,)), ((), ()))
    group_size = math.gcd(4, pair_total)

    def one_group(group_index):
        pair_start = group_index * group_size
        tiles = []
        for offset in range(group_size):
            left = lax.dynamic_index_in_dim(
                stacked_rows, first_blocks[pair_start + offset], 0, keepdims=False
            )
            right = lax.dynamic_index_in_dim(
                stacked_rows, second_blocks[pair_start + offset], 0, keepdims=False
            )
            tiles.append(
                lax.dot_general(left, right, contract, preferred_element_type=jnp.float32)
            )
        keep_mask = pair_start + lax.iota(jnp.int32, group_size) < live_count
        return jnp.where(keep_mask[:, None, None], jnp.stack(tiles, axis=0), jnp.float32(0.0))

    grouped = lax.map(one_group, jnp.arange(pair_total // group_size, dtype=jnp.int32))
    terms = grouped.reshape(pair_total, TILE, TILE)
    mine = lax.psum_scatter(terms.astype(jnp.bfloat16), "row", scatter_dimension=0, tiled=True)
    return mine[None]


def chunk_kernel(bits, sources, started, occ_local, info, table, *refs):
    slabs, refs = refs[:sources], refs[sources:]
    before, refs = (refs[:2], refs[2:]) if started else (None, refs)
    send_ref, keep_ref, stage, packed_rows, turned, pick, arrived = refs[:7]
    started_tiles, started_arrived = refs[7:] if started else (None, None)
    share = send_ref.shape[0]
    rows_total, domain = slabs[0].shape
    groups = rows_total // GROUP
    per_group = GROUP // occ_local
    held = per_group * CAP
    pair_total = share * ROWS
    batch = info[0] ^ bits
    send_first = (info[1] ^ 2) * share
    keep_first = info[1] * share
    owner_at = 2
    codes_at = owner_at + 2 * occ_local + bits * (pair_total + 1)
    live = info[codes_at + pair_total]

    def slab_copy(source, group):
        rows = pl.ds(pl.multiple_of(group * GROUP, GROUP), GROUP)
        place = source * groups + group
        staged = pl.ds(pl.multiple_of(place * GROUP, GROUP), GROUP)
        return pltpu.make_async_copy(
            slabs[source].at[rows, :], stage.at[staged, :], arrived.at[place]
        )

    for source in range(sources):
        for group in range(groups):
            slab_copy(source, group).start()
    if started:
        start_copies = [
            pltpu.make_async_copy(before[i], started_tiles.at[i], started_arrived.at[i])
            for i in range(2)
        ]
        for copy in start_copies:
            copy.start()

    first = jnp.int32(0)
    for source in range(sources):
        owners = owner_at + (source + (0 if sources == 2 else int(started))) * occ_local
        mine = [info[owners + orbital] == batch for orbital in range(occ_local)]
        number = sum(each.astype(jnp.int32) for each in mine)

        lane = lax.broadcasted_iota(jnp.int32, (1, GROUP), 1)
        orbital_of = lane & (occ_local - 1)
        base = (lane >> (occ_local.bit_length() - 1)) * number
        target = jnp.full((1, GROUP), -1, jnp.int32)
        rank = jnp.int32(0)
        for orbital in range(occ_local):
            shift = jnp.where(mine[orbital], rank, -GROUP * CAP)
            target = jnp.where(orbital_of == orbital, base + shift, target)
            rank = rank + mine[orbital].astype(jnp.int32)
        slot = lax.broadcasted_iota(jnp.int32, (held, GROUP), 0)
        pick[...] = (slot == target).astype(jnp.bfloat16)

        def pack(group, carry, source=source, number=number, first=first):
            slab_copy(source, group).wait()
            staged = pl.multiple_of((source * groups + group) * GROUP, GROUP)
            start = pl.multiple_of((first + group * number) * per_group, per_group)
            for column in range(0, domain, 2 * TILE):
                columns = slice(column, column + 2 * TILE)
                packed = jnp.dot(
                    pick[...], stage[pl.ds(staged, GROUP), columns],
                    preferred_element_type=jnp.float32,
                )
                packed_rows[pl.ds(start, held), columns] = packed.astype(jnp.bfloat16)
            return carry

        lax.fori_loop(0, groups, pack, 0)
        first = first + groups * number

    filled = pl.multiple_of(first * per_group, per_group)
    packed_rows[pl.ds(filled, GROUP), :] = jnp.zeros((GROUP, domain), jnp.bfloat16)
    parts = (filled + GROUP - 1) // GROUP

    def turn(part, carry):
        at = pl.multiple_of(part * GROUP, GROUP)
        for column in range(0, domain, TILE):
            columns = slice(column, column + TILE)
            turned[columns, pl.ds(at, GROUP)] = packed_rows[pl.ds(at, GROUP), columns].T
        return carry

    lax.fori_loop(0, parts, turn, 0)
    if started:
        for copy in start_copies:
            copy.wait()

    def tiles(depth):
        def tile(pair, out, at, side):
            value = jnp.zeros((TILE, TILE), jnp.float32)
            if depth:
                code = info[codes_at + pair]
                left = pl.multiple_of(table[2 * code], TILE)
                right = pl.multiple_of(table[2 * code + 1], TILE)
                product = jnp.dot(
                    turned[pl.ds(left, TILE), :depth],
                    packed_rows[:depth, pl.ds(right, TILE)],
                    preferred_element_type=jnp.float32,
                )
                value = jnp.where(pair < live, product, value)
            if started:
                value = value + started_tiles[side, at]
            out[at] = value.astype(out.dtype)

        width = math.gcd(4, share)

        def several(turn_at, carry):
            for offset in range(width):
                at = turn_at * width + offset
                tile(send_first + at, send_ref, at, 0)
                tile(keep_first + at, keep_ref, at, 1)
            return carry

        lax.fori_loop(0, share // width, several, 0)

    for part_count in range(turned.shape[1] // GROUP + 1):
        pl.when(parts == part_count)(functools.partial(tiles, part_count * GROUP))


def tile_chunk(bits, info, table, slabs, occ_local, share, send_type, before=()):
    sources = len(slabs)
    rows_total, domain = slabs[0].shape
    groups = rows_total // GROUP
    held = GROUP // occ_local * CAP
    depth = -(-sources * groups * held // GROUP) * GROUP
    tiles = (share, TILE, TILE)
    anywhere = pl.BlockSpec(memory_space=pl.ANY)
    in_vmem = pl.BlockSpec(memory_space=pltpu.VMEM)
    in_smem = pl.BlockSpec(memory_space=pltpu.SMEM)
    scratch = [
        pltpu.VMEM((sources * rows_total, domain), jnp.bfloat16),
        pltpu.VMEM((depth + GROUP, domain), jnp.bfloat16),
        pltpu.VMEM((domain, depth), jnp.bfloat16),
        pltpu.VMEM((held, GROUP), jnp.bfloat16),
        pltpu.SemaphoreType.DMA((sources * groups,)),
    ]
    if before:
        scratch += [pltpu.VMEM((2, *tiles), jnp.float32), pltpu.SemaphoreType.DMA((2,))]
    return pl.pallas_call(
        functools.partial(chunk_kernel, bits, sources, bool(before), occ_local),
        in_specs=[in_smem, in_smem] + [anywhere] * (sources + len(before)),
        out_specs=[in_vmem, in_vmem],
        scratch_shapes=scratch,
        out_shape=[
            jax.ShapeDtypeStruct(tiles, send_type),
            jax.ShapeDtypeStruct(tiles, jnp.float32),
        ],
        compiler_params=pltpu.CompilerParams(vmem_limit_bytes=56 * 1024 * 1024),
        cost_estimate=pl.CostEstimate(
            flops=4 * share * TILE * TILE * depth + 2 * depth * GROUP * domain,
            bytes_accessed=2 * sources * rows_total * domain + 6 * share * TILE * TILE,
            transcendentals=0,
        ),
        name="tile_chunk",
    )(info, table, *slabs, *before)


def pair_table(blocks):
    return jnp.asarray(
        [TILE * block for left in range(blocks) for right in range(left, blocks)
         for block in (left, right)],
        jnp.int32,
    )


def tile_plan(half_tensor, batch_owner, pair_list, live_pairs):
    batches = lax.axis_size("orb")
    rows = lax.axis_size("row")
    aux_local, occ_local, domain = half_tensor.shape
    share = pair_list.shape[1] // rows
    row_at = lax.axis_index("row")
    orb_at = lax.axis_index("orb")

    def exchange(array, axis, bits):
        size = lax.axis_size(axis)
        return lax.ppermute(array, axis, [(i, i ^ bits) for i in range(size)])

    own_rows = half_tensor.reshape(aux_local * occ_local, domain)
    other_rows = exchange(own_rows, "row", 1)
    own_owner = batch_owner[:, 0]
    own_pairs = jnp.concatenate([pair_list[0], live_pairs])
    info = jnp.concatenate(
        [jnp.stack([orb_at, row_at]), own_owner, exchange(own_owner, "row", 1), own_pairs]
        + [exchange(own_pairs, "orb", bits) for bits in range(1, batches)]
    )
    table = pair_table(domain // TILE)

    def chunk(bits, slabs, send_type=jnp.bfloat16, before=()):
        return tile_chunk(bits, info, table, slabs, occ_local, share, send_type, before)

    def over_x(send, keep):
        return keep + exchange(send, "row", 2).astype(jnp.float32)

    def after(array, earlier):
        return lax.optimization_barrier((array, earlier))

    started = chunk(3, (own_rows,), jnp.float32)
    send_3, keep_3 = chunk(3, (other_rows,), before=started)
    send_2, keep_2 = chunk(2, (own_rows, other_rows))
    send_1, keep_1 = chunk(1, (own_rows, other_rows))
    far = over_x(send_3, keep_3).astype(jnp.bfloat16)
    other_rows, far = after(other_rows, far)
    far = exchange(far, "orb", 1)
    send_0, keep_0 = chunk(0, (own_rows, other_rows))
    term_2 = over_x(send_2, keep_2)
    across = exchange((term_2 + far.astype(jnp.float32)).astype(jnp.bfloat16), "orb", 2)
    near = exchange(over_x(send_1, keep_1).astype(jnp.bfloat16), "orb", 1)
    total = over_x(send_0, keep_0) + near.astype(jnp.float32) + across.astype(jnp.float32)
    return total.astype(jnp.bfloat16)[None]


def per_device(half_tensor, batch_owner, pair_list, live_pairs):
    batches = lax.axis_size("orb")
    rows = lax.axis_size("row")
    aux_local, occ_local, domain = half_tensor.shape
    pair_total = pair_list.shape[1]
    tile_elements = batches * pair_total * TILE * TILE
    slab_elements = batches * CAP * aux_local * domain
    fits = (
        rows == ROWS
        and batches == 4
        and pair_total % rows == 0
        and occ_local & (occ_local - 1) == 0
        and GROUP % occ_local == 0
        and aux_local * occ_local % GROUP == 0
        and tile_elements <= slab_elements
    )
    plan = tile_plan if fits else slab_plan
    return plan(half_tensor, batch_owner, pair_list, live_pairs)


def solution(mesh):
    return jax.shard_map(
        per_device,
        mesh=mesh,
        in_specs=(
            P(("grp", "orb"), "row", None),
            P(("grp", "row"), None),
            P(("grp", "orb"), None),
            P(("grp", "orb")),
        ),
        out_specs=P(("grp", "orb"), "row", None, None),
        check_vma=False,
    )
```

```python
import functools
import math

import jax
import jax.numpy as jnp
from jax import lax
from jax.experimental import pallas as pl
from jax.experimental.pallas import tpu as pltpu
from jax.sharding import PartitionSpec as P

TILE = 128
CAP = 8
GROUP = 256
ROWS = 4


def block_pairs(pair_codes, blocks):
    row_grid = lax.broadcasted_iota(jnp.int32, (blocks, blocks), 0)
    col_grid = lax.broadcasted_iota(jnp.int32, (blocks, blocks), 1)
    code_grid = row_grid * blocks - row_grid * (row_grid - 1) // 2 + (col_grid - row_grid)
    upper_part = col_grid >= row_grid
    matches = (code_grid[None, :, :] == pair_codes[:, None, None]) & upper_part[None, :, :]
    first_blocks = jnp.sum(jnp.where(matches, row_grid[None], 0), axis=(1, 2))
    second_blocks = jnp.sum(jnp.where(matches, col_grid[None], 0), axis=(1, 2))
    return (first_blocks, second_blocks)


def slot_sources(owner_local, batches, capacity):
    local_count = owner_local.shape[0]
    batch_ids = lax.broadcasted_iota(jnp.int32, (local_count, batches), 1)
    onehot = (owner_local[:, None] == batch_ids).astype(jnp.int32)
    ranking = jnp.cumsum(onehot, axis=0) - 1
    slot_of = jnp.sum(ranking * onehot, axis=1)
    target = owner_local * capacity + slot_of
    slot_ids = lax.broadcasted_iota(jnp.int32, (local_count, batches * capacity), 1)
    orbital_ids = lax.broadcasted_iota(jnp.int32, (local_count, batches * capacity), 0)
    slot_hits = target[:, None] == slot_ids
    source_row = jnp.sum(jnp.where(slot_hits, orbital_ids, 0), axis=0)
    filled = jnp.any(slot_hits, axis=0)
    return jnp.where(filled, source_row, local_count)


def slab_plan(half_tensor, batch_owner, pair_list, live_pairs):
    batches = lax.axis_size("orb")
    aux_local, occ_local, domain = half_tensor.shape
    blocks = domain // TILE
    sources = slot_sources(batch_owner[:, 0], batches, CAP)
    block_major = half_tensor.reshape(aux_local, occ_local, blocks, TILE).transpose(2, 1, 0, 3)
    outgoing = jnp.take(block_major, sources, axis=1, mode="fill", fill_value=0)
    arrived = lax.all_to_all(outgoing, "orb", split_axis=1, concat_axis=2, tiled=True)
    stacked_rows = arrived.reshape(blocks, -1, TILE)
    first_blocks, second_blocks = block_pairs(pair_list[0], blocks)
    live_count = live_pairs[0]
    pair_total = pair_list.shape[1]
    contract = (((0,), (0,)), ((), ()))
    group_size = math.gcd(4, pair_total)

    def one_group(group_index):
        pair_start = group_index * group_size
        tiles = []
        for offset in range(group_size):
            left = lax.dynamic_index_in_dim(
                stacked_rows, first_blocks[pair_start + offset], 0, keepdims=False
            )
            right = lax.dynamic_index_in_dim(
                stacked_rows, second_blocks[pair_start + offset], 0, keepdims=False
            )
            tiles.append(
                lax.dot_general(left, right, contract, preferred_element_type=jnp.float32)
            )
        keep_mask = pair_start + lax.iota(jnp.int32, group_size) < live_count
        return jnp.where(keep_mask[:, None, None], jnp.stack(tiles, axis=0), jnp.float32(0.0))

    grouped = lax.map(one_group, jnp.arange(pair_total // group_size, dtype=jnp.int32))
    terms = grouped.reshape(pair_total, TILE, TILE)
    mine = lax.psum_scatter(terms.astype(jnp.bfloat16), "row", scatter_dimension=0, tiled=True)
    return mine[None]


def chunk_kernel(bits, occ_local, share, info, table, *refs):
    slabs, (send_out, keep_out) = refs[:2], refs[2:4]
    stage, packed_rows, turned, pick, send_ref, keep_ref, arrived, left_off = refs[4:]
    sources = len(slabs)
    rows_total, domain = slabs[0].shape
    groups = rows_total // GROUP
    per_group = GROUP // occ_local
    held = per_group * CAP
    pair_total = share * ROWS
    batch = info[0] ^ bits
    send_first = (info[1] ^ 2) * share
    keep_first = info[1] * share
    owner_at = 2
    codes_at = owner_at + sources * occ_local + bits * (pair_total + 1)
    live = info[codes_at + pair_total]

    def slab_copy(source, group):
        rows = pl.ds(pl.multiple_of(group * GROUP, GROUP), GROUP)
        place = source * groups + group
        staged = pl.ds(pl.multiple_of(place * GROUP, GROUP), GROUP)
        return pltpu.make_async_copy(
            slabs[source].at[rows, :], stage.at[staged, :], arrived.at[place]
        )

    for source in range(sources):
        for group in range(groups):
            slab_copy(source, group).start()

    first = jnp.int32(0)
    for source in range(sources):
        owners = owner_at + source * occ_local
        mine = [info[owners + orbital] == batch for orbital in range(occ_local)]
        number = sum(each.astype(jnp.int32) for each in mine)

        lane = lax.broadcasted_iota(jnp.int32, (1, GROUP), 1)
        orbital_of = lane & (occ_local - 1)
        base = (lane >> (occ_local.bit_length() - 1)) * number
        target = jnp.full((1, GROUP), -1, jnp.int32)
        rank = jnp.int32(0)
        for orbital in range(occ_local):
            shift = jnp.where(mine[orbital], rank, -GROUP * CAP)
            target = jnp.where(orbital_of == orbital, base + shift, target)
            rank = rank + mine[orbital].astype(jnp.int32)
        slot = lax.broadcasted_iota(jnp.int32, (held, GROUP), 0)
        pick[...] = (slot == target).astype(jnp.bfloat16)

        def pack(group, carry, source=source, number=number, first=first):
            slab_copy(source, group).wait()
            staged = pl.multiple_of((source * groups + group) * GROUP, GROUP)
            start = pl.multiple_of((first + group * number) * per_group, per_group)
            for batch_of in range(0, domain, 8 * TILE):
                pieces = [
                    slice(column, column + 2 * TILE)
                    for column in range(batch_of, batch_of + 8 * TILE, 2 * TILE)
                ]
                packed = [
                    jnp.dot(
                        pick[...], stage[pl.ds(staged, GROUP), columns],
                        preferred_element_type=jnp.float32,
                    ).astype(jnp.bfloat16)
                    for columns in pieces
                ]
                for columns, piece in zip(pieces, packed):
                    packed_rows[pl.ds(start, held), columns] = piece
            return carry

        lax.fori_loop(0, groups, pack, 0)
        first = first + groups * number

    filled = pl.multiple_of(first * per_group, per_group)
    packed_rows[pl.ds(filled, GROUP), :] = jnp.zeros((GROUP, domain), jnp.bfloat16)
    parts = (filled + GROUP - 1) // GROUP

    def turn(part, carry):
        at = pl.multiple_of(part * GROUP, GROUP)
        for batch_of in range(0, domain, 4 * TILE):
            pieces = [
                slice(column, column + TILE)
                for column in range(batch_of, batch_of + 4 * TILE, TILE)
            ]
            blocks = [packed_rows[pl.ds(at, GROUP), columns].T for columns in pieces]
            for columns, block in zip(pieces, blocks):
                turned[columns, pl.ds(at, GROUP)] = block
        return carry

    lax.fori_loop(0, parts, turn, 0)

    width = math.gcd(2, share)

    def out_copies(turn_at):
        at = pl.ds(turn_at * width, width)
        return [
            pltpu.make_async_copy(held_tiles.at[at], out.at[at], left_off.at[side, turn_at])
            for side, (held_tiles, out) in enumerate(
                ((send_ref, send_out), (keep_ref, keep_out))
            )
        ]

    def tiles(depth):
        def tile(pair):
            zero = jnp.zeros((TILE, TILE), jnp.float32)
            if not depth:
                return zero
            code = info[codes_at + pair]
            left = pl.multiple_of(table[2 * code], TILE)
            right = pl.multiple_of(table[2 * code + 1], TILE)
            product = jnp.dot(
                turned[pl.ds(left, TILE), :depth],
                packed_rows[:depth, pl.ds(right, TILE)],
                preferred_element_type=jnp.float32,
            )
            return jnp.where(pair < live, product, zero)

        def several(turn_at, carry):
            ats = [turn_at * width + offset for offset in range(width)]
            sends = [tile(send_first + at).astype(send_ref.dtype) for at in ats]
            keeps = [tile(keep_first + at) for at in ats]
            for at, send, keep in zip(ats, sends, keeps):
                send_ref[at] = send
                keep_ref[at] = keep
            for copy in out_copies(turn_at):
                copy.start()
            return carry

        lax.fori_loop(0, share // width, several, 0)

    for part_count in range(turned.shape[1] // GROUP + 1):
        pl.when(parts == part_count)(functools.partial(tiles, part_count * GROUP))

    def drain(turn_at, carry):
        for copy in out_copies(turn_at):
            copy.wait()
        return carry

    lax.fori_loop(0, share // width, drain, 0)


def tile_chunk(bits, info, table, slabs, occ_local, share):
    sources = len(slabs)
    rows_total, domain = slabs[0].shape
    groups = rows_total // GROUP
    held = GROUP // occ_local * CAP
    depth = -(-sources * groups * held // GROUP) * GROUP
    tiles = (share, TILE, TILE)
    anywhere = pl.BlockSpec(memory_space=pl.ANY)
    in_smem = pl.BlockSpec(memory_space=pltpu.SMEM)
    return pl.pallas_call(
        functools.partial(chunk_kernel, bits, occ_local, share),
        in_specs=[in_smem, in_smem] + [anywhere] * sources,
        out_specs=[anywhere, anywhere],
        scratch_shapes=[
            pltpu.VMEM((sources * rows_total, domain), jnp.bfloat16),
            pltpu.VMEM((depth + GROUP, domain), jnp.bfloat16),
            pltpu.VMEM((domain, depth), jnp.bfloat16),
            pltpu.VMEM((held, GROUP), jnp.bfloat16),
            pltpu.VMEM(tiles, jnp.bfloat16),
            pltpu.VMEM(tiles, jnp.float32),
            pltpu.SemaphoreType.DMA((sources * groups,)),
            pltpu.SemaphoreType.DMA((2, share)),
        ],
        out_shape=[
            jax.ShapeDtypeStruct(tiles, jnp.bfloat16),
            jax.ShapeDtypeStruct(tiles, jnp.float32),
        ],
        compiler_params=pltpu.CompilerParams(vmem_limit_bytes=56 * 1024 * 1024),
        cost_estimate=pl.CostEstimate(
            flops=4 * share * TILE * TILE * depth + 2 * depth * GROUP * domain,
            bytes_accessed=2 * sources * rows_total * domain + 6 * share * TILE * TILE,
            transcendentals=0,
        ),
        name="tile_chunk",
    )(info, table, *slabs)


def pair_table(blocks):
    return jnp.asarray(
        [TILE * block for left in range(blocks) for right in range(left, blocks)
         for block in (left, right)],
        jnp.int32,
    )


def tile_plan(half_tensor, batch_owner, pair_list, live_pairs):
    batches = lax.axis_size("orb")
    rows = lax.axis_size("row")
    aux_local, occ_local, domain = half_tensor.shape
    share = pair_list.shape[1] // rows
    row_at = lax.axis_index("row")
    orb_at = lax.axis_index("orb")

    def exchange(array, axis, bits):
        size = lax.axis_size(axis)
        return lax.ppermute(array, axis, [(i, i ^ bits) for i in range(size)])

    own_rows = half_tensor.reshape(aux_local * occ_local, domain)
    other_rows = exchange(own_rows, "row", 1)
    own_owner = batch_owner[:, 0]
    own_pairs = jnp.concatenate([pair_list[0], live_pairs])
    info = jnp.concatenate(
        [jnp.stack([orb_at, row_at]), own_owner, exchange(own_owner, "row", 1), own_pairs]
        + [exchange(own_pairs, "orb", bits) for bits in range(1, batches)]
    )
    table = pair_table(domain // TILE)

    def chunk(bits):
        return tile_chunk(bits, info, table, (own_rows, other_rows), occ_local, share)

    def over_x(send, keep):
        return keep + exchange(send, "row", 2).astype(jnp.float32)

    def after(array, earlier):
        return lax.optimization_barrier((array, earlier))

    send_3, keep_3 = chunk(3)
    send_2, keep_2 = chunk(2)
    send_1, keep_1 = chunk(1)
    far = over_x(send_3, keep_3).astype(jnp.bfloat16)
    other_rows, far = after(other_rows, far)
    far = exchange(far, "orb", 1)
    send_0, keep_0 = chunk(0)
    term_2 = over_x(send_2, keep_2)
    across = exchange((term_2 + far.astype(jnp.float32)).astype(jnp.bfloat16), "orb", 2)
    near = exchange(over_x(send_1, keep_1).astype(jnp.bfloat16), "orb", 1)
    total = over_x(send_0, keep_0) + near.astype(jnp.float32) + across.astype(jnp.float32)
    return total.astype(jnp.bfloat16)[None]


def per_device(half_tensor, batch_owner, pair_list, live_pairs):
    batches = lax.axis_size("orb")
    rows = lax.axis_size("row")
    aux_local, occ_local, domain = half_tensor.shape
    pair_total = pair_list.shape[1]
    tile_elements = batches * pair_total * TILE * TILE
    slab_elements = batches * CAP * aux_local * domain
    fits = (
        rows == ROWS
        and batches == 4
        and pair_total % rows == 0
        and occ_local & (occ_local - 1) == 0
        and GROUP % occ_local == 0
        and aux_local * occ_local % GROUP == 0
        and tile_elements <= slab_elements
    )
    plan = tile_plan if fits else slab_plan
    return plan(half_tensor, batch_owner, pair_list, live_pairs)


def solution(mesh):
    return jax.shard_map(
        per_device,
        mesh=mesh,
        in_specs=(
            P(("grp", "orb"), "row", None),
            P(("grp", "row"), None),
            P(("grp", "orb"), None),
            P(("grp", "orb")),
        ),
        out_specs=P(("grp", "orb"), "row", None, None),
        check_vma=False,
    )
```

```python
import functools
import math

import jax
import jax.numpy as jnp
from jax import lax
from jax.experimental import pallas as pl
from jax.experimental.pallas import tpu as pltpu
from jax.sharding import PartitionSpec as P

TILE = 128
CAP = 8
GROUP = 256
ROWS = 4


def block_pairs(pair_codes, blocks):
    row_grid = lax.broadcasted_iota(jnp.int32, (blocks, blocks), 0)
    col_grid = lax.broadcasted_iota(jnp.int32, (blocks, blocks), 1)
    code_grid = row_grid * blocks - row_grid * (row_grid - 1) // 2 + (col_grid - row_grid)
    upper_part = col_grid >= row_grid
    matches = (code_grid[None, :, :] == pair_codes[:, None, None]) & upper_part[None, :, :]
    first_blocks = jnp.sum(jnp.where(matches, row_grid[None], 0), axis=(1, 2))
    second_blocks = jnp.sum(jnp.where(matches, col_grid[None], 0), axis=(1, 2))
    return (first_blocks, second_blocks)


def slot_sources(owner_local, batches, capacity):
    local_count = owner_local.shape[0]
    batch_ids = lax.broadcasted_iota(jnp.int32, (local_count, batches), 1)
    onehot = (owner_local[:, None] == batch_ids).astype(jnp.int32)
    ranking = jnp.cumsum(onehot, axis=0) - 1
    slot_of = jnp.sum(ranking * onehot, axis=1)
    target = owner_local * capacity + slot_of
    slot_ids = lax.broadcasted_iota(jnp.int32, (local_count, batches * capacity), 1)
    orbital_ids = lax.broadcasted_iota(jnp.int32, (local_count, batches * capacity), 0)
    slot_hits = target[:, None] == slot_ids
    source_row = jnp.sum(jnp.where(slot_hits, orbital_ids, 0), axis=0)
    filled = jnp.any(slot_hits, axis=0)
    return jnp.where(filled, source_row, local_count)


def slab_plan(half_tensor, batch_owner, pair_list, live_pairs):
    batches = lax.axis_size("orb")
    aux_local, occ_local, domain = half_tensor.shape
    blocks = domain // TILE
    sources = slot_sources(batch_owner[:, 0], batches, CAP)
    block_major = half_tensor.reshape(aux_local, occ_local, blocks, TILE).transpose(2, 1, 0, 3)
    outgoing = jnp.take(block_major, sources, axis=1, mode="fill", fill_value=0)
    arrived = lax.all_to_all(outgoing, "orb", split_axis=1, concat_axis=2, tiled=True)
    stacked_rows = arrived.reshape(blocks, -1, TILE)
    first_blocks, second_blocks = block_pairs(pair_list[0], blocks)
    live_count = live_pairs[0]
    pair_total = pair_list.shape[1]
    contract = (((0,), (0,)), ((), ()))
    group_size = math.gcd(4, pair_total)

    def one_group(group_index):
        pair_start = group_index * group_size
        tiles = []
        for offset in range(group_size):
            left = lax.dynamic_index_in_dim(
                stacked_rows, first_blocks[pair_start + offset], 0, keepdims=False
            )
            right = lax.dynamic_index_in_dim(
                stacked_rows, second_blocks[pair_start + offset], 0, keepdims=False
            )
            tiles.append(
                lax.dot_general(left, right, contract, preferred_element_type=jnp.float32)
            )
        keep_mask = pair_start + lax.iota(jnp.int32, group_size) < live_count
        return jnp.where(keep_mask[:, None, None], jnp.stack(tiles, axis=0), jnp.float32(0.0))

    grouped = lax.map(one_group, jnp.arange(pair_total // group_size, dtype=jnp.int32))
    terms = grouped.reshape(pair_total, TILE, TILE)
    mine = lax.psum_scatter(terms.astype(jnp.bfloat16), "row", scatter_dimension=0, tiled=True)
    return mine[None]


def lane_targets(positions, occ_local, stride, step):
    lane = lax.broadcasted_iota(jnp.int32, (1, GROUP), 1)
    orbital_of = lane & (occ_local - 1)
    base = (lane >> (occ_local.bit_length() - 1)) * step
    target = jnp.full((1, GROUP), -1, jnp.int32)
    for orbital in range(occ_local):
        target = jnp.where(orbital_of == orbital, base + positions[orbital] * stride, target)
    return target


def one_hot(target, height):
    slot = lax.broadcasted_iota(jnp.int32, (height, GROUP), 0)
    return (slot == target).astype(jnp.bfloat16)


def sort_kernel(batches, occ_local, owner, slab, sorted_out, stage, ordered, pick, arrived, left):
    rows_total, domain = slab.shape
    groups = rows_total // GROUP
    per_group = GROUP // occ_local
    piece = 2 * TILE

    def slab_copy(group):
        rows = pl.ds(group * GROUP, GROUP)
        return pltpu.make_async_copy(slab.at[rows, :], stage.at[rows, :], arrived.at[group])

    def out_copy(column):
        columns = pl.ds(column * piece, piece)
        return pltpu.make_async_copy(
            ordered.at[:, columns], sorted_out.at[:, columns], left.at[column]
        )

    for group in range(groups):
        slab_copy(group).start()
    owners = [owner[orbital] for orbital in range(occ_local)]
    positions = [jnp.int32(0)] * occ_local
    rank = jnp.int32(0)
    for batch in range(batches):
        for orbital in range(occ_local):
            mine = owners[orbital] == batch
            positions[orbital] = jnp.where(mine, rank, positions[orbital])
            rank = rank + mine.astype(jnp.int32)
    pick[...] = one_hot(lane_targets(positions, occ_local, per_group, 1), GROUP)
    for group in range(groups):
        slab_copy(group).wait()

    for column in range(domain // piece):
        columns = slice(column * piece, (column + 1) * piece)
        for group in range(groups):
            moved = jnp.dot(
                pick[...], stage[group * GROUP:(group + 1) * GROUP, columns],
                preferred_element_type=jnp.float32,
            ).astype(jnp.bfloat16)
            for unit in range(occ_local):
                to = (unit * groups + group) * per_group
                ordered[to:to + per_group, columns] = (
                    moved[unit * per_group:(unit + 1) * per_group]
                )
        out_copy(column).start()
    for column in range(domain // piece):
        out_copy(column).wait()


def sort_rows(owner, slab, batches):
    occ_local, = owner.shape
    rows_total, domain = slab.shape
    anywhere = pl.BlockSpec(memory_space=pl.ANY)
    return pl.pallas_call(
        functools.partial(sort_kernel, batches, occ_local),
        in_specs=[pl.BlockSpec(memory_space=pltpu.SMEM), anywhere],
        out_specs=anywhere,
        scratch_shapes=[
            pltpu.VMEM((rows_total, domain), jnp.bfloat16),
            pltpu.VMEM((rows_total, domain), jnp.bfloat16),
            pltpu.VMEM((GROUP, GROUP), jnp.bfloat16),
            pltpu.SemaphoreType.DMA((rows_total // GROUP,)),
            pltpu.SemaphoreType.DMA((domain // (2 * TILE),)),
        ],
        out_shape=jax.ShapeDtypeStruct((rows_total, domain), jnp.bfloat16),
        compiler_params=pltpu.CompilerParams(vmem_limit_bytes=56 * 1024 * 1024),
        cost_estimate=pl.CostEstimate(
            flops=2 * rows_total * GROUP * domain,
            bytes_accessed=4 * rows_total * domain,
            transcendentals=0,
        ),
        name="sort_rows",
    )(owner, slab)


def chunk_kernel(bits, occ_local, share, info, codes, table, own_sorted, other_rows, *refs):
    send_out, keep_out = refs[:2]
    stage, packed_rows, turned, pick, send_ref, keep_ref = refs[2:8]
    own_arrived, other_arrived, left_off = refs[8:]
    rows_total, domain = other_rows.shape
    groups = rows_total // GROUP
    per_group = GROUP // occ_local
    per_orbital = rows_total // occ_local
    held = per_group * CAP
    batch = info[0] ^ bits
    send_first = (info[1] ^ 2) * share
    keep_first = info[1] * share
    live = codes[share * ROWS]

    def other_copy(group):
        rows = pl.ds(pl.multiple_of(group * GROUP, GROUP), GROUP)
        return pltpu.make_async_copy(
            other_rows.at[rows, :], stage.at[rows, :], other_arrived.at[group]
        )

    for group in range(groups):
        other_copy(group).start()

    owners = [info[2 + orbital] for orbital in range(occ_local)]
    earlier = sum((owner < batch).astype(jnp.int32) for owner in owners)
    own_count = sum((owner == batch).astype(jnp.int32) for owner in owners)

    def own_copy(orbital):
        rows = pl.ds(pl.multiple_of((earlier + orbital) * per_orbital, per_orbital), per_orbital)
        to = pl.ds(pl.multiple_of(orbital * per_orbital, per_orbital), per_orbital)
        return pltpu.make_async_copy(
            own_sorted.at[rows, :], packed_rows.at[to, :], own_arrived.at[orbital]
        )

    def own_start(orbital, carry):
        own_copy(orbital).start()
        return carry

    def own_wait(orbital, carry):
        own_copy(orbital).wait()
        return carry

    lax.fori_loop(0, own_count, own_start, 0)

    mine = [info[2 + occ_local + orbital] == batch for orbital in range(occ_local)]
    positions = []
    other_count = jnp.int32(0)
    for each in mine:
        positions.append(jnp.where(each, other_count, -GROUP * CAP))
        other_count = other_count + each.astype(jnp.int32)
    pick[...] = one_hot(lane_targets(positions, occ_local, 1, other_count), held)

    def pack(group, carry):
        other_copy(group).wait()
        staged = pl.multiple_of(group * GROUP, GROUP)
        start = own_count * per_orbital + group * other_count * per_group
        start = pl.multiple_of(start, per_group)
        for batch_of in range(0, domain, 8 * TILE):
            pieces = [
                slice(column, column + 2 * TILE)
                for column in range(batch_of, batch_of + 8 * TILE, 2 * TILE)
            ]
            packed = [
                jnp.dot(
                    pick[...], stage[pl.ds(staged, GROUP), columns],
                    preferred_element_type=jnp.float32,
                ).astype(jnp.bfloat16)
                for columns in pieces
            ]
            for columns, piece in zip(pieces, packed):
                packed_rows[pl.ds(start, held), columns] = piece
        return carry

    lax.fori_loop(0, groups, pack, 0)
    filled = pl.multiple_of((own_count + other_count) * per_orbital, per_orbital)
    packed_rows[pl.ds(filled, GROUP), :] = jnp.zeros((GROUP, domain), jnp.bfloat16)
    parts = (filled + GROUP - 1) // GROUP
    lax.fori_loop(0, own_count, own_wait, 0)

    def turn(part, carry):
        at = pl.multiple_of(part * GROUP, GROUP)
        for batch_of in range(0, domain, 4 * TILE):
            pieces = [
                slice(column, column + TILE)
                for column in range(batch_of, batch_of + 4 * TILE, TILE)
            ]
            blocks = [packed_rows[pl.ds(at, GROUP), columns].T for columns in pieces]
            for columns, block in zip(pieces, blocks):
                turned[columns, pl.ds(at, GROUP)] = block
        return carry

    lax.fori_loop(0, parts, turn, 0)

    width = math.gcd(2, share)

    def out_copies(turn_at):
        at = pl.ds(turn_at * width, width)
        return [
            pltpu.make_async_copy(held_tiles.at[at], out.at[at], left_off.at[side, turn_at])
            for side, (held_tiles, out) in enumerate(
                ((send_ref, send_out), (keep_ref, keep_out))
            )
        ]

    def tiles(depth):
        def tile(pair):
            zero = jnp.zeros((TILE, TILE), jnp.float32)
            if not depth:
                return zero
            code = codes[pair]
            left = pl.multiple_of(table[2 * code], TILE)
            right = pl.multiple_of(table[2 * code + 1], TILE)
            product = jnp.dot(
                turned[pl.ds(left, TILE), :depth],
                packed_rows[:depth, pl.ds(right, TILE)],
                preferred_element_type=jnp.float32,
            )
            return jnp.where(pair < live, product, zero)

        def several(turn_at, carry):
            ats = [turn_at * width + offset for offset in range(width)]
            sends = [tile(send_first + at).astype(send_ref.dtype) for at in ats]
            keeps = [tile(keep_first + at) for at in ats]
            for at, send, keep in zip(ats, sends, keeps):
                send_ref[at] = send
                keep_ref[at] = keep
            for copy in out_copies(turn_at):
                copy.start()
            return carry

        lax.fori_loop(0, share // width, several, 0)

    for part_count in range(turned.shape[1] // GROUP + 1):
        pl.when(parts == part_count)(functools.partial(tiles, part_count * GROUP))

    def drain(turn_at, carry):
        for copy in out_copies(turn_at):
            copy.wait()
        return carry

    lax.fori_loop(0, share // width, drain, 0)


def tile_chunk(bits, info, codes, table, own_sorted, other_rows, occ_local, share):
    rows_total, domain = other_rows.shape
    groups = rows_total // GROUP
    held = GROUP // occ_local * CAP
    depth = 2 * groups * held
    tiles = (share, TILE, TILE)
    anywhere = pl.BlockSpec(memory_space=pl.ANY)
    in_smem = pl.BlockSpec(memory_space=pltpu.SMEM)
    return pl.pallas_call(
        functools.partial(chunk_kernel, bits, occ_local, share),
        in_specs=[in_smem] * 3 + [anywhere] * 2,
        out_specs=[anywhere, anywhere],
        scratch_shapes=[
            pltpu.VMEM((rows_total, domain), jnp.bfloat16),
            pltpu.VMEM((depth + GROUP, domain), jnp.bfloat16),
            pltpu.VMEM((domain, depth), jnp.bfloat16),
            pltpu.VMEM((held, GROUP), jnp.bfloat16),
            pltpu.VMEM(tiles, jnp.bfloat16),
            pltpu.VMEM(tiles, jnp.float32),
            pltpu.SemaphoreType.DMA((CAP,)),
            pltpu.SemaphoreType.DMA((groups,)),
            pltpu.SemaphoreType.DMA((2, share)),
        ],
        out_shape=[
            jax.ShapeDtypeStruct(tiles, jnp.bfloat16),
            jax.ShapeDtypeStruct(tiles, jnp.float32),
        ],
        compiler_params=pltpu.CompilerParams(vmem_limit_bytes=56 * 1024 * 1024),
        cost_estimate=pl.CostEstimate(
            flops=4 * share * TILE * TILE * depth + depth * GROUP * domain,
            bytes_accessed=3 * rows_total * domain + 6 * share * TILE * TILE,
            transcendentals=0,
        ),
        name="tile_chunk",
    )(info, codes, table, own_sorted, other_rows)


def pair_table(blocks):
    return jnp.asarray(
        [TILE * block for left in range(blocks) for right in range(left, blocks)
         for block in (left, right)],
        jnp.int32,
    )


def tile_plan(half_tensor, batch_owner, pair_list, live_pairs):
    batches = lax.axis_size("orb")
    rows = lax.axis_size("row")
    aux_local, occ_local, domain = half_tensor.shape
    share = pair_list.shape[1] // rows
    row_at = lax.axis_index("row")
    orb_at = lax.axis_index("orb")

    def exchange(array, axis, bits):
        size = lax.axis_size(axis)
        return lax.ppermute(array, axis, [(i, i ^ bits) for i in range(size)])

    def after(array, earlier):
        return lax.optimization_barrier((array, earlier))

    own_rows = half_tensor.reshape(aux_local * occ_local, domain)
    other_rows = exchange(own_rows, "row", 1)
    own_owner = batch_owner[:, 0]
    other_owner = exchange(own_owner, "row", 1)
    info = jnp.concatenate([jnp.stack([orb_at, row_at]), own_owner, other_owner])
    own_sorted = sort_rows(own_owner, own_rows, batches)
    own_codes = jnp.concatenate([pair_list[0], live_pairs])
    own_codes, own_sorted = after(own_codes, own_sorted)
    codes = {bits: exchange(own_codes, "orb", bits) for bits in (3, 2, 1)} | {0: own_codes}
    table = pair_table(domain // TILE)

    def chunk(bits):
        return tile_chunk(
            bits, info, codes[bits], table, own_sorted, other_rows, occ_local, share
        )

    def over_x(send, keep):
        return keep + exchange(send, "row", 2).astype(jnp.float32)

    send_3, keep_3 = chunk(3)
    send_2, keep_2 = chunk(2)
    send_1, keep_1 = chunk(1)
    far = over_x(send_3, keep_3).astype(jnp.bfloat16)
    other_rows, far = after(other_rows, far)
    far = exchange(far, "orb", 1)
    send_0, keep_0 = chunk(0)
    term_2 = over_x(send_2, keep_2)
    across = exchange((term_2 + far.astype(jnp.float32)).astype(jnp.bfloat16), "orb", 2)
    near = exchange(over_x(send_1, keep_1).astype(jnp.bfloat16), "orb", 1)
    total = over_x(send_0, keep_0) + near.astype(jnp.float32) + across.astype(jnp.float32)
    return total.astype(jnp.bfloat16)[None]


def per_device(half_tensor, batch_owner, pair_list, live_pairs):
    batches = lax.axis_size("orb")
    rows = lax.axis_size("row")
    aux_local, occ_local, domain = half_tensor.shape
    pair_total = pair_list.shape[1]
    tile_elements = batches * pair_total * TILE * TILE
    slab_elements = batches * CAP * aux_local * domain
    fits = (
        rows == ROWS
        and batches == 4
        and pair_total % rows == 0
        and occ_local & (occ_local - 1) == 0
        and GROUP % occ_local == 0
        and aux_local * occ_local % GROUP == 0
        and tile_elements <= slab_elements
    )
    plan = tile_plan if fits else slab_plan
    return plan(half_tensor, batch_owner, pair_list, live_pairs)


def solution(mesh):
    return jax.shard_map(
        per_device,
        mesh=mesh,
        in_specs=(
            P(("grp", "orb"), "row", None),
            P(("grp", "row"), None),
            P(("grp", "orb"), None),
            P(("grp", "orb")),
        ),
        out_specs=P(("grp", "orb"), "row", None, None),
        check_vma=False,
    )
```

```python
import functools
import math

import jax
import jax.numpy as jnp
from jax import lax
from jax.experimental import pallas as pl
from jax.experimental.pallas import tpu as pltpu
from jax.sharding import PartitionSpec as P

TILE = 128
CAP = 8
GROUP = 256
ROWS = 4


def block_pairs(pair_codes, blocks):
    row_grid = lax.broadcasted_iota(jnp.int32, (blocks, blocks), 0)
    col_grid = lax.broadcasted_iota(jnp.int32, (blocks, blocks), 1)
    code_grid = row_grid * blocks - row_grid * (row_grid - 1) // 2 + (col_grid - row_grid)
    upper_part = col_grid >= row_grid
    matches = (code_grid[None, :, :] == pair_codes[:, None, None]) & upper_part[None, :, :]
    first_blocks = jnp.sum(jnp.where(matches, row_grid[None], 0), axis=(1, 2))
    second_blocks = jnp.sum(jnp.where(matches, col_grid[None], 0), axis=(1, 2))
    return (first_blocks, second_blocks)


def slot_sources(owner_local, batches, capacity):
    local_count = owner_local.shape[0]
    batch_ids = lax.broadcasted_iota(jnp.int32, (local_count, batches), 1)
    onehot = (owner_local[:, None] == batch_ids).astype(jnp.int32)
    ranking = jnp.cumsum(onehot, axis=0) - 1
    slot_of = jnp.sum(ranking * onehot, axis=1)
    target = owner_local * capacity + slot_of
    slot_ids = lax.broadcasted_iota(jnp.int32, (local_count, batches * capacity), 1)
    orbital_ids = lax.broadcasted_iota(jnp.int32, (local_count, batches * capacity), 0)
    slot_hits = target[:, None] == slot_ids
    source_row = jnp.sum(jnp.where(slot_hits, orbital_ids, 0), axis=0)
    filled = jnp.any(slot_hits, axis=0)
    return jnp.where(filled, source_row, local_count)


def slab_plan(half_tensor, batch_owner, pair_list, live_pairs):
    batches = lax.axis_size("orb")
    aux_local, occ_local, domain = half_tensor.shape
    blocks = domain // TILE
    sources = slot_sources(batch_owner[:, 0], batches, CAP)
    block_major = half_tensor.reshape(aux_local, occ_local, blocks, TILE).transpose(2, 1, 0, 3)
    outgoing = jnp.take(block_major, sources, axis=1, mode="fill", fill_value=0)
    arrived = lax.all_to_all(outgoing, "orb", split_axis=1, concat_axis=2, tiled=True)
    stacked_rows = arrived.reshape(blocks, -1, TILE)
    first_blocks, second_blocks = block_pairs(pair_list[0], blocks)
    live_count = live_pairs[0]
    pair_total = pair_list.shape[1]
    contract = (((0,), (0,)), ((), ()))
    group_size = math.gcd(4, pair_total)

    def one_group(group_index):
        pair_start = group_index * group_size
        tiles = []
        for offset in range(group_size):
            left = lax.dynamic_index_in_dim(
                stacked_rows, first_blocks[pair_start + offset], 0, keepdims=False
            )
            right = lax.dynamic_index_in_dim(
                stacked_rows, second_blocks[pair_start + offset], 0, keepdims=False
            )
            tiles.append(
                lax.dot_general(left, right, contract, preferred_element_type=jnp.float32)
            )
        keep_mask = pair_start + lax.iota(jnp.int32, group_size) < live_count
        return jnp.where(keep_mask[:, None, None], jnp.stack(tiles, axis=0), jnp.float32(0.0))

    grouped = lax.map(one_group, jnp.arange(pair_total // group_size, dtype=jnp.int32))
    terms = grouped.reshape(pair_total, TILE, TILE)
    mine = lax.psum_scatter(terms.astype(jnp.bfloat16), "row", scatter_dimension=0, tiled=True)
    return mine[None]


def chunk_kernel(occ_local, share, info, codes, own_rows, other_rows, *refs):
    send_out, keep_out = refs[:2]
    stage, packed_rows, turned, pick, sums, send_ref, left_at, right_at = refs[2:10]
    arrived, left_off = refs[10:]
    rows_total, domain = own_rows.shape
    blocks = domain // TILE
    groups = rows_total // GROUP
    per_group = GROUP // occ_local
    held = per_group * CAP
    pair_total = share * ROWS
    live, batch = codes[pair_total], codes[pair_total + 1]

    def slab_copy(place):
        slab = own_rows if place < groups else other_rows
        return pltpu.make_async_copy(
            slab.at[pl.ds(place % groups * GROUP, GROUP), :],
            stage.at[pl.ds(place * GROUP, GROUP), :],
            arrived.at[place],
        )

    for place in range(2 * groups):
        slab_copy(place).start()

    lane = lax.broadcasted_iota(jnp.int32, (1, GROUP), 1)
    orbital_of = lane & (occ_local - 1)
    turn_of = lane >> (occ_local.bit_length() - 1)
    slot = lax.broadcasted_iota(jnp.int32, (held, GROUP), 0)
    counts = []
    for source in range(2):
        count = jnp.int32(0)
        rank = jnp.full((1, GROUP), -GROUP * CAP, jnp.int32)
        for orbital in range(occ_local):
            mine = info[1 + source * occ_local + orbital] == batch
            rank = jnp.where(orbital_of == orbital, jnp.where(mine, count, -GROUP * CAP), rank)
            count = count + mine.astype(jnp.int32)
        pick[source] = (slot == turn_of * count + rank).astype(jnp.bfloat16)
        counts.append(count)

    def decode(at, carry):
        first = jnp.where(at < share, info[0] ^ 2, info[0]) * share
        pair = first + jnp.where(at < share, at, at - share)
        code = codes[pair]
        left = jnp.int32(0)
        start = jnp.int32(0)
        for block in range(1, blocks):
            past = code >= block * blocks - block * (block - 1) // 2
            left = left + past.astype(jnp.int32)
            start = start + jnp.where(past, blocks - block + 1, 0)
        left_at[at] = jnp.where(pair < live, left * TILE, -1)
        right_at[at] = (code - start + left) * TILE
        return carry

    lax.fori_loop(0, 2 * share, decode, 0)

    def pack(place, carry):
        rows = pl.ds(pl.multiple_of(place * GROUP, GROUP), GROUP)
        pltpu.make_async_copy(
            own_rows.at[pl.ds(0, GROUP), :], stage.at[rows, :], arrived.at[place]
        ).wait()
        source = place // groups
        before = jnp.minimum(place, groups) * counts[0]
        before = before + jnp.maximum(place - groups, 0) * counts[1]
        start = pl.multiple_of(before * per_group, per_group)
        for column in range(0, domain, 2 * TILE):
            columns = slice(column, column + 2 * TILE)
            packed = jnp.dot(
                pick[source], stage[rows, columns], preferred_element_type=jnp.float32
            )
            packed_rows[pl.ds(start, held), columns] = packed.astype(jnp.bfloat16)
        return carry

    lax.fori_loop(0, 2 * groups, pack, 0)
    filled = pl.multiple_of((counts[0] + counts[1]) * groups * per_group, per_group)
    packed_rows[pl.ds(filled, GROUP), :] = jnp.zeros((GROUP, domain), jnp.bfloat16)
    parts = jnp.maximum((filled + GROUP - 1) // GROUP, 1)

    width = math.gcd(4, share)

    def out_copies(turn_at):
        sends = pl.ds(turn_at * width, width)
        keeps = pl.ds(share + turn_at * width, width)
        return (
            pltpu.make_async_copy(send_ref.at[sends], send_out.at[sends], left_off.at[0, turn_at]),
            pltpu.make_async_copy(sums.at[keeps], keep_out.at[sends], left_off.at[1, turn_at]),
        )

    def add_part(part, carry):
        rows = pl.ds(pl.multiple_of(part * GROUP, GROUP), GROUP)
        for column in range(0, domain, TILE):
            columns = slice(column, column + TILE)
            turned[columns, :] = packed_rows[rows, columns].T

        def several(turn_at, carry):
            for offset in range(2 * width):
                at = turn_at * width + offset % width + offset // width * share
                left = left_at[at]
                known = pl.multiple_of(jnp.maximum(left, 0), TILE)
                right = pl.multiple_of(right_at[at], TILE)
                product = jnp.dot(
                    turned[pl.ds(known, TILE), :],
                    packed_rows[rows, pl.ds(right, TILE)],
                    preferred_element_type=jnp.float32,
                )
                product = jnp.where(left >= 0, product, jnp.float32(0.0))
                sums[at] = jnp.where(part > 0, sums[at], jnp.float32(0.0)) + product

            @pl.when(part == parts - 1)
            def _():
                sends = pl.ds(turn_at * width, width)
                send_ref[sends] = sums[sends].astype(send_ref.dtype)
                for copy in out_copies(turn_at):
                    copy.start()

            return carry

        lax.fori_loop(0, share // width, several, 0)
        return carry

    lax.fori_loop(0, parts, add_part, 0)
    for turn_at in range(share // width):
        for copy in out_copies(turn_at):
            copy.wait()


def tile_chunk(info, codes, own_rows, other_rows, occ_local, share):
    rows_total, domain = own_rows.shape
    groups = rows_total // GROUP
    held = GROUP // occ_local * CAP
    depth = 2 * groups * held
    tiles = (share, TILE, TILE)
    anywhere = pl.BlockSpec(memory_space=pl.ANY)
    in_smem = pl.BlockSpec(memory_space=pltpu.SMEM)
    return pl.pallas_call(
        functools.partial(chunk_kernel, occ_local, share),
        in_specs=[in_smem, in_smem, anywhere, anywhere],
        out_specs=[anywhere, anywhere],
        scratch_shapes=[
            pltpu.VMEM((2 * rows_total, domain), jnp.bfloat16),
            pltpu.VMEM((depth + GROUP, domain), jnp.bfloat16),
            pltpu.VMEM((domain, GROUP), jnp.bfloat16),
            pltpu.VMEM((2, held, GROUP), jnp.bfloat16),
            pltpu.VMEM((2 * share, TILE, TILE), jnp.float32),
            pltpu.VMEM(tiles, jnp.bfloat16),
            pltpu.SMEM((2 * share,), jnp.int32),
            pltpu.SMEM((2 * share,), jnp.int32),
            pltpu.SemaphoreType.DMA((2 * groups,)),
            pltpu.SemaphoreType.DMA((2, share)),
        ],
        out_shape=[
            jax.ShapeDtypeStruct(tiles, jnp.bfloat16),
            jax.ShapeDtypeStruct(tiles, jnp.float32),
        ],
        compiler_params=pltpu.CompilerParams(vmem_limit_bytes=56 * 1024 * 1024),
        cost_estimate=pl.CostEstimate(
            flops=4 * share * TILE * TILE * depth + 2 * depth * GROUP * domain,
            bytes_accessed=4 * rows_total * domain + 6 * share * TILE * TILE,
            transcendentals=0,
        ),
        name="tile_chunk",
    )(info, codes, own_rows, other_rows)


def tile_plan(half_tensor, batch_owner, pair_list, live_pairs):
    batches = lax.axis_size("orb")
    rows = lax.axis_size("row")
    aux_local, occ_local, domain = half_tensor.shape
    share = pair_list.shape[1] // rows
    row_at = lax.axis_index("row")
    orb_at = lax.axis_index("orb")

    def exchange(array, axis, bits):
        size = lax.axis_size(axis)
        return lax.ppermute(array, axis, [(i, i ^ bits) for i in range(size)])

    def after(array, earlier):
        return lax.optimization_barrier((array, earlier))

    def after(array, earlier):
        return lax.optimization_barrier((array, earlier))

    own_rows = half_tensor.reshape(aux_local * occ_local, domain)
    other_rows = exchange(own_rows, "row", 1)
    own_owner = batch_owner[:, 0]
    other_owner = exchange(own_owner, "row", 1)
    info = jnp.concatenate([row_at[None], own_owner, other_owner])
    own_codes = jnp.concatenate([pair_list[0], live_pairs, orb_at[None]])
    codes = [exchange(own_codes, "orb", bits) for bits in (3, 2, 1)]
    codes = lax.optimization_barrier(tuple(codes))[::-1]
    codes = (own_codes, *codes)

    def chunk(bits):
        return tile_chunk(info, codes[bits], own_rows, other_rows, occ_local, share)

    def over_x(send, keep):
        return keep + exchange(send, "row", 2).astype(jnp.float32)

    send_3, keep_3 = chunk(3)
    send_2, keep_2 = chunk(2)
    far = over_x(send_3, keep_3).astype(jnp.bfloat16)
    other_rows, far = after(other_rows, far)
    far = exchange(far, "orb", 1)
    send_1, keep_1 = chunk(1)
    across = (over_x(send_2, keep_2) + far.astype(jnp.float32)).astype(jnp.bfloat16)
    other_rows, across = after(other_rows, across)
    across = exchange(across, "orb", 2)
    send_0, keep_0 = chunk(0)
    near = exchange(over_x(send_1, keep_1).astype(jnp.bfloat16), "orb", 1)
    beside = near.astype(jnp.float32) + across.astype(jnp.float32)
    beside, keep_0 = after(beside, keep_0)
    total = over_x(send_0, keep_0) + beside
    return total.astype(jnp.bfloat16)[None]


def per_device(half_tensor, batch_owner, pair_list, live_pairs):
    batches = lax.axis_size("orb")
    rows = lax.axis_size("row")
    aux_local, occ_local, domain = half_tensor.shape
    pair_total = pair_list.shape[1]
    tile_elements = batches * pair_total * TILE * TILE
    slab_elements = batches * CAP * aux_local * domain
    fits = (
        rows == ROWS
        and batches == 4
        and pair_total % rows == 0
        and occ_local & (occ_local - 1) == 0
        and GROUP % occ_local == 0
        and aux_local * occ_local % GROUP == 0
        and tile_elements <= slab_elements
    )
    plan = tile_plan if fits else slab_plan
    return plan(half_tensor, batch_owner, pair_list, live_pairs)


def solution(mesh):
    return jax.shard_map(
        per_device,
        mesh=mesh,
        in_specs=(
            P(("grp", "orb"), "row", None),
            P(("grp", "row"), None),
            P(("grp", "orb"), None),
            P(("grp", "orb")),
        ),
        out_specs=P(("grp", "orb"), "row", None, None),
        check_vma=False,
    )
```

```python
import functools
import math

import jax
import jax.numpy as jnp
from jax import lax
from jax.experimental import pallas as pl
from jax.experimental.pallas import tpu as pltpu
from jax.sharding import PartitionSpec as P

TILE = 128
CAP = 8
GROUP = 256
ROWS = 4


def block_pairs(pair_codes, blocks):
    row_grid = lax.broadcasted_iota(jnp.int32, (blocks, blocks), 0)
    col_grid = lax.broadcasted_iota(jnp.int32, (blocks, blocks), 1)
    code_grid = row_grid * blocks - row_grid * (row_grid - 1) // 2 + (col_grid - row_grid)
    upper_part = col_grid >= row_grid
    matches = (code_grid[None, :, :] == pair_codes[:, None, None]) & upper_part[None, :, :]
    first_blocks = jnp.sum(jnp.where(matches, row_grid[None], 0), axis=(1, 2))
    second_blocks = jnp.sum(jnp.where(matches, col_grid[None], 0), axis=(1, 2))
    return (first_blocks, second_blocks)


def slot_sources(owner_local, batches, capacity):
    local_count = owner_local.shape[0]
    batch_ids = lax.broadcasted_iota(jnp.int32, (local_count, batches), 1)
    onehot = (owner_local[:, None] == batch_ids).astype(jnp.int32)
    ranking = jnp.cumsum(onehot, axis=0) - 1
    slot_of = jnp.sum(ranking * onehot, axis=1)
    target = owner_local * capacity + slot_of
    slot_ids = lax.broadcasted_iota(jnp.int32, (local_count, batches * capacity), 1)
    orbital_ids = lax.broadcasted_iota(jnp.int32, (local_count, batches * capacity), 0)
    slot_hits = target[:, None] == slot_ids
    source_row = jnp.sum(jnp.where(slot_hits, orbital_ids, 0), axis=0)
    filled = jnp.any(slot_hits, axis=0)
    return jnp.where(filled, source_row, local_count)


def slab_plan(half_tensor, batch_owner, pair_list, live_pairs):
    batches = lax.axis_size("orb")
    aux_local, occ_local, domain = half_tensor.shape
    blocks = domain // TILE
    sources = slot_sources(batch_owner[:, 0], batches, CAP)
    block_major = half_tensor.reshape(aux_local, occ_local, blocks, TILE).transpose(2, 1, 0, 3)
    outgoing = jnp.take(block_major, sources, axis=1, mode="fill", fill_value=0)
    arrived = lax.all_to_all(outgoing, "orb", split_axis=1, concat_axis=2, tiled=True)
    stacked_rows = arrived.reshape(blocks, -1, TILE)
    first_blocks, second_blocks = block_pairs(pair_list[0], blocks)
    live_count = live_pairs[0]
    pair_total = pair_list.shape[1]
    contract = (((0,), (0,)), ((), ()))
    group_size = math.gcd(4, pair_total)

    def one_group(group_index):
        pair_start = group_index * group_size
        tiles = []
        for offset in range(group_size):
            left = lax.dynamic_index_in_dim(
                stacked_rows, first_blocks[pair_start + offset], 0, keepdims=False
            )
            right = lax.dynamic_index_in_dim(
                stacked_rows, second_blocks[pair_start + offset], 0, keepdims=False
            )
            tiles.append(
                lax.dot_general(left, right, contract, preferred_element_type=jnp.float32)
            )
        keep_mask = pair_start + lax.iota(jnp.int32, group_size) < live_count
        return jnp.where(keep_mask[:, None, None], jnp.stack(tiles, axis=0), jnp.float32(0.0))

    grouped = lax.map(one_group, jnp.arange(pair_total // group_size, dtype=jnp.int32))
    terms = grouped.reshape(pair_total, TILE, TILE)
    mine = lax.psum_scatter(terms.astype(jnp.bfloat16), "row", scatter_dimension=0, tiled=True)
    return mine[None]


def chunk_kernel(occ_local, share, own_owner, other_owner, codes, own_rows, other_rows, *refs):
    send_out, keep_out = refs[:2]
    stage, packed_rows, turned, pick, sums, send_ref, left_at, right_at = refs[2:10]
    arrived, left_off = refs[10:]
    rows_total, domain = own_rows.shape
    blocks = domain // TILE
    groups = rows_total // GROUP
    per_group = GROUP // occ_local
    held = per_group * CAP
    pair_total = share * ROWS
    live, batch = codes[pair_total], codes[pair_total + 1]

    def slab_copy(place):
        slab = own_rows if place < groups else other_rows
        return pltpu.make_async_copy(
            slab.at[pl.ds(place % groups * GROUP, GROUP), :],
            stage.at[pl.ds(place * GROUP, GROUP), :],
            arrived.at[place],
        )

    for place in range(2 * groups):
        slab_copy(place).start()

    lane = lax.broadcasted_iota(jnp.int32, (1, GROUP), 1)
    orbital_of = lane & (occ_local - 1)
    turn_of = lane >> (occ_local.bit_length() - 1)
    slot = lax.broadcasted_iota(jnp.int32, (held, GROUP), 0)
    counts = []
    for source, owner in enumerate((own_owner, other_owner)):
        count = jnp.int32(0)
        rank = jnp.full((1, GROUP), -GROUP * CAP, jnp.int32)
        for orbital in range(occ_local):
            mine = owner[orbital] == batch
            rank = jnp.where(orbital_of == orbital, jnp.where(mine, count, -GROUP * CAP), rank)
            count = count + mine.astype(jnp.int32)
        pick[source] = (slot == turn_of * count + rank).astype(jnp.bfloat16)
        counts.append(count)

    row_at = lax.axis_index("row")

    def decode(at, carry):
        first = jnp.where(at < share, row_at ^ 2, row_at) * share
        pair = first + jnp.where(at < share, at, at - share)
        code = codes[pair]
        left = jnp.int32(0)
        start = jnp.int32(0)
        for block in range(1, blocks):
            past = code >= block * blocks - block * (block - 1) // 2
            left = left + past.astype(jnp.int32)
            start = start + jnp.where(past, blocks - block + 1, 0)
        left_at[at] = jnp.where(pair < live, left * TILE, domain)
        right_at[at] = (code - start + left) * TILE
        return carry

    lax.fori_loop(0, 2 * share, decode, 0)
    sums[...] = jnp.zeros(sums.shape, jnp.float32)
    turned[domain:, :] = jnp.zeros((TILE, GROUP), jnp.bfloat16)

    def pack(place, carry):
        rows = pl.ds(pl.multiple_of(place * GROUP, GROUP), GROUP)
        pltpu.make_async_copy(
            own_rows.at[pl.ds(0, GROUP), :], stage.at[rows, :], arrived.at[place]
        ).wait()
        source = place // groups
        before = jnp.minimum(place, groups) * counts[0]
        before = before + jnp.maximum(place - groups, 0) * counts[1]
        start = pl.multiple_of(before * per_group, per_group)
        for column in range(0, domain, 2 * TILE):
            columns = slice(column, column + 2 * TILE)
            packed = jnp.dot(
                pick[source], stage[rows, columns], preferred_element_type=jnp.float32
            )
            packed_rows[pl.ds(start, held), columns] = packed.astype(jnp.bfloat16)
        return carry

    lax.fori_loop(0, 2 * groups, pack, 0)
    filled = pl.multiple_of((counts[0] + counts[1]) * groups * per_group, per_group)
    packed_rows[pl.ds(filled, GROUP), :] = jnp.zeros((GROUP, domain), jnp.bfloat16)
    parts = jnp.maximum((filled + GROUP - 1) // GROUP, 1)

    width = math.gcd(4, share)

    def out_copies(turn_at):
        sends = pl.ds(turn_at * width, width)
        keeps = pl.ds(share + turn_at * width, width)
        return (
            pltpu.make_async_copy(send_ref.at[sends], send_out.at[sends], left_off.at[0, turn_at]),
            pltpu.make_async_copy(sums.at[keeps], keep_out.at[sends], left_off.at[1, turn_at]),
        )

    def add_part(part, carry):
        rows = pl.ds(pl.multiple_of(part * GROUP, GROUP), GROUP)
        for column in range(0, domain, TILE):
            columns = slice(column, column + TILE)
            turned[columns, :] = packed_rows[rows, columns].T

        for turn_at in range(share // width):
            sends = slice(turn_at * width, (turn_at + 1) * width)
            for offset in range(width):
                for at in (sends.start + offset, share + sends.start + offset):
                    left = pl.multiple_of(left_at[at], TILE)
                    right = pl.multiple_of(right_at[at], TILE)
                    sums[at] += jnp.dot(
                        turned[pl.ds(left, TILE), :],
                        packed_rows[rows, pl.ds(right, TILE)],
                        preferred_element_type=jnp.float32,
                    )

            @pl.when(part == parts - 1)
            def _(turn_at=turn_at, sends=sends):
                send_ref[sends] = sums[sends].astype(send_ref.dtype)
                for copy in out_copies(turn_at):
                    copy.start()

        return carry

    lax.fori_loop(0, parts, add_part, 0)
    for turn_at in range(share // width):
        for copy in out_copies(turn_at):
            copy.wait()


def tile_chunk(owners, codes, own_rows, other_rows, occ_local, share):
    rows_total, domain = own_rows.shape
    groups = rows_total // GROUP
    held = GROUP // occ_local * CAP
    depth = 2 * groups * held
    tiles = (share, TILE, TILE)
    anywhere = pl.BlockSpec(memory_space=pl.ANY)
    in_smem = pl.BlockSpec(memory_space=pltpu.SMEM)
    return pl.pallas_call(
        functools.partial(chunk_kernel, occ_local, share),
        in_specs=[in_smem] * 3 + [anywhere] * 2,
        out_specs=[anywhere, anywhere],
        scratch_shapes=[
            pltpu.VMEM((2 * rows_total, domain), jnp.bfloat16),
            pltpu.VMEM((depth + GROUP, domain), jnp.bfloat16),
            pltpu.VMEM((domain + TILE, GROUP), jnp.bfloat16),
            pltpu.VMEM((2, held, GROUP), jnp.bfloat16),
            pltpu.VMEM((2 * share, TILE, TILE), jnp.float32),
            pltpu.VMEM(tiles, jnp.bfloat16),
            pltpu.SMEM((2 * share,), jnp.int32),
            pltpu.SMEM((2 * share,), jnp.int32),
            pltpu.SemaphoreType.DMA((2 * groups,)),
            pltpu.SemaphoreType.DMA((2, share)),
        ],
        out_shape=[
            jax.ShapeDtypeStruct(tiles, jnp.bfloat16),
            jax.ShapeDtypeStruct(tiles, jnp.float32),
        ],
        compiler_params=pltpu.CompilerParams(vmem_limit_bytes=56 * 1024 * 1024),
        cost_estimate=pl.CostEstimate(
            flops=4 * share * TILE * TILE * depth + 2 * depth * GROUP * domain,
            bytes_accessed=4 * rows_total * domain + 6 * share * TILE * TILE,
            transcendentals=0,
        ),
        name="tile_chunk",
    )(*owners, codes, own_rows, other_rows)


def tile_plan(half_tensor, batch_owner, pair_list, live_pairs):
    batches = lax.axis_size("orb")
    rows = lax.axis_size("row")
    aux_local, occ_local, domain = half_tensor.shape
    share = pair_list.shape[1] // rows
    orb_at = lax.axis_index("orb")

    def exchange(array, axis, bits):
        size = lax.axis_size(axis)
        return lax.ppermute(array, axis, [(i, i ^ bits) for i in range(size)])

    def after(array, earlier):
        return lax.optimization_barrier((array, earlier))

    def after(array, earlier):
        return lax.optimization_barrier((array, earlier))

    own_rows = half_tensor.reshape(aux_local * occ_local, domain)
    other_rows = exchange(own_rows, "row", 1)
    own_owner = batch_owner[:, 0]
    owners = own_owner, exchange(own_owner, "row", 1)
    own_codes = jnp.concatenate([pair_list[0], live_pairs, orb_at[None]])
    codes = [exchange(own_codes, "orb", bits) for bits in (3, 2, 1)]
    codes = lax.optimization_barrier(tuple(codes))[::-1]
    codes = (own_codes, *codes)

    def chunk(bits):
        return tile_chunk(owners, codes[bits], own_rows, other_rows, occ_local, share)

    def over_x(send, keep):
        return keep + exchange(send, "row", 2).astype(jnp.float32)

    send_3, keep_3 = chunk(3)
    send_2, keep_2 = chunk(2)
    far = over_x(send_3, keep_3).astype(jnp.bfloat16)
    other_rows, far = after(other_rows, far)
    far = exchange(far, "orb", 1)
    send_1, keep_1 = chunk(1)
    across = (over_x(send_2, keep_2) + far.astype(jnp.float32)).astype(jnp.bfloat16)
    other_rows, across = after(other_rows, across)
    across = exchange(across, "orb", 2)
    send_0, keep_0 = chunk(0)
    keep_1, send_0 = after(keep_1, send_0)
    near = exchange(over_x(send_1, keep_1).astype(jnp.bfloat16), "orb", 1)
    beside = near.astype(jnp.float32) + across.astype(jnp.float32)
    beside, keep_0 = after(beside, keep_0)
    total = over_x(send_0, keep_0) + beside
    return total.astype(jnp.bfloat16)[None]


def per_device(half_tensor, batch_owner, pair_list, live_pairs):
    batches = lax.axis_size("orb")
    rows = lax.axis_size("row")
    aux_local, occ_local, domain = half_tensor.shape
    pair_total = pair_list.shape[1]
    tile_elements = batches * pair_total * TILE * TILE
    slab_elements = batches * CAP * aux_local * domain
    fits = (
        rows == ROWS
        and batches == 4
        and pair_total % rows == 0
        and occ_local & (occ_local - 1) == 0
        and GROUP % occ_local == 0
        and aux_local * occ_local % GROUP == 0
        and tile_elements <= slab_elements
    )
    plan = tile_plan if fits else slab_plan
    return plan(half_tensor, batch_owner, pair_list, live_pairs)


def solution(mesh):
    return jax.shard_map(
        per_device,
        mesh=mesh,
        in_specs=(
            P(("grp", "orb"), "row", None),
            P(("grp", "row"), None),
            P(("grp", "orb"), None),
            P(("grp", "orb")),
        ),
        out_specs=P(("grp", "orb"), "row", None, None),
        check_vma=False,
    )
```

```python
import functools
import math

import jax
import jax.numpy as jnp
from jax import lax
from jax.experimental import pallas as pl
from jax.experimental.pallas import tpu as pltpu
from jax.sharding import PartitionSpec as P

TILE = 128
CAP = 8
GROUP = 256
PART = 512
ROWS = 4


def block_pairs(pair_codes, blocks):
    row_grid = lax.broadcasted_iota(jnp.int32, (blocks, blocks), 0)
    col_grid = lax.broadcasted_iota(jnp.int32, (blocks, blocks), 1)
    code_grid = row_grid * blocks - row_grid * (row_grid - 1) // 2 + (col_grid - row_grid)
    upper_part = col_grid >= row_grid
    matches = (code_grid[None, :, :] == pair_codes[:, None, None]) & upper_part[None, :, :]
    first_blocks = jnp.sum(jnp.where(matches, row_grid[None], 0), axis=(1, 2))
    second_blocks = jnp.sum(jnp.where(matches, col_grid[None], 0), axis=(1, 2))
    return (first_blocks, second_blocks)


def slot_sources(owner_local, batches, capacity):
    local_count = owner_local.shape[0]
    batch_ids = lax.broadcasted_iota(jnp.int32, (local_count, batches), 1)
    onehot = (owner_local[:, None] == batch_ids).astype(jnp.int32)
    ranking = jnp.cumsum(onehot, axis=0) - 1
    slot_of = jnp.sum(ranking * onehot, axis=1)
    target = owner_local * capacity + slot_of
    slot_ids = lax.broadcasted_iota(jnp.int32, (local_count, batches * capacity), 1)
    orbital_ids = lax.broadcasted_iota(jnp.int32, (local_count, batches * capacity), 0)
    slot_hits = target[:, None] == slot_ids
    source_row = jnp.sum(jnp.where(slot_hits, orbital_ids, 0), axis=0)
    filled = jnp.any(slot_hits, axis=0)
    return jnp.where(filled, source_row, local_count)


def slab_plan(half_tensor, batch_owner, pair_list, live_pairs):
    batches = lax.axis_size("orb")
    aux_local, occ_local, domain = half_tensor.shape
    blocks = domain // TILE
    sources = slot_sources(batch_owner[:, 0], batches, CAP)
    block_major = half_tensor.reshape(aux_local, occ_local, blocks, TILE).transpose(2, 1, 0, 3)
    outgoing = jnp.take(block_major, sources, axis=1, mode="fill", fill_value=0)
    arrived = lax.all_to_all(outgoing, "orb", split_axis=1, concat_axis=2, tiled=True)
    stacked_rows = arrived.reshape(blocks, -1, TILE)
    first_blocks, second_blocks = block_pairs(pair_list[0], blocks)
    live_count = live_pairs[0]
    pair_total = pair_list.shape[1]
    contract = (((0,), (0,)), ((), ()))
    group_size = math.gcd(4, pair_total)

    def one_group(group_index):
        pair_start = group_index * group_size
        tiles = []
        for offset in range(group_size):
            left = lax.dynamic_index_in_dim(
                stacked_rows, first_blocks[pair_start + offset], 0, keepdims=False
            )
            right = lax.dynamic_index_in_dim(
                stacked_rows, second_blocks[pair_start + offset], 0, keepdims=False
            )
            tiles.append(
                lax.dot_general(left, right, contract, preferred_element_type=jnp.float32)
            )
        keep_mask = pair_start + lax.iota(jnp.int32, group_size) < live_count
        return jnp.where(keep_mask[:, None, None], jnp.stack(tiles, axis=0), jnp.float32(0.0))

    grouped = lax.map(one_group, jnp.arange(pair_total // group_size, dtype=jnp.int32))
    terms = grouped.reshape(pair_total, TILE, TILE)
    mine = lax.psum_scatter(terms.astype(jnp.bfloat16), "row", scatter_dimension=0, tiled=True)
    return mine[None]


def chunk_kernel(occ_local, share, own_owner, other_owner, codes, own_rows, other_rows, *refs):
    send_ref, keep_ref, packed_rows, turned, pick, partial_send, left_at, right_at = refs
    rows_total, domain = own_rows.shape
    blocks = domain // TILE
    groups = rows_total // GROUP
    per_group = GROUP // occ_local
    held = per_group * CAP
    pair_total = share * ROWS
    live, batch = codes[pair_total], codes[pair_total + 1]

    lane = lax.broadcasted_iota(jnp.int32, (1, GROUP), 1)
    orbital_of = lane & (occ_local - 1)
    turn_of = lane >> (occ_local.bit_length() - 1)
    slot = lax.broadcasted_iota(jnp.int32, (held, GROUP), 0)
    counts = []
    for source, owner in enumerate((own_owner, other_owner)):
        count = jnp.int32(0)
        rank = jnp.full((1, GROUP), -GROUP * CAP, jnp.int32)
        for orbital in range(occ_local):
            mine = owner[orbital] == batch
            rank = jnp.where(orbital_of == orbital, jnp.where(mine, count, -GROUP * CAP), rank)
            count = count + mine.astype(jnp.int32)
        pick[source] = (slot == turn_of * count + rank).astype(jnp.bfloat16)
        counts.append(count)

    row_at = lax.axis_index("row")

    def decode(at, carry):
        first = jnp.where(at < share, row_at ^ 2, row_at) * share
        pair = first + jnp.where(at < share, at, at - share)
        code = codes[pair]
        left = jnp.int32(0)
        start = jnp.int32(0)
        for block in range(1, blocks):
            past = code >= block * blocks - block * (block - 1) // 2
            left = left + past.astype(jnp.int32)
            start = start + jnp.where(past, blocks - block + 1, 0)
        left_at[at] = jnp.where(pair < live, left * TILE, domain)
        right_at[at] = (code - start + left) * TILE
        return carry

    lax.fori_loop(0, 2 * share, decode, 0)
    turned[domain:, :] = jnp.zeros((TILE, PART), jnp.bfloat16)

    before = jnp.int32(0)
    for source, slab in enumerate((own_rows, other_rows)):
        def pack(group, carry, source=source, slab=slab, before=before):
            rows = pl.ds(pl.multiple_of(group * GROUP, GROUP), GROUP)
            start = pl.multiple_of((before + group * counts[source]) * per_group, per_group)
            for column in range(0, domain, 2 * TILE):
                columns = slice(column, column + 2 * TILE)
                packed = jnp.dot(
                    pick[source], slab[rows, columns], preferred_element_type=jnp.float32
                )
                packed_rows[pl.ds(start, held), columns] = packed.astype(jnp.bfloat16)
            return carry

        lax.fori_loop(0, groups, pack, 0)
        before = before + groups * counts[source]

    filled = pl.multiple_of(before * per_group, per_group)
    packed_rows[pl.ds(filled, PART), :] = jnp.zeros((PART, domain), jnp.bfloat16)
    parts = jnp.maximum((filled + PART - 1) // PART, 1)

    width = math.gcd(4, share)

    def add_part(part, fresh):
        rows = pl.ds(pl.multiple_of(part * PART, PART), PART)
        for column in range(0, domain, TILE):
            columns = slice(column, column + TILE)
            turned[columns, :] = packed_rows[rows, columns].T

        def product(at):
            left = pl.multiple_of(left_at[at], TILE)
            right = pl.multiple_of(right_at[at], TILE)
            return jnp.dot(
                turned[pl.ds(left, TILE), :],
                packed_rows[rows, pl.ds(right, TILE)],
                preferred_element_type=jnp.float32,
            )

        def several(turn_at, carry):
            for offset in range(width):
                at = turn_at * width + offset
                sent, kept = product(at), product(share + at)
                if not fresh:
                    sent, kept = sent + partial_send[at], kept + keep_ref[at]
                send_ref[at] = sent.astype(send_ref.dtype)
                partial_send[at] = sent
                keep_ref[at] = kept
            return carry

        lax.fori_loop(0, share // width, several, 0)

    add_part(0, True)

    def more(part, carry):
        add_part(part, False)
        return carry

    lax.fori_loop(1, parts, more, 0)


def tile_chunk(owners, codes, own_rows, other_rows, occ_local, share):
    rows_total, domain = own_rows.shape
    groups = rows_total // GROUP
    held = GROUP // occ_local * CAP
    depth = 2 * groups * held
    tiles = (share, TILE, TILE)
    in_vmem = pl.BlockSpec(memory_space=pltpu.VMEM)
    in_smem = pl.BlockSpec(memory_space=pltpu.SMEM)
    return pl.pallas_call(
        functools.partial(chunk_kernel, occ_local, share),
        in_specs=[in_smem] * 3 + [in_vmem] * 2,
        out_specs=[in_vmem, in_vmem],
        scratch_shapes=[
            pltpu.VMEM((depth + PART, domain), jnp.bfloat16),
            pltpu.VMEM((domain + TILE, PART), jnp.bfloat16),
            pltpu.VMEM((2, held, GROUP), jnp.bfloat16),
            pltpu.VMEM(tiles, jnp.float32),
            pltpu.SMEM((2 * share,), jnp.int32),
            pltpu.SMEM((2 * share,), jnp.int32),
        ],
        out_shape=[
            jax.ShapeDtypeStruct(tiles, jnp.bfloat16),
            jax.ShapeDtypeStruct(tiles, jnp.float32),
        ],
        compiler_params=pltpu.CompilerParams(vmem_limit_bytes=24 * 1024 * 1024),
        cost_estimate=pl.CostEstimate(
            flops=4 * share * TILE * TILE * depth + 2 * depth * GROUP * domain,
            bytes_accessed=4 * rows_total * domain + 6 * share * TILE * TILE,
            transcendentals=0,
        ),
        name="tile_chunk",
    )(*owners, codes, own_rows, other_rows)


def tile_plan(half_tensor, batch_owner, pair_list, live_pairs):
    batches = lax.axis_size("orb")
    rows = lax.axis_size("row")
    aux_local, occ_local, domain = half_tensor.shape
    share = pair_list.shape[1] // rows
    orb_at = lax.axis_index("orb")

    def exchange(array, axis, bits):
        size = lax.axis_size(axis)
        return lax.ppermute(array, axis, [(i, i ^ bits) for i in range(size)])

    def after(array, earlier):
        return lax.optimization_barrier((array, earlier))

    def after(array, earlier):
        return lax.optimization_barrier((array, earlier))

    own_rows = half_tensor.reshape(aux_local * occ_local, domain)
    other_rows = exchange(own_rows, "row", 1)
    own_owner = batch_owner[:, 0]
    owners = own_owner, exchange(own_owner, "row", 1)
    own_codes = jnp.concatenate([pair_list[0], live_pairs, orb_at[None]])
    codes = [exchange(own_codes, "orb", bits) for bits in (3, 2, 1)]
    codes = lax.optimization_barrier(tuple(codes))[::-1]
    codes = (own_codes, *codes)

    def chunk(bits):
        return tile_chunk(owners, codes[bits], own_rows, other_rows, occ_local, share)

    def over_x(send, keep):
        return keep + exchange(send, "row", 2).astype(jnp.float32)

    send_3, keep_3 = chunk(3)
    send_2, keep_2 = chunk(2)
    far = over_x(send_3, keep_3).astype(jnp.bfloat16)
    other_rows, far = after(other_rows, far)
    far = exchange(far, "orb", 1)
    send_1, keep_1 = chunk(1)
    across = (over_x(send_2, keep_2) + far.astype(jnp.float32)).astype(jnp.bfloat16)
    other_rows, across = after(other_rows, across)
    across = exchange(across, "orb", 2)
    send_0, keep_0 = chunk(0)
    keep_1, send_0 = after(keep_1, send_0)
    near = exchange(over_x(send_1, keep_1).astype(jnp.bfloat16), "orb", 1)
    beside = near.astype(jnp.float32) + across.astype(jnp.float32)
    beside, keep_0 = after(beside, keep_0)
    total = over_x(send_0, keep_0) + beside
    return total.astype(jnp.bfloat16)[None]


def per_device(half_tensor, batch_owner, pair_list, live_pairs):
    batches = lax.axis_size("orb")
    rows = lax.axis_size("row")
    aux_local, occ_local, domain = half_tensor.shape
    pair_total = pair_list.shape[1]
    tile_elements = batches * pair_total * TILE * TILE
    slab_elements = batches * CAP * aux_local * domain
    fits = (
        rows == ROWS
        and batches == 4
        and pair_total % rows == 0
        and occ_local & (occ_local - 1) == 0
        and GROUP % occ_local == 0
        and aux_local * occ_local % GROUP == 0
        and tile_elements <= slab_elements
    )
    plan = tile_plan if fits else slab_plan
    return plan(half_tensor, batch_owner, pair_list, live_pairs)


def solution(mesh):
    return jax.shard_map(
        per_device,
        mesh=mesh,
        in_specs=(
            P(("grp", "orb"), "row", None),
            P(("grp", "row"), None),
            P(("grp", "orb"), None),
            P(("grp", "orb")),
        ),
        out_specs=P(("grp", "orb"), "row", None, None),
        check_vma=False,
    )
```

```python
import functools
import math

import jax
import jax.numpy as jnp
from jax import lax
from jax.experimental import pallas as pl
from jax.experimental.pallas import tpu as pltpu
from jax.sharding import PartitionSpec as P

TILE = 128
CAP = 8
GROUP = 256
PART = 512
ROWS = 4
SHIFT = 16


def block_pairs(pair_codes, blocks):
    row_grid = lax.broadcasted_iota(jnp.int32, (blocks, blocks), 0)
    col_grid = lax.broadcasted_iota(jnp.int32, (blocks, blocks), 1)
    code_grid = row_grid * blocks - row_grid * (row_grid - 1) // 2 + (col_grid - row_grid)
    upper_part = col_grid >= row_grid
    matches = (code_grid[None, :, :] == pair_codes[:, None, None]) & upper_part[None, :, :]
    first_blocks = jnp.sum(jnp.where(matches, row_grid[None], 0), axis=(1, 2))
    second_blocks = jnp.sum(jnp.where(matches, col_grid[None], 0), axis=(1, 2))
    return (first_blocks, second_blocks)


def slot_sources(owner_local, batches, capacity):
    local_count = owner_local.shape[0]
    batch_ids = lax.broadcasted_iota(jnp.int32, (local_count, batches), 1)
    onehot = (owner_local[:, None] == batch_ids).astype(jnp.int32)
    ranking = jnp.cumsum(onehot, axis=0) - 1
    slot_of = jnp.sum(ranking * onehot, axis=1)
    target = owner_local * capacity + slot_of
    slot_ids = lax.broadcasted_iota(jnp.int32, (local_count, batches * capacity), 1)
    orbital_ids = lax.broadcasted_iota(jnp.int32, (local_count, batches * capacity), 0)
    slot_hits = target[:, None] == slot_ids
    source_row = jnp.sum(jnp.where(slot_hits, orbital_ids, 0), axis=0)
    filled = jnp.any(slot_hits, axis=0)
    return jnp.where(filled, source_row, local_count)


def slab_plan(half_tensor, batch_owner, pair_list, live_pairs):
    batches = lax.axis_size("orb")
    aux_local, occ_local, domain = half_tensor.shape
    blocks = domain // TILE
    sources = slot_sources(batch_owner[:, 0], batches, CAP)
    block_major = half_tensor.reshape(aux_local, occ_local, blocks, TILE).transpose(2, 1, 0, 3)
    outgoing = jnp.take(block_major, sources, axis=1, mode="fill", fill_value=0)
    arrived = lax.all_to_all(outgoing, "orb", split_axis=1, concat_axis=2, tiled=True)
    stacked_rows = arrived.reshape(blocks, -1, TILE)
    first_blocks, second_blocks = block_pairs(pair_list[0], blocks)
    live_count = live_pairs[0]
    pair_total = pair_list.shape[1]
    contract = (((0,), (0,)), ((), ()))
    group_size = math.gcd(4, pair_total)

    def one_group(group_index):
        pair_start = group_index * group_size
        tiles = []
        for offset in range(group_size):
            left = lax.dynamic_index_in_dim(
                stacked_rows, first_blocks[pair_start + offset], 0, keepdims=False
            )
            right = lax.dynamic_index_in_dim(
                stacked_rows, second_blocks[pair_start + offset], 0, keepdims=False
            )
            tiles.append(
                lax.dot_general(left, right, contract, preferred_element_type=jnp.float32)
            )
        keep_mask = pair_start + lax.iota(jnp.int32, group_size) < live_count
        return jnp.where(keep_mask[:, None, None], jnp.stack(tiles, axis=0), jnp.float32(0.0))

    grouped = lax.map(one_group, jnp.arange(pair_total // group_size, dtype=jnp.int32))
    terms = grouped.reshape(pair_total, TILE, TILE)
    mine = lax.psum_scatter(terms.astype(jnp.bfloat16), "row", scatter_dimension=0, tiled=True)
    return mine[None]


def chunk_kernel(occ_local, share, own_owner, other_owner, codes, own_rows, other_rows, *refs):
    send_out, keep_out = refs[:2]
    stage, packed_rows, turned, pick, sums, send_ref, arrived, left_off = refs[2:]
    rows_total, domain = own_rows.shape
    groups = rows_total // GROUP
    per_group = GROUP // occ_local
    held = per_group * CAP
    batch = codes[share * ROWS]

    def slab_copy(place):
        slab = own_rows if place < groups else other_rows
        return pltpu.make_async_copy(
            slab.at[pl.ds(place % groups * GROUP, GROUP), :],
            stage.at[pl.ds(place * GROUP, GROUP), :],
            arrived.at[place],
        )

    for place in range(2 * groups):
        slab_copy(place).start()

    lane = lax.broadcasted_iota(jnp.int32, (1, GROUP), 1)
    orbital_of = lane & (occ_local - 1)
    turn_of = lane >> (occ_local.bit_length() - 1)
    slot = lax.broadcasted_iota(jnp.int32, (held, GROUP), 0)
    counts = []
    for source, owner in enumerate((own_owner, other_owner)):
        count = jnp.int32(0)
        rank = jnp.full((1, GROUP), -GROUP * CAP, jnp.int32)
        for orbital in range(occ_local):
            mine = owner[orbital] == batch
            rank = jnp.where(orbital_of == orbital, jnp.where(mine, count, -GROUP * CAP), rank)
            count = count + mine.astype(jnp.int32)
        pick[source] = (slot == turn_of * count + rank).astype(jnp.bfloat16)
        counts.append(count)
    turned[domain:, :] = jnp.zeros((TILE, PART), jnp.bfloat16)

    def pack(place, carry):
        rows = pl.ds(pl.multiple_of(place * GROUP, GROUP), GROUP)
        pltpu.make_async_copy(
            own_rows.at[pl.ds(0, GROUP), :], stage.at[rows, :], arrived.at[place]
        ).wait()
        source = (place >= groups).astype(jnp.int32)
        before = jnp.minimum(place, groups) * counts[0]
        before = before + jnp.maximum(place - groups, 0) * counts[1]
        start = pl.multiple_of(before * per_group, per_group)
        for column in range(0, domain, 2 * TILE):
            columns = slice(column, column + 2 * TILE)
            packed = jnp.dot(
                pick[source], stage[rows, columns], preferred_element_type=jnp.float32
            )
            packed_rows[pl.ds(start, held), columns] = packed.astype(jnp.bfloat16)
        return carry

    lax.fori_loop(0, 2 * groups, pack, 0)
    filled = pl.multiple_of((counts[0] + counts[1]) * groups * per_group, per_group)
    packed_rows[pl.ds(filled, PART), :] = jnp.zeros((PART, domain), jnp.bfloat16)
    parts = jnp.maximum((filled + PART - 1) // PART, 1)

    row_at = lax.axis_index("row")
    send_first = (row_at ^ 2) * share
    keep_first = row_at * share
    width = math.gcd(4, share)

    def out_copies(turn_at):
        sends = pl.ds(turn_at * width, width)
        keeps = pl.ds(share + turn_at * width, width)
        return (
            pltpu.make_async_copy(send_ref.at[sends], send_out.at[sends], left_off.at[0, turn_at]),
            pltpu.make_async_copy(sums.at[keeps], keep_out.at[sends], left_off.at[1, turn_at]),
        )

    def add_part(part, fresh):
        rows = pl.ds(pl.multiple_of(part * PART, PART), PART)
        for column in range(0, domain, TILE):
            columns = slice(column, column + TILE)
            turned[columns, :] = packed_rows[rows, columns].T

        def several(turn_at, carry):
            for offset in range(width):
                at = turn_at * width + offset
                for pair, to in ((send_first + at, at), (keep_first + at, share + at)):
                    code = codes[pair]
                    left = pl.multiple_of(code >> SHIFT, TILE)
                    right = pl.multiple_of(code & ((1 << SHIFT) - 1), TILE)
                    product = jnp.dot(
                        turned[pl.ds(left, TILE), :],
                        packed_rows[rows, pl.ds(right, TILE)],
                        preferred_element_type=jnp.float32,
                    )
                    sums[to] = product if fresh else sums[to] + product

            @pl.when(part == parts - 1)
            def _():
                sends = pl.ds(turn_at * width, width)
                send_ref[sends] = sums[sends].astype(send_ref.dtype)
                for copy in out_copies(turn_at):
                    copy.start()

            return carry

        lax.fori_loop(0, share // width, several, 0)

    add_part(jnp.int32(0), True)

    def more(part, carry):
        add_part(part, False)
        return carry

    lax.fori_loop(1, parts, more, 0)
    for turn_at in range(share // width):
        for copy in out_copies(turn_at):
            copy.wait()


def tile_chunk(owners, codes, own_rows, other_rows, occ_local, share):
    rows_total, domain = own_rows.shape
    groups = rows_total // GROUP
    held = GROUP // occ_local * CAP
    depth = 2 * groups * held
    tiles = (share, TILE, TILE)
    anywhere = pl.BlockSpec(memory_space=pl.ANY)
    in_smem = pl.BlockSpec(memory_space=pltpu.SMEM)
    return pl.pallas_call(
        functools.partial(chunk_kernel, occ_local, share),
        in_specs=[in_smem] * 3 + [anywhere] * 2,
        out_specs=[anywhere, anywhere],
        scratch_shapes=[
            pltpu.VMEM((2 * rows_total, domain), jnp.bfloat16),
            pltpu.VMEM((depth + PART, domain), jnp.bfloat16),
            pltpu.VMEM((domain + TILE, PART), jnp.bfloat16),
            pltpu.VMEM((2, held, GROUP), jnp.bfloat16),
            pltpu.VMEM((2 * share, TILE, TILE), jnp.float32),
            pltpu.VMEM(tiles, jnp.bfloat16),
            pltpu.SemaphoreType.DMA((2 * groups,)),
            pltpu.SemaphoreType.DMA((2, share)),
        ],
        out_shape=[
            jax.ShapeDtypeStruct(tiles, jnp.bfloat16),
            jax.ShapeDtypeStruct(tiles, jnp.float32),
        ],
        compiler_params=pltpu.CompilerParams(vmem_limit_bytes=56 * 1024 * 1024),
        cost_estimate=pl.CostEstimate(
            flops=4 * share * TILE * TILE * depth + 2 * depth * GROUP * domain,
            bytes_accessed=4 * rows_total * domain + 6 * share * TILE * TILE,
            transcendentals=0,
        ),
        name="tile_chunk",
    )(*owners, codes, own_rows, other_rows)


def block_columns(pair_codes, live, blocks):
    left = jnp.zeros_like(pair_codes)
    start = jnp.zeros_like(pair_codes)
    for block in range(1, blocks):
        first = block * blocks - block * (block - 1) // 2
        left = jnp.where(pair_codes >= first, block, left)
        start = jnp.where(pair_codes >= first, first, start)
    right = pair_codes - start + left
    left = jnp.where(lax.iota(jnp.int32, pair_codes.shape[0]) < live, left, blocks)
    return ((left << SHIFT) + right) * TILE


def tile_plan(half_tensor, batch_owner, pair_list, live_pairs):
    rows = lax.axis_size("row")
    aux_local, occ_local, domain = half_tensor.shape
    share = pair_list.shape[1] // rows
    orb_at = lax.axis_index("orb")
    inner = (orb_at == 1) | (orb_at == 2)
    swap = [(i, i ^ 1) for i in range(4)]
    step_a = [(0, 1), (3, 2), (1, 3), (2, 0)]
    step_b = [(0, 2), (3, 1), (1, 0), (2, 3)]

    def exchange(array, bits):
        return lax.ppermute(array, "row", [(i, i ^ bits) for i in range(rows)])

    def after(array, earlier):
        return lax.optimization_barrier((array, earlier))

    def over_x(send, keep):
        return keep + exchange(send, 2).astype(jnp.float32)

    own_rows = half_tensor.reshape(aux_local * occ_local, domain)
    other_rows = exchange(own_rows, 1)
    own_owner = batch_owner[:, 0]
    owners = own_owner, exchange(own_owner, 1)
    columns = block_columns(pair_list[0], live_pairs[0], domain // TILE)
    own_codes = jnp.concatenate([columns, orb_at[None]])
    far_codes = lax.ppermute(own_codes, "orb", [(i, i ^ 3) for i in range(4)])
    a_codes = lax.ppermute(own_codes, "orb", [(to, at) for at, to in step_a])
    b_codes = lax.ppermute(own_codes, "orb", [(to, at) for at, to in step_b])
    far_codes, a_codes, b_codes = lax.optimization_barrier((far_codes, a_codes, b_codes))

    def chunk(codes, other_rows):
        return tile_chunk(owners, codes, own_rows, other_rows, occ_local, share)

    far_send, far_keep = chunk(far_codes, other_rows)
    a_send, a_keep = chunk(a_codes, other_rows)
    far = over_x(far_send, far_keep).astype(jnp.bfloat16)
    other_rows, far = after(other_rows, far)
    far = lax.ppermute(far, "orb", swap).astype(jnp.float32)
    b_send, b_keep = chunk(b_codes, other_rows)
    a_term = over_x(a_send, a_keep) + jnp.where(inner, far, 0.0)
    other_rows, a_term = after(other_rows, a_term.astype(jnp.bfloat16))
    a_term = lax.ppermute(a_term, "orb", step_a)
    own_send, own_keep = chunk(own_codes, other_rows)
    b_keep, own_send = after(b_keep, own_send)
    b_term = over_x(b_send, b_keep) + jnp.where(inner, 0.0, far)
    b_term = lax.ppermute(b_term.astype(jnp.bfloat16), "orb", step_b)
    beside = a_term.astype(jnp.float32) + b_term.astype(jnp.float32)
    beside, own_keep = after(beside, own_keep)
    total = over_x(own_send, own_keep) + beside
    return total.astype(jnp.bfloat16)[None]


def per_device(half_tensor, batch_owner, pair_list, live_pairs):
    batches = lax.axis_size("orb")
    rows = lax.axis_size("row")
    aux_local, occ_local, domain = half_tensor.shape
    pair_total = pair_list.shape[1]
    tile_elements = batches * pair_total * TILE * TILE
    slab_elements = batches * CAP * aux_local * domain
    fits = (
        rows == ROWS
        and batches == 4
        and pair_total % rows == 0
        and occ_local & (occ_local - 1) == 0
        and GROUP % occ_local == 0
        and aux_local * occ_local % GROUP == 0
        and tile_elements <= slab_elements
    )
    plan = tile_plan if fits else slab_plan
    return plan(half_tensor, batch_owner, pair_list, live_pairs)


def solution(mesh):
    return jax.shard_map(
        per_device,
        mesh=mesh,
        in_specs=(
            P(("grp", "orb"), "row", None),
            P(("grp", "row"), None),
            P(("grp", "orb"), None),
            P(("grp", "orb")),
        ),
        out_specs=P(("grp", "orb"), "row", None, None),
        check_vma=False,
    )
```

```python
import functools
import math

import jax
import jax.numpy as jnp
from jax import lax
from jax.experimental import pallas as pl
from jax.experimental.pallas import tpu as pltpu
from jax.sharding import PartitionSpec as P

TILE = 128
CAP = 8
GROUP = 256
PART = 512
ROWS = 4
SHIFT = 16


def block_pairs(pair_codes, blocks):
    row_grid = lax.broadcasted_iota(jnp.int32, (blocks, blocks), 0)
    col_grid = lax.broadcasted_iota(jnp.int32, (blocks, blocks), 1)
    code_grid = row_grid * blocks - row_grid * (row_grid - 1) // 2 + (col_grid - row_grid)
    upper_part = col_grid >= row_grid
    matches = (code_grid[None, :, :] == pair_codes[:, None, None]) & upper_part[None, :, :]
    first_blocks = jnp.sum(jnp.where(matches, row_grid[None], 0), axis=(1, 2))
    second_blocks = jnp.sum(jnp.where(matches, col_grid[None], 0), axis=(1, 2))
    return (first_blocks, second_blocks)


def slot_sources(owner_local, batches, capacity):
    local_count = owner_local.shape[0]
    batch_ids = lax.broadcasted_iota(jnp.int32, (local_count, batches), 1)
    onehot = (owner_local[:, None] == batch_ids).astype(jnp.int32)
    ranking = jnp.cumsum(onehot, axis=0) - 1
    slot_of = jnp.sum(ranking * onehot, axis=1)
    target = owner_local * capacity + slot_of
    slot_ids = lax.broadcasted_iota(jnp.int32, (local_count, batches * capacity), 1)
    orbital_ids = lax.broadcasted_iota(jnp.int32, (local_count, batches * capacity), 0)
    slot_hits = target[:, None] == slot_ids
    source_row = jnp.sum(jnp.where(slot_hits, orbital_ids, 0), axis=0)
    filled = jnp.any(slot_hits, axis=0)
    return jnp.where(filled, source_row, local_count)


def slab_plan(half_tensor, batch_owner, pair_list, live_pairs):
    batches = lax.axis_size("orb")
    aux_local, occ_local, domain = half_tensor.shape
    blocks = domain // TILE
    sources = slot_sources(batch_owner[:, 0], batches, CAP)
    block_major = half_tensor.reshape(aux_local, occ_local, blocks, TILE).transpose(2, 1, 0, 3)
    outgoing = jnp.take(block_major, sources, axis=1, mode="fill", fill_value=0)
    arrived = lax.all_to_all(outgoing, "orb", split_axis=1, concat_axis=2, tiled=True)
    stacked_rows = arrived.reshape(blocks, -1, TILE)
    first_blocks, second_blocks = block_pairs(pair_list[0], blocks)
    live_count = live_pairs[0]
    pair_total = pair_list.shape[1]
    contract = (((0,), (0,)), ((), ()))
    group_size = math.gcd(4, pair_total)

    def one_group(group_index):
        pair_start = group_index * group_size
        tiles = []
        for offset in range(group_size):
            left = lax.dynamic_index_in_dim(
                stacked_rows, first_blocks[pair_start + offset], 0, keepdims=False
            )
            right = lax.dynamic_index_in_dim(
                stacked_rows, second_blocks[pair_start + offset], 0, keepdims=False
            )
            tiles.append(
                lax.dot_general(left, right, contract, preferred_element_type=jnp.float32)
            )
        keep_mask = pair_start + lax.iota(jnp.int32, group_size) < live_count
        return jnp.where(keep_mask[:, None, None], jnp.stack(tiles, axis=0), jnp.float32(0.0))

    grouped = lax.map(one_group, jnp.arange(pair_total // group_size, dtype=jnp.int32))
    terms = grouped.reshape(pair_total, TILE, TILE)
    mine = lax.psum_scatter(terms.astype(jnp.bfloat16), "row", scatter_dimension=0, tiled=True)
    return mine[None]


def sort_kernel(batches, occ_local, first, owner, slab, sorted_out, stage, ordered, pick, arrived, left):
    rows_total, width = sorted_out.shape
    groups = rows_total // GROUP
    per_group = GROUP // occ_local
    piece = 2 * TILE

    def slab_copy(group):
        rows = pl.ds(group * GROUP, GROUP)
        return pltpu.make_async_copy(
            slab.at[rows, pl.ds(first, width)], stage.at[rows, :], arrived.at[group]
        )

    def out_copy(column):
        columns = pl.ds(column * piece, piece)
        return pltpu.make_async_copy(
            ordered.at[:, columns], sorted_out.at[:, columns], left.at[column]
        )

    for group in range(groups):
        slab_copy(group).start()
    owners = [owner[orbital] for orbital in range(occ_local)]
    positions = [jnp.int32(0)] * occ_local
    rank = jnp.int32(0)
    for batch in range(batches):
        for orbital in range(occ_local):
            mine = owners[orbital] == batch
            positions[orbital] = jnp.where(mine, rank, positions[orbital])
            rank = rank + mine.astype(jnp.int32)
    lane = lax.broadcasted_iota(jnp.int32, (1, GROUP), 1)
    orbital_of = lane & (occ_local - 1)
    target = lane >> (occ_local.bit_length() - 1)
    for orbital in range(occ_local):
        target = target + jnp.where(orbital_of == orbital, positions[orbital] * per_group, 0)
    slot = lax.broadcasted_iota(jnp.int32, (GROUP, GROUP), 0)
    pick[...] = (slot == target).astype(jnp.bfloat16)
    for group in range(groups):
        slab_copy(group).wait()

    for column in range(width // piece):
        columns = slice(column * piece, (column + 1) * piece)
        for group in range(groups):
            moved = jnp.dot(
                pick[...], stage[group * GROUP:(group + 1) * GROUP, columns],
                preferred_element_type=jnp.float32,
            ).astype(jnp.bfloat16)
            for unit in range(occ_local):
                to = (unit * groups + group) * per_group
                ordered[to:to + per_group, columns] = (
                    moved[unit * per_group:(unit + 1) * per_group]
                )
        out_copy(column).start()
    for column in range(width // piece):
        out_copy(column).wait()


def sort_rows(owner, slab, first, width, batches):
    occ_local, = owner.shape
    rows_total = slab.shape[0]
    anywhere = pl.BlockSpec(memory_space=pl.ANY)
    return pl.pallas_call(
        functools.partial(sort_kernel, batches, occ_local, first),
        in_specs=[pl.BlockSpec(memory_space=pltpu.SMEM), anywhere],
        out_specs=anywhere,
        scratch_shapes=[
            pltpu.VMEM((rows_total, width), jnp.bfloat16),
            pltpu.VMEM((rows_total, width), jnp.bfloat16),
            pltpu.VMEM((GROUP, GROUP), jnp.bfloat16),
            pltpu.SemaphoreType.DMA((rows_total // GROUP,)),
            pltpu.SemaphoreType.DMA((width // (2 * TILE),)),
        ],
        out_shape=jax.ShapeDtypeStruct((rows_total, width), jnp.bfloat16),
        compiler_params=pltpu.CompilerParams(vmem_limit_bytes=56 * 1024 * 1024),
        cost_estimate=pl.CostEstimate(
            flops=2 * rows_total * GROUP * width,
            bytes_accessed=4 * rows_total * width,
            transcendentals=0,
        ),
        name="sort_rows",
    )(owner, slab)


def chunk_kernel(occ_local, share, own_owner, other_owner, codes, *refs):
    slabs = refs[:2], refs[2:4]
    send_out, keep_out = refs[4:6]
    packed_rows, turned, sums, send_ref, arrived, left_off = refs[6:]
    rows_total, half = refs[0].shape
    domain = 2 * half
    per_orbital = rows_total // occ_local
    batch = codes[share * ROWS]

    filled = jnp.int32(0)
    pieces = []
    for source, owner in enumerate((own_owner, other_owner)):
        owners = [owner[orbital] for orbital in range(occ_local)]
        earlier = sum((each < batch).astype(jnp.int32) for each in owners)
        count = sum((each == batch).astype(jnp.int32) for each in owners)

        def copies(orbital, source=source, earlier=earlier, filled=filled):
            at = pl.multiple_of((earlier + orbital) * per_orbital, per_orbital)
            to = pl.multiple_of((filled + orbital) * per_orbital, per_orbital)
            return [
                pltpu.make_async_copy(
                    slabs[source][side].at[pl.ds(at, per_orbital), :],
                    packed_rows.at[pl.ds(to, per_orbital), pl.ds(side * half, half)],
                    arrived.at[source, side, orbital],
                )
                for side in range(2)
            ]

        def start(orbital, carry, copies=copies):
            for copy in copies(orbital):
                copy.start()
            return carry

        lax.fori_loop(0, count, start, 0)
        pieces.append((copies, count))
        filled = filled + count

    end = pl.multiple_of(filled * per_orbital, per_orbital)
    packed_rows[pl.ds(end, PART), :] = jnp.zeros((PART, domain), jnp.bfloat16)
    turned[domain:, :] = jnp.zeros((TILE, PART), jnp.bfloat16)
    parts = jnp.maximum((end + PART - 1) // PART, 1)
    for copies, count in pieces:
        def wait(orbital, carry, copies=copies):
            for copy in copies(orbital):
                copy.wait()
            return carry

        lax.fori_loop(0, count, wait, 0)

    row_at = lax.axis_index("row")
    send_first = (row_at ^ 2) * share
    keep_first = row_at * share
    width = math.gcd(4, share)

    def out_copies(turn_at):
        sends = pl.ds(turn_at * width, width)
        keeps = pl.ds(share + turn_at * width, width)
        return (
            pltpu.make_async_copy(send_ref.at[sends], send_out.at[sends], left_off.at[0, turn_at]),
            pltpu.make_async_copy(sums.at[keeps], keep_out.at[sends], left_off.at[1, turn_at]),
        )

    def add_part(part, fresh):
        rows = pl.ds(pl.multiple_of(part * PART, PART), PART)
        for column in range(0, domain, TILE):
            columns = slice(column, column + TILE)
            turned[columns, :] = packed_rows[rows, columns].T

        def several(turn_at, carry):
            for offset in range(width):
                at = turn_at * width + offset
                for pair, to in ((send_first + at, at), (keep_first + at, share + at)):
                    code = codes[pair]
                    left = pl.multiple_of(code >> SHIFT, TILE)
                    right = pl.multiple_of(code & ((1 << SHIFT) - 1), TILE)
                    product = jnp.dot(
                        turned[pl.ds(left, TILE), :],
                        packed_rows[rows, pl.ds(right, TILE)],
                        preferred_element_type=jnp.float32,
                    )
                    sums[to] = product if fresh else sums[to] + product

            @pl.when(part == parts - 1)
            def _():
                sends = pl.ds(turn_at * width, width)
                send_ref[sends] = sums[sends].astype(send_ref.dtype)
                for copy in out_copies(turn_at):
                    copy.start()

            return carry

        lax.fori_loop(0, share // width, several, 0)

    add_part(jnp.int32(0), True)

    def more(part, carry):
        add_part(part, False)
        return carry

    lax.fori_loop(1, parts, more, 0)
    for turn_at in range(share // width):
        for copy in out_copies(turn_at):
            copy.wait()


def tile_chunk(owners, codes, slabs, share):
    occ_local, = owners[0].shape
    rows_total, half = slabs[0].shape
    domain = 2 * half
    depth = 2 * CAP * (rows_total // occ_local)
    tiles = (share, TILE, TILE)
    anywhere = pl.BlockSpec(memory_space=pl.ANY)
    in_smem = pl.BlockSpec(memory_space=pltpu.SMEM)
    return pl.pallas_call(
        functools.partial(chunk_kernel, occ_local, share),
        in_specs=[in_smem] * 3 + [anywhere] * 4,
        out_specs=[anywhere, anywhere],
        scratch_shapes=[
            pltpu.VMEM((depth + PART, domain), jnp.bfloat16),
            pltpu.VMEM((domain + TILE, PART), jnp.bfloat16),
            pltpu.VMEM((2 * share, TILE, TILE), jnp.float32),
            pltpu.VMEM(tiles, jnp.bfloat16),
            pltpu.SemaphoreType.DMA((2, 2, CAP)),
            pltpu.SemaphoreType.DMA((2, share)),
        ],
        out_shape=[
            jax.ShapeDtypeStruct(tiles, jnp.bfloat16),
            jax.ShapeDtypeStruct(tiles, jnp.float32),
        ],
        compiler_params=pltpu.CompilerParams(vmem_limit_bytes=56 * 1024 * 1024),
        cost_estimate=pl.CostEstimate(
            flops=4 * share * TILE * TILE * depth,
            bytes_accessed=2 * depth * domain + 6 * share * TILE * TILE,
            transcendentals=0,
        ),
        name="tile_chunk",
    )(*owners, codes, *slabs)


def block_columns(pair_codes, live, blocks):
    left = jnp.zeros_like(pair_codes)
    start = jnp.zeros_like(pair_codes)
    for block in range(1, blocks):
        first = block * blocks - block * (block - 1) // 2
        left = jnp.where(pair_codes >= first, block, left)
        start = jnp.where(pair_codes >= first, first, start)
    right = pair_codes - start + left
    left = jnp.where(lax.iota(jnp.int32, pair_codes.shape[0]) < live, left, blocks)
    return ((left << SHIFT) + right) * TILE


def tile_plan(half_tensor, batch_owner, pair_list, live_pairs):
    rows = lax.axis_size("row")
    aux_local, occ_local, domain = half_tensor.shape
    share = pair_list.shape[1] // rows
    orb_at = lax.axis_index("orb")
    inner = (orb_at == 1) | (orb_at == 2)
    swap = [(i, i ^ 1) for i in range(4)]
    step_a = [(0, 1), (3, 2), (1, 3), (2, 0)]
    step_b = [(0, 2), (3, 1), (1, 0), (2, 3)]

    def exchange(array, bits):
        return lax.ppermute(array, "row", [(i, i ^ bits) for i in range(rows)])

    def after(array, earlier):
        return lax.optimization_barrier((array, earlier))

    def over_x(send, keep):
        return keep + exchange(send, 2).astype(jnp.float32)

    own_rows = half_tensor.reshape(aux_local * occ_local, domain)
    own_owner = batch_owner[:, 0]
    half = domain // 2
    own_halves = [sort_rows(own_owner, own_rows, first, half, 4) for first in (0, half)]
    other_halves = [exchange(each, 1) for each in own_halves]
    other_owner = exchange(own_owner, 1)
    columns = block_columns(pair_list[0], live_pairs[0], domain // TILE)
    own_codes = jnp.concatenate([columns, orb_at[None]])
    own_codes, own_halves[1] = after(own_codes, own_halves[1])
    slabs = (*own_halves, *other_halves)
    far_codes = lax.ppermute(own_codes, "orb", [(i, i ^ 3) for i in range(4)])
    own_codes, other_owner = after(own_codes, other_owner)
    a_codes = lax.ppermute(own_codes, "orb", [(to, at) for at, to in step_a])
    b_codes = lax.ppermute(own_codes, "orb", [(to, at) for at, to in step_b])
    far_codes, a_codes, b_codes = lax.optimization_barrier((far_codes, a_codes, b_codes))
    owners = own_owner, other_owner

    def chunk(codes):
        return tile_chunk(owners, codes, slabs, share)

    far_send, far_keep = chunk(far_codes)
    a_send, a_keep = chunk(a_codes)
    far = over_x(far_send, far_keep).astype(jnp.bfloat16)
    b_codes, far = after(b_codes, far)
    far = lax.ppermute(far, "orb", swap).astype(jnp.float32)
    b_send, b_keep = chunk(b_codes)
    a_term = over_x(a_send, a_keep) + jnp.where(inner, far, 0.0)
    own_codes, a_term = after(own_codes, a_term.astype(jnp.bfloat16))
    a_term = lax.ppermute(a_term, "orb", step_a)
    own_send, own_keep = chunk(own_codes)
    b_keep, own_send = after(b_keep, own_send)
    b_term = over_x(b_send, b_keep) + jnp.where(inner, 0.0, far)
    b_term = lax.ppermute(b_term.astype(jnp.bfloat16), "orb", step_b)
    beside = a_term.astype(jnp.float32) + b_term.astype(jnp.float32)
    beside, own_keep = after(beside, own_keep)
    total = over_x(own_send, own_keep) + beside
    return total.astype(jnp.bfloat16)[None]


def per_device(half_tensor, batch_owner, pair_list, live_pairs):
    batches = lax.axis_size("orb")
    rows = lax.axis_size("row")
    aux_local, occ_local, domain = half_tensor.shape
    pair_total = pair_list.shape[1]
    tile_elements = batches * pair_total * TILE * TILE
    slab_elements = batches * CAP * aux_local * domain
    fits = (
        rows == ROWS
        and batches == 4
        and pair_total % rows == 0
        and occ_local & (occ_local - 1) == 0
        and GROUP % occ_local == 0
        and domain % (4 * TILE) == 0
        and aux_local * occ_local % GROUP == 0
        and tile_elements <= slab_elements
    )
    plan = tile_plan if fits else slab_plan
    return plan(half_tensor, batch_owner, pair_list, live_pairs)


def solution(mesh):
    return jax.shard_map(
        per_device,
        mesh=mesh,
        in_specs=(
            P(("grp", "orb"), "row", None),
            P(("grp", "row"), None),
            P(("grp", "orb"), None),
            P(("grp", "orb")),
        ),
        out_specs=P(("grp", "orb"), "row", None, None),
        check_vma=False,
    )
```

```python
import functools
import math

import jax
import jax.numpy as jnp
from jax import lax
from jax.experimental import pallas as pl
from jax.experimental.pallas import tpu as pltpu
from jax.sharding import PartitionSpec as P

TILE = 128
CAP = 8
GROUP = 256
PART = 512
ROWS = 4
SHIFT = 16


def block_pairs(pair_codes, blocks):
    row_grid = lax.broadcasted_iota(jnp.int32, (blocks, blocks), 0)
    col_grid = lax.broadcasted_iota(jnp.int32, (blocks, blocks), 1)
    code_grid = row_grid * blocks - row_grid * (row_grid - 1) // 2 + (col_grid - row_grid)
    upper_part = col_grid >= row_grid
    matches = (code_grid[None, :, :] == pair_codes[:, None, None]) & upper_part[None, :, :]
    first_blocks = jnp.sum(jnp.where(matches, row_grid[None], 0), axis=(1, 2))
    second_blocks = jnp.sum(jnp.where(matches, col_grid[None], 0), axis=(1, 2))
    return (first_blocks, second_blocks)


def slot_sources(owner_local, batches, capacity):
    local_count = owner_local.shape[0]
    batch_ids = lax.broadcasted_iota(jnp.int32, (local_count, batches), 1)
    onehot = (owner_local[:, None] == batch_ids).astype(jnp.int32)
    ranking = jnp.cumsum(onehot, axis=0) - 1
    slot_of = jnp.sum(ranking * onehot, axis=1)
    target = owner_local * capacity + slot_of
    slot_ids = lax.broadcasted_iota(jnp.int32, (local_count, batches * capacity), 1)
    orbital_ids = lax.broadcasted_iota(jnp.int32, (local_count, batches * capacity), 0)
    slot_hits = target[:, None] == slot_ids
    source_row = jnp.sum(jnp.where(slot_hits, orbital_ids, 0), axis=0)
    filled = jnp.any(slot_hits, axis=0)
    return jnp.where(filled, source_row, local_count)


def slab_plan(half_tensor, batch_owner, pair_list, live_pairs):
    batches = lax.axis_size("orb")
    aux_local, occ_local, domain = half_tensor.shape
    blocks = domain // TILE
    sources = slot_sources(batch_owner[:, 0], batches, CAP)
    block_major = half_tensor.reshape(aux_local, occ_local, blocks, TILE).transpose(2, 1, 0, 3)
    outgoing = jnp.take(block_major, sources, axis=1, mode="fill", fill_value=0)
    arrived = lax.all_to_all(outgoing, "orb", split_axis=1, concat_axis=2, tiled=True)
    stacked_rows = arrived.reshape(blocks, -1, TILE)
    first_blocks, second_blocks = block_pairs(pair_list[0], blocks)
    live_count = live_pairs[0]
    pair_total = pair_list.shape[1]
    contract = (((0,), (0,)), ((), ()))
    group_size = math.gcd(4, pair_total)

    def one_group(group_index):
        pair_start = group_index * group_size
        tiles = []
        for offset in range(group_size):
            left = lax.dynamic_index_in_dim(
                stacked_rows, first_blocks[pair_start + offset], 0, keepdims=False
            )
            right = lax.dynamic_index_in_dim(
                stacked_rows, second_blocks[pair_start + offset], 0, keepdims=False
            )
            tiles.append(
                lax.dot_general(left, right, contract, preferred_element_type=jnp.float32)
            )
        keep_mask = pair_start + lax.iota(jnp.int32, group_size) < live_count
        return jnp.where(keep_mask[:, None, None], jnp.stack(tiles, axis=0), jnp.float32(0.0))

    grouped = lax.map(one_group, jnp.arange(pair_total // group_size, dtype=jnp.int32))
    terms = grouped.reshape(pair_total, TILE, TILE)
    mine = lax.psum_scatter(terms.astype(jnp.bfloat16), "row", scatter_dimension=0, tiled=True)
    return mine[None]


def chunk_kernel(occ_local, share, own_owner, other_owner, codes, own_rows, other_rows, *refs):
    send_out, keep_out = refs[:2]
    stage, packed_rows, turned, pick, sums, send_ref, arrived, left_off = refs[2:]
    rows_total, domain = own_rows.shape
    groups = rows_total // GROUP
    per_group = GROUP // occ_local
    held = per_group * CAP
    batch = codes[share * ROWS]

    def slab_copy(place):
        slab = own_rows if place < groups else other_rows
        return pltpu.make_async_copy(
            slab.at[pl.ds(place % groups * GROUP, GROUP), :],
            stage.at[pl.ds(place * GROUP, GROUP), :],
            arrived.at[place],
        )

    for place in range(2 * groups):
        slab_copy(place).start()

    lane = lax.broadcasted_iota(jnp.int32, (1, GROUP), 1)
    orbital_of = lane & (occ_local - 1)
    turn_of = lane >> (occ_local.bit_length() - 1)
    slot = lax.broadcasted_iota(jnp.int32, (held, GROUP), 0)
    counts = []
    for source, owner in enumerate((own_owner, other_owner)):
        count = jnp.int32(0)
        rank = jnp.full((1, GROUP), -GROUP * CAP, jnp.int32)
        for orbital in range(occ_local):
            mine = owner[orbital] == batch
            rank = jnp.where(orbital_of == orbital, jnp.where(mine, count, -GROUP * CAP), rank)
            count = count + mine.astype(jnp.int32)
        pick[source] = (slot == turn_of * count + rank).astype(jnp.bfloat16)
        counts.append(count)
    turned[domain:, :] = jnp.zeros((TILE, PART), jnp.bfloat16)

    def pack(place, carry):
        rows = pl.ds(pl.multiple_of(place * GROUP, GROUP), GROUP)
        pltpu.make_async_copy(
            own_rows.at[pl.ds(0, GROUP), :], stage.at[rows, :], arrived.at[place]
        ).wait()
        source = (place >= groups).astype(jnp.int32)
        before = jnp.minimum(place, groups) * counts[0]
        before = before + jnp.maximum(place - groups, 0) * counts[1]
        start = pl.multiple_of(before * per_group, per_group)
        for column in range(0, domain, 2 * TILE):
            columns = slice(column, column + 2 * TILE)
            packed = jnp.dot(
                pick[source], stage[rows, columns], preferred_element_type=jnp.float32
            )
            packed_rows[pl.ds(start, held), columns] = packed.astype(jnp.bfloat16)
        return carry

    lax.fori_loop(0, 2 * groups, pack, 0)
    filled = pl.multiple_of((counts[0] + counts[1]) * groups * per_group, per_group)
    packed_rows[pl.ds(filled, PART), :] = jnp.zeros((PART, domain), jnp.bfloat16)
    parts = jnp.maximum((filled + PART - 1) // PART, 1)

    row_at = lax.axis_index("row")
    send_first = (row_at ^ 2) * share
    keep_first = row_at * share
    width = math.gcd(4, share)
    blocks_at_once = math.gcd(4, domain // TILE)

    def out_copies(turn_at):
        sends = pl.ds(turn_at * width, width)
        keeps = pl.ds(share + turn_at * width, width)
        return (
            pltpu.make_async_copy(send_ref.at[sends], send_out.at[sends], left_off.at[0, turn_at]),
            pltpu.make_async_copy(sums.at[keeps], keep_out.at[sends], left_off.at[1, turn_at]),
        )

    def add_part(part, fresh):
        rows = pl.ds(pl.multiple_of(part * PART, PART), PART)

        def turn(group, carry):
            for block in range(blocks_at_once):
                column = pl.multiple_of((group * blocks_at_once + block) * TILE, TILE)
                columns = pl.ds(column, TILE)
                turned[columns, :] = packed_rows[rows, columns].T
            return carry

        lax.fori_loop(0, domain // TILE // blocks_at_once, turn, 0)

        def several(turn_at, carry):
            for offset in range(width):
                at = turn_at * width + offset
                for pair, to in ((send_first + at, at), (keep_first + at, share + at)):
                    code = codes[pair]
                    left = pl.multiple_of(code >> SHIFT, TILE)
                    right = pl.multiple_of(code & ((1 << SHIFT) - 1), TILE)
                    product = jnp.dot(
                        turned[pl.ds(left, TILE), :],
                        packed_rows[rows, pl.ds(right, TILE)],
                        preferred_element_type=jnp.float32,
                    )
                    sums[to] = product if fresh else sums[to] + product

            @pl.when(part == parts - 1)
            def _():
                sends = pl.ds(turn_at * width, width)
                send_ref[sends] = sums[sends].astype(send_ref.dtype)
                for copy in out_copies(turn_at):
                    copy.start()

            return carry

        lax.fori_loop(0, share // width, several, 0)

    add_part(jnp.int32(0), True)

    def more(part, carry):
        add_part(part, False)
        return carry

    lax.fori_loop(1, parts, more, 0)
    for turn_at in range(share // width):
        for copy in out_copies(turn_at):
            copy.wait()


def tile_chunk(owners, codes, own_rows, other_rows, occ_local, share):
    rows_total, domain = own_rows.shape
    groups = rows_total // GROUP
    held = GROUP // occ_local * CAP
    depth = 2 * groups * held
    tiles = (share, TILE, TILE)
    anywhere = pl.BlockSpec(memory_space=pl.ANY)
    in_smem = pl.BlockSpec(memory_space=pltpu.SMEM)
    return pl.pallas_call(
        functools.partial(chunk_kernel, occ_local, share),
        in_specs=[in_smem] * 3 + [anywhere] * 2,
        out_specs=[anywhere, anywhere],
        scratch_shapes=[
            pltpu.VMEM((2 * rows_total, domain), jnp.bfloat16),
            pltpu.VMEM((depth + PART, domain), jnp.bfloat16),
            pltpu.VMEM((domain + TILE, PART), jnp.bfloat16),
            pltpu.VMEM((2, held, GROUP), jnp.bfloat16),
            pltpu.VMEM((2 * share, TILE, TILE), jnp.float32),
            pltpu.VMEM(tiles, jnp.bfloat16),
            pltpu.SemaphoreType.DMA((2 * groups,)),
            pltpu.SemaphoreType.DMA((2, share)),
        ],
        out_shape=[
            jax.ShapeDtypeStruct(tiles, jnp.bfloat16),
            jax.ShapeDtypeStruct(tiles, jnp.float32),
        ],
        compiler_params=pltpu.CompilerParams(vmem_limit_bytes=56 * 1024 * 1024),
        cost_estimate=pl.CostEstimate(
            flops=4 * share * TILE * TILE * depth + 2 * depth * GROUP * domain,
            bytes_accessed=4 * rows_total * domain + 6 * share * TILE * TILE,
            transcendentals=0,
        ),
        name="tile_chunk",
    )(*owners, codes, own_rows, other_rows)


def block_columns(pair_codes, live, blocks):
    left = jnp.zeros_like(pair_codes)
    start = jnp.zeros_like(pair_codes)
    for block in range(1, blocks):
        first = block * blocks - block * (block - 1) // 2
        left = jnp.where(pair_codes >= first, block, left)
        start = jnp.where(pair_codes >= first, first, start)
    right = pair_codes - start + left
    left = jnp.where(lax.iota(jnp.int32, pair_codes.shape[0]) < live, left, blocks)
    return ((left << SHIFT) + right) * TILE


def tile_plan(half_tensor, batch_owner, pair_list, live_pairs):
    rows = lax.axis_size("row")
    aux_local, occ_local, domain = half_tensor.shape
    share = pair_list.shape[1] // rows
    orb_at = lax.axis_index("orb")
    inner = (orb_at == 1) | (orb_at == 2)
    swap = [(i, i ^ 1) for i in range(4)]
    step_a = [(0, 1), (3, 2), (1, 3), (2, 0)]
    step_b = [(0, 2), (3, 1), (1, 0), (2, 3)]

    def exchange(array, bits):
        return lax.ppermute(array, "row", [(i, i ^ bits) for i in range(rows)])

    def after(array, earlier):
        return lax.optimization_barrier((array, earlier))

    def over_x(send, keep):
        return keep + exchange(send, 2).astype(jnp.float32)

    own_rows = half_tensor.reshape(aux_local * occ_local, domain)
    other_rows = exchange(own_rows, 1)
    own_owner = batch_owner[:, 0]
    other_owner = exchange(own_owner, 1)
    columns = block_columns(pair_list[0], live_pairs[0], domain // TILE)
    own_codes = jnp.concatenate([columns, orb_at[None]])
    far_codes = lax.ppermute(own_codes, "orb", [(i, i ^ 3) for i in range(4)])
    own_codes, other_owner = after(own_codes, other_owner)
    a_codes = lax.ppermute(own_codes, "orb", [(to, at) for at, to in step_a])
    b_codes = lax.ppermute(own_codes, "orb", [(to, at) for at, to in step_b])
    far_codes, a_codes, b_codes = lax.optimization_barrier((far_codes, a_codes, b_codes))
    owners = own_owner, other_owner

    def chunk(codes, other_rows):
        return tile_chunk(owners, codes, own_rows, other_rows, occ_local, share)

    far_send, far_keep = chunk(far_codes, other_rows)
    a_send, a_keep = chunk(a_codes, other_rows)
    far = over_x(far_send, far_keep).astype(jnp.bfloat16)
    other_rows, far = after(other_rows, far)
    far = lax.ppermute(far, "orb", swap).astype(jnp.float32)
    b_send, b_keep = chunk(b_codes, other_rows)
    a_term = over_x(a_send, a_keep) + jnp.where(inner, far, 0.0)
    other_rows, a_term = after(other_rows, a_term.astype(jnp.bfloat16))
    a_term = lax.ppermute(a_term, "orb", step_a)
    own_send, own_keep = chunk(own_codes, other_rows)
    b_keep, own_send = after(b_keep, own_send)
    b_term = over_x(b_send, b_keep) + jnp.where(inner, 0.0, far)
    b_term = lax.ppermute(b_term.astype(jnp.bfloat16), "orb", step_b)
    beside = over_x(own_send, own_keep) + a_term.astype(jnp.float32)
    beside, b_term = after(beside, b_term)
    total = beside + b_term.astype(jnp.float32)
    return total.astype(jnp.bfloat16)[None]


def per_device(half_tensor, batch_owner, pair_list, live_pairs):
    batches = lax.axis_size("orb")
    rows = lax.axis_size("row")
    aux_local, occ_local, domain = half_tensor.shape
    pair_total = pair_list.shape[1]
    tile_elements = batches * pair_total * TILE * TILE
    slab_elements = batches * CAP * aux_local * domain
    fits = (
        rows == ROWS
        and batches == 4
        and pair_total % rows == 0
        and occ_local & (occ_local - 1) == 0
        and GROUP % occ_local == 0
        and aux_local * occ_local % GROUP == 0
        and tile_elements <= slab_elements
    )
    plan = tile_plan if fits else slab_plan
    return plan(half_tensor, batch_owner, pair_list, live_pairs)


def solution(mesh):
    return jax.shard_map(
        per_device,
        mesh=mesh,
        in_specs=(
            P(("grp", "orb"), "row", None),
            P(("grp", "row"), None),
            P(("grp", "orb"), None),
            P(("grp", "orb")),
        ),
        out_specs=P(("grp", "orb"), "row", None, None),
        check_vma=False,
    )
```

```python
import functools
import math

import jax
import jax.numpy as jnp
from jax import lax
from jax.experimental import pallas as pl
from jax.experimental.pallas import tpu as pltpu
from jax.sharding import PartitionSpec as P

TILE = 128
CAP = 8
GROUP = 256
PART = 512
ROWS = 4
SHIFT = 16


def block_pairs(pair_codes, blocks):
    row_grid = lax.broadcasted_iota(jnp.int32, (blocks, blocks), 0)
    col_grid = lax.broadcasted_iota(jnp.int32, (blocks, blocks), 1)
    code_grid = row_grid * blocks - row_grid * (row_grid - 1) // 2 + (col_grid - row_grid)
    upper_part = col_grid >= row_grid
    matches = (code_grid[None, :, :] == pair_codes[:, None, None]) & upper_part[None, :, :]
    first_blocks = jnp.sum(jnp.where(matches, row_grid[None], 0), axis=(1, 2))
    second_blocks = jnp.sum(jnp.where(matches, col_grid[None], 0), axis=(1, 2))
    return (first_blocks, second_blocks)


def slot_sources(owner_local, batches, capacity):
    local_count = owner_local.shape[0]
    batch_ids = lax.broadcasted_iota(jnp.int32, (local_count, batches), 1)
    onehot = (owner_local[:, None] == batch_ids).astype(jnp.int32)
    ranking = jnp.cumsum(onehot, axis=0) - 1
    slot_of = jnp.sum(ranking * onehot, axis=1)
    target = owner_local * capacity + slot_of
    slot_ids = lax.broadcasted_iota(jnp.int32, (local_count, batches * capacity), 1)
    orbital_ids = lax.broadcasted_iota(jnp.int32, (local_count, batches * capacity), 0)
    slot_hits = target[:, None] == slot_ids
    source_row = jnp.sum(jnp.where(slot_hits, orbital_ids, 0), axis=0)
    filled = jnp.any(slot_hits, axis=0)
    return jnp.where(filled, source_row, local_count)


def slab_plan(half_tensor, batch_owner, pair_list, live_pairs):
    batches = lax.axis_size("orb")
    aux_local, occ_local, domain = half_tensor.shape
    blocks = domain // TILE
    sources = slot_sources(batch_owner[:, 0], batches, CAP)
    block_major = half_tensor.reshape(aux_local, occ_local, blocks, TILE).transpose(2, 1, 0, 3)
    outgoing = jnp.take(block_major, sources, axis=1, mode="fill", fill_value=0)
    arrived = lax.all_to_all(outgoing, "orb", split_axis=1, concat_axis=2, tiled=True)
    stacked_rows = arrived.reshape(blocks, -1, TILE)
    first_blocks, second_blocks = block_pairs(pair_list[0], blocks)
    live_count = live_pairs[0]
    pair_total = pair_list.shape[1]
    contract = (((0,), (0,)), ((), ()))
    group_size = math.gcd(4, pair_total)

    def one_group(group_index):
        pair_start = group_index * group_size
        tiles = []
        for offset in range(group_size):
            left = lax.dynamic_index_in_dim(
                stacked_rows, first_blocks[pair_start + offset], 0, keepdims=False
            )
            right = lax.dynamic_index_in_dim(
                stacked_rows, second_blocks[pair_start + offset], 0, keepdims=False
            )
            tiles.append(
                lax.dot_general(left, right, contract, preferred_element_type=jnp.float32)
            )
        keep_mask = pair_start + lax.iota(jnp.int32, group_size) < live_count
        return jnp.where(keep_mask[:, None, None], jnp.stack(tiles, axis=0), jnp.float32(0.0))

    grouped = lax.map(one_group, jnp.arange(pair_total // group_size, dtype=jnp.int32))
    terms = grouped.reshape(pair_total, TILE, TILE)
    mine = lax.psum_scatter(terms.astype(jnp.bfloat16), "row", scatter_dimension=0, tiled=True)
    return mine[None]


def chunk_kernel(occ_local, share, own_owner, other_owner, codes, own_rows, other_rows, *refs):
    send_out, keep_out = refs[:2]
    stage, packed_rows, turned, pick, sums, send_ref, arrived, left_off = refs[2:]
    rows_total, domain = own_rows.shape
    groups = rows_total // GROUP
    per_group = GROUP // occ_local
    held = per_group * CAP
    batch = codes[share * ROWS]

    def slab_copy(place):
        slab = own_rows if place < groups else other_rows
        return pltpu.make_async_copy(
            slab.at[pl.ds(place % groups * GROUP, GROUP), :],
            stage.at[pl.ds(place * GROUP, GROUP), :],
            arrived.at[place],
        )

    for place in range(2 * groups):
        slab_copy(place).start()

    lane = lax.broadcasted_iota(jnp.int32, (1, GROUP), 1)
    orbital_of = lane & (occ_local - 1)
    turn_of = lane >> (occ_local.bit_length() - 1)
    slot = lax.broadcasted_iota(jnp.int32, (held, GROUP), 0)
    counts = []
    for source, owner in enumerate((own_owner, other_owner)):
        count = jnp.int32(0)
        rank = jnp.full((1, GROUP), -GROUP * CAP, jnp.int32)
        for orbital in range(occ_local):
            mine = owner[orbital] == batch
            rank = jnp.where(orbital_of == orbital, jnp.where(mine, count, -GROUP * CAP), rank)
            count = count + mine.astype(jnp.int32)
        pick[source] = (slot == turn_of * count + rank).astype(jnp.bfloat16)
        counts.append(count)
    turned[domain:, :] = jnp.zeros((TILE, PART), jnp.bfloat16)

    def pack(place, carry):
        rows = pl.ds(pl.multiple_of(place * GROUP, GROUP), GROUP)
        pltpu.make_async_copy(
            own_rows.at[pl.ds(0, GROUP), :], stage.at[rows, :], arrived.at[place]
        ).wait()
        source = (place >= groups).astype(jnp.int32)
        before = jnp.minimum(place, groups) * counts[0]
        before = before + jnp.maximum(place - groups, 0) * counts[1]
        start = pl.multiple_of(before * per_group, per_group)
        for column in range(0, domain, 2 * TILE):
            columns = slice(column, column + 2 * TILE)
            packed = jnp.dot(
                pick[source], stage[rows, columns], preferred_element_type=jnp.float32
            )
            packed_rows[pl.ds(start, held), columns] = packed.astype(jnp.bfloat16)
        return carry

    lax.fori_loop(0, 2 * groups, pack, 0)
    filled = pl.multiple_of((counts[0] + counts[1]) * groups * per_group, per_group)
    packed_rows[pl.ds(filled, PART), :] = jnp.zeros((PART, domain), jnp.bfloat16)
    parts = jnp.maximum((filled + PART - 1) // PART, 1)

    row_at = lax.axis_index("row")
    send_first = (row_at ^ 2) * share
    keep_first = row_at * share
    width = math.gcd(4, share)

    def out_copies(turn_at):
        sends = pl.ds(turn_at * width, width)
        keeps = pl.ds(share + turn_at * width, width)
        return (
            pltpu.make_async_copy(send_ref.at[sends], send_out.at[sends], left_off.at[0, turn_at]),
            pltpu.make_async_copy(sums.at[keeps], keep_out.at[sends], left_off.at[1, turn_at]),
        )

    def add_part(part, fresh):
        rows = pl.ds(pl.multiple_of(part * PART, PART), PART)
        for column in range(0, domain, TILE):
            columns = slice(column, column + TILE)
            turned[columns, :] = packed_rows[rows, columns].T

        def several(turn_at, carry):
            for offset in range(width):
                at = turn_at * width + offset
                for pair, to in ((send_first + at, at), (keep_first + at, share + at)):
                    code = codes[pair]
                    left = pl.multiple_of(code >> SHIFT, TILE)
                    right = pl.multiple_of(code & ((1 << SHIFT) - 1), TILE)
                    product = jnp.dot(
                        turned[pl.ds(left, TILE), :],
                        packed_rows[rows, pl.ds(right, TILE)],
                        preferred_element_type=jnp.float32,
                    )
                    sums[to] = product if fresh else sums[to] + product

            @pl.when(part == parts - 1)
            def _():
                sends = pl.ds(turn_at * width, width)
                send_ref[sends] = sums[sends].astype(send_ref.dtype)
                for copy in out_copies(turn_at):
                    copy.start()

            return carry

        lax.fori_loop(0, share // width, several, 0)

    add_part(jnp.int32(0), True)

    def more(part, carry):
        add_part(part, False)
        return carry

    lax.fori_loop(1, parts, more, 0)
    for turn_at in range(share // width):
        for copy in out_copies(turn_at):
            copy.wait()


def tile_chunk(owners, codes, own_rows, other_rows, occ_local, share):
    rows_total, domain = own_rows.shape
    groups = rows_total // GROUP
    held = GROUP // occ_local * CAP
    depth = 2 * groups * held
    tiles = (share, TILE, TILE)
    anywhere = pl.BlockSpec(memory_space=pl.ANY)
    in_smem = pl.BlockSpec(memory_space=pltpu.SMEM)
    return pl.pallas_call(
        functools.partial(chunk_kernel, occ_local, share),
        in_specs=[in_smem] * 3 + [anywhere] * 2,
        out_specs=[anywhere, anywhere],
        scratch_shapes=[
            pltpu.VMEM((2 * rows_total, domain), jnp.bfloat16),
            pltpu.VMEM((depth + PART, domain), jnp.bfloat16),
            pltpu.VMEM((domain + TILE, PART), jnp.bfloat16),
            pltpu.VMEM((2, held, GROUP), jnp.bfloat16),
            pltpu.VMEM((2 * share, TILE, TILE), jnp.float32),
            pltpu.VMEM(tiles, jnp.bfloat16),
            pltpu.SemaphoreType.DMA((2 * groups,)),
            pltpu.SemaphoreType.DMA((2, share)),
        ],
        out_shape=[
            jax.ShapeDtypeStruct(tiles, jnp.bfloat16),
            jax.ShapeDtypeStruct(tiles, jnp.float32),
        ],
        compiler_params=pltpu.CompilerParams(vmem_limit_bytes=56 * 1024 * 1024),
        cost_estimate=pl.CostEstimate(
            flops=4 * share * TILE * TILE * depth + 2 * depth * GROUP * domain,
            bytes_accessed=4 * rows_total * domain + 6 * share * TILE * TILE,
            transcendentals=0,
        ),
        name="tile_chunk",
    )(*owners, codes, own_rows, other_rows)


def block_columns(pair_codes, live, blocks):
    left = jnp.zeros_like(pair_codes)
    start = jnp.zeros_like(pair_codes)
    for block in range(1, blocks):
        first = block * blocks - block * (block - 1) // 2
        left = jnp.where(pair_codes >= first, block, left)
        start = jnp.where(pair_codes >= first, first, start)
    right = pair_codes - start + left
    left = jnp.where(lax.iota(jnp.int32, pair_codes.shape[0]) < live, left, blocks)
    return ((left << SHIFT) + right) * TILE


def tile_plan(half_tensor, batch_owner, pair_list, live_pairs):
    rows = lax.axis_size("row")
    aux_local, occ_local, domain = half_tensor.shape
    share = pair_list.shape[1] // rows
    orb_at = lax.axis_index("orb")
    inner = (orb_at == 1) | (orb_at == 2)
    swap = [(i, i ^ 1) for i in range(4)]
    step_a = [(0, 1), (3, 2), (1, 3), (2, 0)]
    step_b = [(0, 2), (3, 1), (1, 0), (2, 3)]

    def exchange(array, bits):
        return lax.ppermute(array, "row", [(i, i ^ bits) for i in range(rows)])

    def after(array, earlier):
        return lax.optimization_barrier((array, earlier))

    def over_x(send, keep):
        return keep + exchange(send, 2).astype(jnp.float32)

    own_rows = half_tensor.reshape(aux_local * occ_local, domain)
    other_rows = exchange(own_rows, 1)
    own_owner = batch_owner[:, 0]
    owners = own_owner, exchange(own_owner, 1)
    columns = block_columns(pair_list[0], live_pairs[0], domain // TILE)
    own_codes = jnp.concatenate([columns, orb_at[None]])
    far_codes = lax.ppermute(own_codes, "orb", [(i, i ^ 3) for i in range(4)])
    a_codes = lax.ppermute(own_codes, "orb", [(to, at) for at, to in step_a])
    b_codes = lax.ppermute(own_codes, "orb", [(to, at) for at, to in step_b])
    b_codes, a_codes, far_codes = lax.optimization_barrier((b_codes, a_codes, far_codes))

    def chunk(codes, other_rows):
        return tile_chunk(owners, codes, own_rows, other_rows, occ_local, share)

    far_send, far_keep = chunk(far_codes, other_rows)
    a_send, a_keep = chunk(a_codes, other_rows)
    far = over_x(far_send, far_keep).astype(jnp.bfloat16)
    other_rows, far = after(other_rows, far)
    far = lax.ppermute(far, "orb", swap).astype(jnp.float32)
    b_send, b_keep = chunk(b_codes, other_rows)
    a_term = over_x(a_send, a_keep) + jnp.where(inner, far, 0.0)
    other_rows, a_term = after(other_rows, a_term.astype(jnp.bfloat16))
    a_term = lax.ppermute(a_term, "orb", step_a)
    own_send, own_keep = chunk(own_codes, other_rows)
    b_keep, own_send = after(b_keep, own_send)
    b_term = over_x(b_send, b_keep) + jnp.where(inner, 0.0, far)
    b_term = lax.ppermute(b_term.astype(jnp.bfloat16), "orb", step_b)
    own_other = exchange(own_send, 2)
    part = own_keep + a_term.astype(jnp.float32)
    b_term, own_other, part = lax.optimization_barrier((b_term, own_other, part))
    total = part + own_other.astype(jnp.float32) + b_term.astype(jnp.float32)
    return total.astype(jnp.bfloat16)[None]


def per_device(half_tensor, batch_owner, pair_list, live_pairs):
    batches = lax.axis_size("orb")
    rows = lax.axis_size("row")
    aux_local, occ_local, domain = half_tensor.shape
    pair_total = pair_list.shape[1]
    tile_elements = batches * pair_total * TILE * TILE
    slab_elements = batches * CAP * aux_local * domain
    fits = (
        rows == ROWS
        and batches == 4
        and pair_total % rows == 0
        and occ_local & (occ_local - 1) == 0
        and GROUP % occ_local == 0
        and aux_local * occ_local % GROUP == 0
        and tile_elements <= slab_elements
    )
    plan = tile_plan if fits else slab_plan
    return plan(half_tensor, batch_owner, pair_list, live_pairs)


def solution(mesh):
    return jax.shard_map(
        per_device,
        mesh=mesh,
        in_specs=(
            P(("grp", "orb"), "row", None),
            P(("grp", "row"), None),
            P(("grp", "orb"), None),
            P(("grp", "orb")),
        ),
        out_specs=P(("grp", "orb"), "row", None, None),
        check_vma=False,
    )
```

```python
import functools
import math

import jax
import jax.numpy as jnp
from jax import lax
from jax.experimental import pallas as pl
from jax.experimental.pallas import tpu as pltpu
from jax.sharding import PartitionSpec as P

TILE = 128
CAP = 8
GROUP = 256
PART = 512
ROWS = 4
SHIFT = 16


def block_pairs(pair_codes, blocks):
    row_grid = lax.broadcasted_iota(jnp.int32, (blocks, blocks), 0)
    col_grid = lax.broadcasted_iota(jnp.int32, (blocks, blocks), 1)
    code_grid = row_grid * blocks - row_grid * (row_grid - 1) // 2 + (col_grid - row_grid)
    upper_part = col_grid >= row_grid
    matches = (code_grid[None, :, :] == pair_codes[:, None, None]) & upper_part[None, :, :]
    first_blocks = jnp.sum(jnp.where(matches, row_grid[None], 0), axis=(1, 2))
    second_blocks = jnp.sum(jnp.where(matches, col_grid[None], 0), axis=(1, 2))
    return (first_blocks, second_blocks)


def slot_sources(owner_local, batches, capacity):
    local_count = owner_local.shape[0]
    batch_ids = lax.broadcasted_iota(jnp.int32, (local_count, batches), 1)
    onehot = (owner_local[:, None] == batch_ids).astype(jnp.int32)
    ranking = jnp.cumsum(onehot, axis=0) - 1
    slot_of = jnp.sum(ranking * onehot, axis=1)
    target = owner_local * capacity + slot_of
    slot_ids = lax.broadcasted_iota(jnp.int32, (local_count, batches * capacity), 1)
    orbital_ids = lax.broadcasted_iota(jnp.int32, (local_count, batches * capacity), 0)
    slot_hits = target[:, None] == slot_ids
    source_row = jnp.sum(jnp.where(slot_hits, orbital_ids, 0), axis=0)
    filled = jnp.any(slot_hits, axis=0)
    return jnp.where(filled, source_row, local_count)


def slab_plan(half_tensor, batch_owner, pair_list, live_pairs):
    batches = lax.axis_size("orb")
    aux_local, occ_local, domain = half_tensor.shape
    blocks = domain // TILE
    sources = slot_sources(batch_owner[:, 0], batches, CAP)
    block_major = half_tensor.reshape(aux_local, occ_local, blocks, TILE).transpose(2, 1, 0, 3)
    outgoing = jnp.take(block_major, sources, axis=1, mode="fill", fill_value=0)
    arrived = lax.all_to_all(outgoing, "orb", split_axis=1, concat_axis=2, tiled=True)
    stacked_rows = arrived.reshape(blocks, -1, TILE)
    first_blocks, second_blocks = block_pairs(pair_list[0], blocks)
    live_count = live_pairs[0]
    pair_total = pair_list.shape[1]
    contract = (((0,), (0,)), ((), ()))
    group_size = math.gcd(4, pair_total)

    def one_group(group_index):
        pair_start = group_index * group_size
        tiles = []
        for offset in range(group_size):
            left = lax.dynamic_index_in_dim(
                stacked_rows, first_blocks[pair_start + offset], 0, keepdims=False
            )
            right = lax.dynamic_index_in_dim(
                stacked_rows, second_blocks[pair_start + offset], 0, keepdims=False
            )
            tiles.append(
                lax.dot_general(left, right, contract, preferred_element_type=jnp.float32)
            )
        keep_mask = pair_start + lax.iota(jnp.int32, group_size) < live_count
        return jnp.where(keep_mask[:, None, None], jnp.stack(tiles, axis=0), jnp.float32(0.0))

    grouped = lax.map(one_group, jnp.arange(pair_total // group_size, dtype=jnp.int32))
    terms = grouped.reshape(pair_total, TILE, TILE)
    mine = lax.psum_scatter(terms.astype(jnp.bfloat16), "row", scatter_dimension=0, tiled=True)
    return mine[None]


def chunk_kernel(occ_local, share, own_owner, other_owner, codes, own_rows, other_rows, *refs):
    send_out, keep_out = refs[:2]
    stage, packed_rows, turned, pick, sums, send_ref, arrived, left_off = refs[2:]
    rows_total, domain = own_rows.shape
    groups = rows_total // GROUP
    per_group = GROUP // occ_local
    held = per_group * CAP
    batch = codes[share * ROWS]

    def slab_copy(place):
        slab = own_rows if place < groups else other_rows
        return pltpu.make_async_copy(
            slab.at[pl.ds(place % groups * GROUP, GROUP), :],
            stage.at[pl.ds(place * GROUP, GROUP), :],
            arrived.at[place],
        )

    for place in range(2 * groups):
        slab_copy(place).start()

    lane = lax.broadcasted_iota(jnp.int32, (1, GROUP), 1)
    orbital_of = lane & (occ_local - 1)
    turn_of = lane >> (occ_local.bit_length() - 1)
    slot = lax.broadcasted_iota(jnp.int32, (held, GROUP), 0)
    counts = []
    for source, owner in enumerate((own_owner, other_owner)):
        count = jnp.int32(0)
        rank = jnp.full((1, GROUP), -GROUP * CAP, jnp.int32)
        for orbital in range(occ_local):
            mine = owner[orbital] == batch
            rank = jnp.where(orbital_of == orbital, jnp.where(mine, count, -GROUP * CAP), rank)
            count = count + mine.astype(jnp.int32)
        pick[source] = (slot == turn_of * count + rank).astype(jnp.bfloat16)
        counts.append(count)
    turned[domain:, :] = jnp.zeros((TILE, PART), jnp.bfloat16)

    def pack(place, carry):
        rows = pl.ds(pl.multiple_of(place * GROUP, GROUP), GROUP)
        pltpu.make_async_copy(
            own_rows.at[pl.ds(0, GROUP), :], stage.at[rows, :], arrived.at[place]
        ).wait()
        source = (place >= groups).astype(jnp.int32)
        before = jnp.minimum(place, groups) * counts[0]
        before = before + jnp.maximum(place - groups, 0) * counts[1]
        start = pl.multiple_of(before * per_group, per_group)
        for column in range(0, domain, 2 * TILE):
            columns = slice(column, column + 2 * TILE)
            packed = jnp.dot(
                pick[source], stage[rows, columns], preferred_element_type=jnp.float32
            )
            packed_rows[pl.ds(start, held), columns] = packed.astype(jnp.bfloat16)
        return carry

    lax.fori_loop(0, 2 * groups, pack, 0)
    filled = pl.multiple_of((counts[0] + counts[1]) * groups * per_group, per_group)
    packed_rows[pl.ds(filled, PART), :] = jnp.zeros((PART, domain), jnp.bfloat16)
    parts = jnp.maximum((filled + PART - 1) // PART, 1)

    row_at = lax.axis_index("row")
    send_first = (row_at ^ 2) * share
    keep_first = row_at * share
    width = math.gcd(4, share)

    def out_copies(turn_at):
        sends = pl.ds(turn_at * width, width)
        keeps = pl.ds(share + turn_at * width, width)
        return (
            pltpu.make_async_copy(send_ref.at[sends], send_out.at[sends], left_off.at[0, turn_at]),
            pltpu.make_async_copy(sums.at[keeps], keep_out.at[sends], left_off.at[1, turn_at]),
        )

    def add_part(part, fresh):
        rows = pl.ds(pl.multiple_of(part * PART, PART), PART)
        for column in range(0, domain, TILE):
            columns = slice(column, column + TILE)
            turned[columns, :] = packed_rows[rows, columns].T

        def several(turn_at, carry):
            for offset in range(width):
                at = turn_at * width + offset
                for pair, to in ((send_first + at, at), (keep_first + at, share + at)):
                    code = codes[pair]
                    left = pl.multiple_of(code >> SHIFT, TILE)
                    right = pl.multiple_of(code & ((1 << SHIFT) - 1), TILE)
                    product = jnp.dot(
                        turned[pl.ds(left, TILE), :],
                        packed_rows[rows, pl.ds(right, TILE)],
                        preferred_element_type=jnp.float32,
                    )
                    sums[to] = product if fresh else sums[to] + product

            @pl.when(part == parts - 1)
            def _():
                sends = pl.ds(turn_at * width, width)
                send_ref[sends] = sums[sends].astype(send_ref.dtype)
                for copy in out_copies(turn_at):
                    copy.start()

            return carry

        lax.fori_loop(0, share // width, several, 0)

    add_part(jnp.int32(0), True)

    def more(part, carry):
        add_part(part, False)
        return carry

    lax.fori_loop(1, parts, more, 0)
    for turn_at in range(share // width):
        for copy in out_copies(turn_at):
            copy.wait()


def tile_chunk(owners, codes, own_rows, other_rows, occ_local, share):
    rows_total, domain = own_rows.shape
    groups = rows_total // GROUP
    held = GROUP // occ_local * CAP
    depth = 2 * groups * held
    tiles = (share, TILE, TILE)
    anywhere = pl.BlockSpec(memory_space=pl.ANY)
    in_smem = pl.BlockSpec(memory_space=pltpu.SMEM)
    return pl.pallas_call(
        functools.partial(chunk_kernel, occ_local, share),
        in_specs=[in_smem] * 3 + [anywhere] * 2,
        out_specs=[anywhere, anywhere],
        scratch_shapes=[
            pltpu.VMEM((2 * rows_total, domain), jnp.bfloat16),
            pltpu.VMEM((depth + PART, domain), jnp.bfloat16),
            pltpu.VMEM((domain + TILE, PART), jnp.bfloat16),
            pltpu.VMEM((2, held, GROUP), jnp.bfloat16),
            pltpu.VMEM((2 * share, TILE, TILE), jnp.float32),
            pltpu.VMEM(tiles, jnp.bfloat16),
            pltpu.SemaphoreType.DMA((2 * groups,)),
            pltpu.SemaphoreType.DMA((2, share)),
        ],
        out_shape=[
            jax.ShapeDtypeStruct(tiles, jnp.bfloat16),
            jax.ShapeDtypeStruct(tiles, jnp.float32),
        ],
        compiler_params=pltpu.CompilerParams(vmem_limit_bytes=56 * 1024 * 1024),
        cost_estimate=pl.CostEstimate(
            flops=4 * share * TILE * TILE * depth + 2 * depth * GROUP * domain,
            bytes_accessed=4 * rows_total * domain + 6 * share * TILE * TILE,
            transcendentals=0,
        ),
        name="tile_chunk",
    )(*owners, codes, own_rows, other_rows)


def block_columns(pair_codes, live, blocks):
    left = jnp.zeros_like(pair_codes)
    start = jnp.zeros_like(pair_codes)
    for block in range(1, blocks):
        first = block * blocks - block * (block - 1) // 2
        left = jnp.where(pair_codes >= first, block, left)
        start = jnp.where(pair_codes >= first, first, start)
    right = pair_codes - start + left
    left = jnp.where(lax.iota(jnp.int32, pair_codes.shape[0]) < live, left, blocks)
    return ((left << SHIFT) + right) * TILE


def tile_plan(half_tensor, batch_owner, pair_list, live_pairs):
    rows = lax.axis_size("row")
    aux_local, occ_local, domain = half_tensor.shape
    share = pair_list.shape[1] // rows
    orb_at = lax.axis_index("orb")
    inner = (orb_at == 1) | (orb_at == 2)
    swap = [(i, i ^ 1) for i in range(4)]
    step_a = [(0, 1), (3, 2), (1, 3), (2, 0)]
    step_b = [(0, 2), (3, 1), (1, 0), (2, 3)]

    def exchange(array, bits):
        return lax.ppermute(array, "row", [(i, i ^ bits) for i in range(rows)])

    def after(array, earlier):
        return lax.optimization_barrier((array, earlier))

    def over_x(send, keep):
        return keep + exchange(send, 2).astype(jnp.float32)

    own_rows = half_tensor.reshape(aux_local * occ_local, domain)
    other_rows = exchange(own_rows, 1)
    own_owner = batch_owner[:, 0]
    owners = own_owner, exchange(own_owner, 1)
    columns = block_columns(pair_list[0], live_pairs[0], domain // TILE)
    own_codes = jnp.concatenate([columns, orb_at[None]])
    far_codes = lax.ppermute(own_codes, "orb", [(i, i ^ 3) for i in range(4)])
    a_codes = lax.ppermute(own_codes, "orb", [(to, at) for at, to in step_a])
    b_codes = lax.ppermute(own_codes, "orb", [(to, at) for at, to in step_b])
    far_codes, a_codes, b_codes = lax.optimization_barrier((far_codes, a_codes, b_codes))

    def chunk(codes, other_rows):
        return tile_chunk(owners, codes, own_rows, other_rows, occ_local, share)

    far_send, far_keep = chunk(far_codes, other_rows)
    a_send, a_keep = chunk(a_codes, other_rows)
    far = over_x(far_send, far_keep).astype(jnp.bfloat16)
    other_rows, far = after(other_rows, far)
    far = lax.ppermute(far, "orb", swap).astype(jnp.float32)
    b_send, b_keep = chunk(b_codes, other_rows)
    a_term = over_x(a_send, a_keep) + jnp.where(inner, far, 0.0)
    other_rows, a_term = after(other_rows, a_term.astype(jnp.bfloat16))
    a_term = lax.ppermute(a_term, "orb", step_a)
    own_send, own_keep = chunk(own_codes, other_rows)
    b_keep, own_send = after(b_keep, own_send)
    b_term = over_x(b_send, b_keep) + jnp.where(inner, 0.0, far)
    b_term = lax.ppermute(b_term.astype(jnp.bfloat16), "orb", step_b)
    own_other = exchange(own_send, 2)
    part = own_keep + a_term.astype(jnp.float32)
    part, own_other, b_term = lax.optimization_barrier((part, own_other, b_term))
    total = part + own_other.astype(jnp.float32) + b_term.astype(jnp.float32)
    return total.astype(jnp.bfloat16)[None]


def per_device(half_tensor, batch_owner, pair_list, live_pairs):
    batches = lax.axis_size("orb")
    rows = lax.axis_size("row")
    aux_local, occ_local, domain = half_tensor.shape
    pair_total = pair_list.shape[1]
    tile_elements = batches * pair_total * TILE * TILE
    slab_elements = batches * CAP * aux_local * domain
    fits = (
        rows == ROWS
        and batches == 4
        and pair_total % rows == 0
        and occ_local & (occ_local - 1) == 0
        and GROUP % occ_local == 0
        and aux_local * occ_local % GROUP == 0
        and tile_elements <= slab_elements
    )
    plan = tile_plan if fits else slab_plan
    return plan(half_tensor, batch_owner, pair_list, live_pairs)


def solution(mesh):
    return jax.shard_map(
        per_device,
        mesh=mesh,
        in_specs=(
            P(("grp", "orb"), "row", None),
            P(("grp", "row"), None),
            P(("grp", "orb"), None),
            P(("grp", "orb")),
        ),
        out_specs=P(("grp", "orb"), "row", None, None),
        check_vma=False,
    )
```

```python
import functools
import math

import jax
import jax.numpy as jnp
from jax import lax
from jax.experimental import pallas as pl
from jax.experimental.pallas import tpu as pltpu
from jax.sharding import PartitionSpec as P

TILE = 128
CAP = 8
GROUP = 256
PART = 512
ROWS = 4
SHIFT = 16


def block_pairs(pair_codes, blocks):
    row_grid = lax.broadcasted_iota(jnp.int32, (blocks, blocks), 0)
    col_grid = lax.broadcasted_iota(jnp.int32, (blocks, blocks), 1)
    code_grid = row_grid * blocks - row_grid * (row_grid - 1) // 2 + (col_grid - row_grid)
    upper_part = col_grid >= row_grid
    matches = (code_grid[None, :, :] == pair_codes[:, None, None]) & upper_part[None, :, :]
    first_blocks = jnp.sum(jnp.where(matches, row_grid[None], 0), axis=(1, 2))
    second_blocks = jnp.sum(jnp.where(matches, col_grid[None], 0), axis=(1, 2))
    return (first_blocks, second_blocks)


def slot_sources(owner_local, batches, capacity):
    local_count = owner_local.shape[0]
    batch_ids = lax.broadcasted_iota(jnp.int32, (local_count, batches), 1)
    onehot = (owner_local[:, None] == batch_ids).astype(jnp.int32)
    ranking = jnp.cumsum(onehot, axis=0) - 1
    slot_of = jnp.sum(ranking * onehot, axis=1)
    target = owner_local * capacity + slot_of
    slot_ids = lax.broadcasted_iota(jnp.int32, (local_count, batches * capacity), 1)
    orbital_ids = lax.broadcasted_iota(jnp.int32, (local_count, batches * capacity), 0)
    slot_hits = target[:, None] == slot_ids
    source_row = jnp.sum(jnp.where(slot_hits, orbital_ids, 0), axis=0)
    filled = jnp.any(slot_hits, axis=0)
    return jnp.where(filled, source_row, local_count)


def slab_plan(half_tensor, batch_owner, pair_list, live_pairs):
    batches = lax.axis_size("orb")
    aux_local, occ_local, domain = half_tensor.shape
    blocks = domain // TILE
    sources = slot_sources(batch_owner[:, 0], batches, CAP)
    block_major = half_tensor.reshape(aux_local, occ_local, blocks, TILE).transpose(2, 1, 0, 3)
    outgoing = jnp.take(block_major, sources, axis=1, mode="fill", fill_value=0)
    arrived = lax.all_to_all(outgoing, "orb", split_axis=1, concat_axis=2, tiled=True)
    stacked_rows = arrived.reshape(blocks, -1, TILE)
    first_blocks, second_blocks = block_pairs(pair_list[0], blocks)
    live_count = live_pairs[0]
    pair_total = pair_list.shape[1]
    contract = (((0,), (0,)), ((), ()))
    group_size = math.gcd(4, pair_total)

    def one_group(group_index):
        pair_start = group_index * group_size
        tiles = []
        for offset in range(group_size):
            left = lax.dynamic_index_in_dim(
                stacked_rows, first_blocks[pair_start + offset], 0, keepdims=False
            )
            right = lax.dynamic_index_in_dim(
                stacked_rows, second_blocks[pair_start + offset], 0, keepdims=False
            )
            tiles.append(
                lax.dot_general(left, right, contract, preferred_element_type=jnp.float32)
            )
        keep_mask = pair_start + lax.iota(jnp.int32, group_size) < live_count
        return jnp.where(keep_mask[:, None, None], jnp.stack(tiles, axis=0), jnp.float32(0.0))

    grouped = lax.map(one_group, jnp.arange(pair_total // group_size, dtype=jnp.int32))
    terms = grouped.reshape(pair_total, TILE, TILE)
    mine = lax.psum_scatter(terms.astype(jnp.bfloat16), "row", scatter_dimension=0, tiled=True)
    return mine[None]


def chunk_kernel(occ_local, share, own_owner, other_owner, codes, own_rows, other_rows, *refs):
    send_out, keep_out = refs[:2]
    stage, packed_rows, turned, pick, unit, sums, send_ref, arrived, left_off = refs[2:]
    rows_total, domain = own_rows.shape
    groups = rows_total // GROUP
    per_group = GROUP // occ_local
    held = per_group * CAP
    batch = codes[share * ROWS]

    def slab_copy(place):
        slab = own_rows if place < groups else other_rows
        return pltpu.make_async_copy(
            slab.at[pl.ds(place % groups * GROUP, GROUP), :],
            stage.at[pl.ds(place * GROUP, GROUP), :],
            arrived.at[place],
        )

    for place in range(2 * groups):
        slab_copy(place).start()

    lane = lax.broadcasted_iota(jnp.int32, (1, GROUP), 1)
    orbital_of = lane & (occ_local - 1)
    turn_of = lane >> (occ_local.bit_length() - 1)
    slot = lax.broadcasted_iota(jnp.int32, (held, GROUP), 0)
    counts = []
    for source, owner in enumerate((own_owner, other_owner)):
        count = jnp.int32(0)
        rank = jnp.full((1, GROUP), -GROUP * CAP, jnp.int32)
        for orbital in range(occ_local):
            mine = owner[orbital] == batch
            rank = jnp.where(orbital_of == orbital, jnp.where(mine, count, -GROUP * CAP), rank)
            count = count + mine.astype(jnp.int32)
        pick[source] = (slot == turn_of * count + rank).astype(jnp.bfloat16)
        counts.append(count)
    turned[domain:, :] = jnp.zeros((TILE, PART), jnp.bfloat16)
    across = lax.broadcasted_iota(jnp.int32, (TILE, TILE), 1)
    down = lax.broadcasted_iota(jnp.int32, (TILE, TILE), 0)
    unit[...] = (across == down).astype(jnp.bfloat16)

    def pack(place, carry):
        rows = pl.ds(pl.multiple_of(place * GROUP, GROUP), GROUP)
        pltpu.make_async_copy(
            own_rows.at[pl.ds(0, GROUP), :], stage.at[rows, :], arrived.at[place]
        ).wait()
        source = (place >= groups).astype(jnp.int32)
        before = jnp.minimum(place, groups) * counts[0]
        before = before + jnp.maximum(place - groups, 0) * counts[1]
        start = pl.multiple_of(before * per_group, per_group)
        for column in range(0, domain, 2 * TILE):
            columns = slice(column, column + 2 * TILE)
            packed = jnp.dot(
                pick[source], stage[rows, columns], preferred_element_type=jnp.float32
            )
            packed_rows[pl.ds(start, held), columns] = packed.astype(jnp.bfloat16)
        return carry

    lax.fori_loop(0, 2 * groups, pack, 0)
    filled = pl.multiple_of((counts[0] + counts[1]) * groups * per_group, per_group)
    packed_rows[pl.ds(filled, PART), :] = jnp.zeros((PART, domain), jnp.bfloat16)
    parts = jnp.maximum((filled + PART - 1) // PART, 1)

    row_at = lax.axis_index("row")
    send_first = (row_at ^ 2) * share
    keep_first = row_at * share
    width = math.gcd(4, share)

    def out_copies(turn_at):
        sends = pl.ds(turn_at * width, width)
        keeps = pl.ds(share + turn_at * width, width)
        return (
            pltpu.make_async_copy(send_ref.at[sends], send_out.at[sends], left_off.at[0, turn_at]),
            pltpu.make_async_copy(sums.at[keeps], keep_out.at[sends], left_off.at[1, turn_at]),
        )

    def add_part(part, fresh):
        rows = pl.ds(pl.multiple_of(part * PART, PART), PART)
        for column in range(0, domain, TILE):
            columns = slice(column, column + TILE)
            block = lax.dot_general(
                unit[...], packed_rows[rows, columns], (((1,), (1,)), ((), ())),
                preferred_element_type=jnp.float32,
            )
            turned[columns, :] = block.astype(jnp.bfloat16)

        def several(turn_at, carry):
            for offset in range(width):
                at = turn_at * width + offset
                for pair, to in ((send_first + at, at), (keep_first + at, share + at)):
                    code = codes[pair]
                    left = pl.multiple_of(code >> SHIFT, TILE)
                    right = pl.multiple_of(code & ((1 << SHIFT) - 1), TILE)
                    product = jnp.dot(
                        turned[pl.ds(left, TILE), :],
                        packed_rows[rows, pl.ds(right, TILE)],
                        preferred_element_type=jnp.float32,
                    )
                    sums[to] = product if fresh else sums[to] + product

            @pl.when(part == parts - 1)
            def _():
                sends = pl.ds(turn_at * width, width)
                send_ref[sends] = sums[sends].astype(send_ref.dtype)
                for copy in out_copies(turn_at):
                    copy.start()

            return carry

        lax.fori_loop(0, share // width, several, 0)

    add_part(jnp.int32(0), True)

    def more(part, carry):
        add_part(part, False)
        return carry

    lax.fori_loop(1, parts, more, 0)
    for turn_at in range(share // width):
        for copy in out_copies(turn_at):
            copy.wait()


def tile_chunk(owners, codes, own_rows, other_rows, occ_local, share):
    rows_total, domain = own_rows.shape
    groups = rows_total // GROUP
    held = GROUP // occ_local * CAP
    depth = 2 * groups * held
    tiles = (share, TILE, TILE)
    anywhere = pl.BlockSpec(memory_space=pl.ANY)
    in_smem = pl.BlockSpec(memory_space=pltpu.SMEM)
    return pl.pallas_call(
        functools.partial(chunk_kernel, occ_local, share),
        in_specs=[in_smem] * 3 + [anywhere] * 2,
        out_specs=[anywhere, anywhere],
        scratch_shapes=[
            pltpu.VMEM((2 * rows_total, domain), jnp.bfloat16),
            pltpu.VMEM((depth + PART, domain), jnp.bfloat16),
            pltpu.VMEM((domain + TILE, PART), jnp.bfloat16),
            pltpu.VMEM((2, held, GROUP), jnp.bfloat16),
            pltpu.VMEM((TILE, TILE), jnp.bfloat16),
            pltpu.VMEM((2 * share, TILE, TILE), jnp.float32),
            pltpu.VMEM(tiles, jnp.bfloat16),
            pltpu.SemaphoreType.DMA((2 * groups,)),
            pltpu.SemaphoreType.DMA((2, share)),
        ],
        out_shape=[
            jax.ShapeDtypeStruct(tiles, jnp.bfloat16),
            jax.ShapeDtypeStruct(tiles, jnp.float32),
        ],
        compiler_params=pltpu.CompilerParams(vmem_limit_bytes=56 * 1024 * 1024),
        cost_estimate=pl.CostEstimate(
            flops=4 * share * TILE * TILE * depth + 2 * depth * GROUP * domain,
            bytes_accessed=4 * rows_total * domain + 6 * share * TILE * TILE,
            transcendentals=0,
        ),
        name="tile_chunk",
    )(*owners, codes, own_rows, other_rows)


def block_columns(pair_codes, live, blocks):
    left = jnp.zeros_like(pair_codes)
    start = jnp.zeros_like(pair_codes)
    for block in range(1, blocks):
        first = block * blocks - block * (block - 1) // 2
        left = jnp.where(pair_codes >= first, block, left)
        start = jnp.where(pair_codes >= first, first, start)
    right = pair_codes - start + left
    left = jnp.where(lax.iota(jnp.int32, pair_codes.shape[0]) < live, left, blocks)
    return ((left << SHIFT) + right) * TILE


def tile_plan(half_tensor, batch_owner, pair_list, live_pairs):
    rows = lax.axis_size("row")
    aux_local, occ_local, domain = half_tensor.shape
    share = pair_list.shape[1] // rows
    orb_at = lax.axis_index("orb")
    inner = (orb_at == 1) | (orb_at == 2)
    swap = [(i, i ^ 1) for i in range(4)]
    step_a = [(0, 1), (3, 2), (1, 3), (2, 0)]
    step_b = [(0, 2), (3, 1), (1, 0), (2, 3)]

    def exchange(array, bits):
        return lax.ppermute(array, "row", [(i, i ^ bits) for i in range(rows)])

    def after(array, earlier):
        return lax.optimization_barrier((array, earlier))

    def over_x(send, keep):
        return keep + exchange(send, 2).astype(jnp.float32)

    own_rows = half_tensor.reshape(aux_local * occ_local, domain)
    other_rows = exchange(own_rows, 1)
    own_owner = batch_owner[:, 0]
    owners = own_owner, exchange(own_owner, 1)
    columns = block_columns(pair_list[0], live_pairs[0], domain // TILE)
    own_codes = jnp.concatenate([columns, orb_at[None]])
    far_codes = lax.ppermute(own_codes, "orb", [(i, i ^ 3) for i in range(4)])
    a_codes = lax.ppermute(own_codes, "orb", [(to, at) for at, to in step_a])
    b_codes = lax.ppermute(own_codes, "orb", [(to, at) for at, to in step_b])
    far_codes, a_codes, b_codes = lax.optimization_barrier((far_codes, a_codes, b_codes))

    def chunk(codes, other_rows):
        return tile_chunk(owners, codes, own_rows, other_rows, occ_local, share)

    far_send, far_keep = chunk(far_codes, other_rows)
    a_send, a_keep = chunk(a_codes, other_rows)
    far = over_x(far_send, far_keep).astype(jnp.bfloat16)
    other_rows, far = after(other_rows, far)
    far = lax.ppermute(far, "orb", swap).astype(jnp.float32)
    b_send, b_keep = chunk(b_codes, other_rows)
    a_term = over_x(a_send, a_keep) + jnp.where(inner, far, 0.0)
    other_rows, a_term = after(other_rows, a_term.astype(jnp.bfloat16))
    a_term = lax.ppermute(a_term, "orb", step_a)
    own_send, own_keep = chunk(own_codes, other_rows)
    b_keep, own_send = after(b_keep, own_send)
    b_term = over_x(b_send, b_keep) + jnp.where(inner, 0.0, far)
    b_term = lax.ppermute(b_term.astype(jnp.bfloat16), "orb", step_b)
    own_other = exchange(own_send, 2)
    part = own_keep + a_term.astype(jnp.float32)
    part, own_other, b_term = lax.optimization_barrier((part, own_other, b_term))
    total = part + own_other.astype(jnp.float32) + b_term.astype(jnp.float32)
    return total.astype(jnp.bfloat16)[None]


def per_device(half_tensor, batch_owner, pair_list, live_pairs):
    batches = lax.axis_size("orb")
    rows = lax.axis_size("row")
    aux_local, occ_local, domain = half_tensor.shape
    pair_total = pair_list.shape[1]
    tile_elements = batches * pair_total * TILE * TILE
    slab_elements = batches * CAP * aux_local * domain
    fits = (
        rows == ROWS
        and batches == 4
        and pair_total % rows == 0
        and occ_local & (occ_local - 1) == 0
        and GROUP % occ_local == 0
        and aux_local * occ_local % GROUP == 0
        and tile_elements <= slab_elements
    )
    plan = tile_plan if fits else slab_plan
    return plan(half_tensor, batch_owner, pair_list, live_pairs)


def solution(mesh):
    return jax.shard_map(
        per_device,
        mesh=mesh,
        in_specs=(
            P(("grp", "orb"), "row", None),
            P(("grp", "row"), None),
            P(("grp", "orb"), None),
            P(("grp", "orb")),
        ),
        out_specs=P(("grp", "orb"), "row", None, None),
        check_vma=False,
    )
```

```python
import functools
import math

import jax
import jax.numpy as jnp
from jax import lax
from jax.experimental import pallas as pl
from jax.experimental.pallas import tpu as pltpu
from jax.sharding import PartitionSpec as P

TILE = 128
CAP = 8
GROUP = 256
PART = 512
ROWS = 4
SHIFT = 16


def block_pairs(pair_codes, blocks):
    row_grid = lax.broadcasted_iota(jnp.int32, (blocks, blocks), 0)
    col_grid = lax.broadcasted_iota(jnp.int32, (blocks, blocks), 1)
    code_grid = row_grid * blocks - row_grid * (row_grid - 1) // 2 + (col_grid - row_grid)
    upper_part = col_grid >= row_grid
    matches = (code_grid[None, :, :] == pair_codes[:, None, None]) & upper_part[None, :, :]
    first_blocks = jnp.sum(jnp.where(matches, row_grid[None], 0), axis=(1, 2))
    second_blocks = jnp.sum(jnp.where(matches, col_grid[None], 0), axis=(1, 2))
    return (first_blocks, second_blocks)


def slot_sources(owner_local, batches, capacity):
    local_count = owner_local.shape[0]
    batch_ids = lax.broadcasted_iota(jnp.int32, (local_count, batches), 1)
    onehot = (owner_local[:, None] == batch_ids).astype(jnp.int32)
    ranking = jnp.cumsum(onehot, axis=0) - 1
    slot_of = jnp.sum(ranking * onehot, axis=1)
    target = owner_local * capacity + slot_of
    slot_ids = lax.broadcasted_iota(jnp.int32, (local_count, batches * capacity), 1)
    orbital_ids = lax.broadcasted_iota(jnp.int32, (local_count, batches * capacity), 0)
    slot_hits = target[:, None] == slot_ids
    source_row = jnp.sum(jnp.where(slot_hits, orbital_ids, 0), axis=0)
    filled = jnp.any(slot_hits, axis=0)
    return jnp.where(filled, source_row, local_count)


def slab_plan(half_tensor, batch_owner, pair_list, live_pairs):
    batches = lax.axis_size("orb")
    aux_local, occ_local, domain = half_tensor.shape
    blocks = domain // TILE
    sources = slot_sources(batch_owner[:, 0], batches, CAP)
    block_major = half_tensor.reshape(aux_local, occ_local, blocks, TILE).transpose(2, 1, 0, 3)
    outgoing = jnp.take(block_major, sources, axis=1, mode="fill", fill_value=0)
    arrived = lax.all_to_all(outgoing, "orb", split_axis=1, concat_axis=2, tiled=True)
    stacked_rows = arrived.reshape(blocks, -1, TILE)
    first_blocks, second_blocks = block_pairs(pair_list[0], blocks)
    live_count = live_pairs[0]
    pair_total = pair_list.shape[1]
    contract = (((0,), (0,)), ((), ()))
    group_size = math.gcd(4, pair_total)

    def one_group(group_index):
        pair_start = group_index * group_size
        tiles = []
        for offset in range(group_size):
            left = lax.dynamic_index_in_dim(
                stacked_rows, first_blocks[pair_start + offset], 0, keepdims=False
            )
            right = lax.dynamic_index_in_dim(
                stacked_rows, second_blocks[pair_start + offset], 0, keepdims=False
            )
            tiles.append(
                lax.dot_general(left, right, contract, preferred_element_type=jnp.float32)
            )
        keep_mask = pair_start + lax.iota(jnp.int32, group_size) < live_count
        return jnp.where(keep_mask[:, None, None], jnp.stack(tiles, axis=0), jnp.float32(0.0))

    grouped = lax.map(one_group, jnp.arange(pair_total // group_size, dtype=jnp.int32))
    terms = grouped.reshape(pair_total, TILE, TILE)
    mine = lax.psum_scatter(terms.astype(jnp.bfloat16), "row", scatter_dimension=0, tiled=True)
    return mine[None]


def chunk_kernel(occ_local, share, own_owner, other_owner, codes, own_rows, other_rows, *refs):
    send_out, keep_out = refs[:2]
    stage, packed_rows, turned, pick, unit, sums, send_ref, arrived, left_off = refs[2:]
    rows_total, domain = own_rows.shape
    groups = rows_total // GROUP
    per_group = GROUP // occ_local
    held = per_group * CAP
    batch = codes[share * ROWS]

    def slab_copy(place):
        slab = own_rows if place < groups else other_rows
        return pltpu.make_async_copy(
            slab.at[pl.ds(place % groups * GROUP, GROUP), :],
            stage.at[pl.ds(place * GROUP, GROUP), :],
            arrived.at[place],
        )

    for place in range(2 * groups):
        slab_copy(place).start()

    lane = lax.broadcasted_iota(jnp.int32, (1, GROUP), 1)
    orbital_of = lane & (occ_local - 1)
    turn_of = lane >> (occ_local.bit_length() - 1)
    slot = lax.broadcasted_iota(jnp.int32, (held, GROUP), 0)
    counts = []
    for source, owner in enumerate((own_owner, other_owner)):
        count = jnp.int32(0)
        rank = jnp.full((1, GROUP), -GROUP * CAP, jnp.int32)
        for orbital in range(occ_local):
            mine = owner[orbital] == batch
            rank = jnp.where(orbital_of == orbital, jnp.where(mine, count, -GROUP * CAP), rank)
            count = count + mine.astype(jnp.int32)
        pick[source] = (slot == turn_of * count + rank).astype(jnp.bfloat16)
        counts.append(count)
    turned[domain:, :] = jnp.zeros((TILE, PART), jnp.bfloat16)
    across = lax.broadcasted_iota(jnp.int32, (GROUP, GROUP), 1)
    down = lax.broadcasted_iota(jnp.int32, (GROUP, GROUP), 0)
    unit[...] = (across == down).astype(jnp.bfloat16)

    def pack(place, carry):
        rows = pl.ds(pl.multiple_of(place * GROUP, GROUP), GROUP)
        pltpu.make_async_copy(
            own_rows.at[pl.ds(0, GROUP), :], stage.at[rows, :], arrived.at[place]
        ).wait()
        source = (place >= groups).astype(jnp.int32)
        before = jnp.minimum(place, groups) * counts[0]
        before = before + jnp.maximum(place - groups, 0) * counts[1]
        start = pl.multiple_of(before * per_group, per_group)
        for column in range(0, domain, 2 * TILE):
            columns = slice(column, column + 2 * TILE)
            packed = jnp.dot(
                pick[source], stage[rows, columns], preferred_element_type=jnp.float32
            )
            packed_rows[pl.ds(start, held), columns] = packed.astype(jnp.bfloat16)
        return carry

    lax.fori_loop(0, 2 * groups, pack, 0)
    filled = pl.multiple_of((counts[0] + counts[1]) * groups * per_group, per_group)
    packed_rows[pl.ds(filled, PART), :] = jnp.zeros((PART, domain), jnp.bfloat16)
    parts = jnp.maximum((filled + PART - 1) // PART, 1)

    row_at = lax.axis_index("row")
    send_first = (row_at ^ 2) * share
    keep_first = row_at * share
    width = math.gcd(4, share)

    def out_copies(turn_at):
        sends = pl.ds(turn_at * width, width)
        keeps = pl.ds(share + turn_at * width, width)
        return (
            pltpu.make_async_copy(send_ref.at[sends], send_out.at[sends], left_off.at[0, turn_at]),
            pltpu.make_async_copy(sums.at[keeps], keep_out.at[sends], left_off.at[1, turn_at]),
        )

    def add_part(part, fresh):
        first_row = pl.multiple_of(part * PART, PART)
        rows = pl.ds(first_row, PART)
        for column in range(0, domain, GROUP):
            columns = slice(column, column + GROUP)
            for row in range(0, PART, GROUP):
                block = lax.dot_general(
                    unit[...], packed_rows[pl.ds(first_row + row, GROUP), columns],
                    (((1,), (1,)), ((), ())), preferred_element_type=jnp.float32,
                )
                turned[columns, row:row + GROUP] = block.astype(jnp.bfloat16)

        def several(turn_at, carry):
            for offset in range(width):
                at = turn_at * width + offset
                lefts, rights = [], []
                for pair in (send_first + at, keep_first + at):
                    code = codes[pair]
                    left = pl.multiple_of(code >> SHIFT, TILE)
                    right = pl.multiple_of(code & ((1 << SHIFT) - 1), TILE)
                    lefts.append(turned[pl.ds(left, TILE), :])
                    rights.append(packed_rows[rows, pl.ds(right, TILE)])
                both = jnp.dot(
                    jnp.concatenate(lefts, axis=0), jnp.concatenate(rights, axis=1),
                    preferred_element_type=jnp.float32,
                )
                for side in range(2):
                    quarter = slice(side * TILE, (side + 1) * TILE)
                    to = side * share + at
                    product = both[quarter, quarter]
                    sums[to] = product if fresh else sums[to] + product

            @pl.when(part == parts - 1)
            def _():
                sends = pl.ds(turn_at * width, width)
                send_ref[sends] = sums[sends].astype(send_ref.dtype)
                for copy in out_copies(turn_at):
                    copy.start()

            return carry

        lax.fori_loop(0, share // width, several, 0)

    add_part(jnp.int32(0), True)

    def more(part, carry):
        add_part(part, False)
        return carry

    lax.fori_loop(1, parts, more, 0)
    for turn_at in range(share // width):
        for copy in out_copies(turn_at):
            copy.wait()


def tile_chunk(owners, codes, own_rows, other_rows, occ_local, share):
    rows_total, domain = own_rows.shape
    groups = rows_total // GROUP
    held = GROUP // occ_local * CAP
    depth = 2 * groups * held
    tiles = (share, TILE, TILE)
    anywhere = pl.BlockSpec(memory_space=pl.ANY)
    in_smem = pl.BlockSpec(memory_space=pltpu.SMEM)
    return pl.pallas_call(
        functools.partial(chunk_kernel, occ_local, share),
        in_specs=[in_smem] * 3 + [anywhere] * 2,
        out_specs=[anywhere, anywhere],
        scratch_shapes=[
            pltpu.VMEM((2 * rows_total, domain), jnp.bfloat16),
            pltpu.VMEM((depth + PART, domain), jnp.bfloat16),
            pltpu.VMEM((domain + TILE, PART), jnp.bfloat16),
            pltpu.VMEM((2, held, GROUP), jnp.bfloat16),
            pltpu.VMEM((GROUP, GROUP), jnp.bfloat16),
            pltpu.VMEM((2 * share, TILE, TILE), jnp.float32),
            pltpu.VMEM(tiles, jnp.bfloat16),
            pltpu.SemaphoreType.DMA((2 * groups,)),
            pltpu.SemaphoreType.DMA((2, share)),
        ],
        out_shape=[
            jax.ShapeDtypeStruct(tiles, jnp.bfloat16),
            jax.ShapeDtypeStruct(tiles, jnp.float32),
        ],
        compiler_params=pltpu.CompilerParams(vmem_limit_bytes=56 * 1024 * 1024),
        cost_estimate=pl.CostEstimate(
            flops=4 * share * TILE * TILE * depth + 2 * depth * GROUP * domain,
            bytes_accessed=4 * rows_total * domain + 6 * share * TILE * TILE,
            transcendentals=0,
        ),
        name="tile_chunk",
    )(*owners, codes, own_rows, other_rows)


def block_columns(pair_codes, live, blocks):
    left = jnp.zeros_like(pair_codes)
    start = jnp.zeros_like(pair_codes)
    for block in range(1, blocks):
        first = block * blocks - block * (block - 1) // 2
        left = jnp.where(pair_codes >= first, block, left)
        start = jnp.where(pair_codes >= first, first, start)
    right = pair_codes - start + left
    left = jnp.where(lax.iota(jnp.int32, pair_codes.shape[0]) < live, left, blocks)
    return ((left << SHIFT) + right) * TILE


def tile_plan(half_tensor, batch_owner, pair_list, live_pairs):
    rows = lax.axis_size("row")
    aux_local, occ_local, domain = half_tensor.shape
    share = pair_list.shape[1] // rows
    orb_at = lax.axis_index("orb")
    inner = (orb_at == 1) | (orb_at == 2)
    swap = [(i, i ^ 1) for i in range(4)]
    step_a = [(0, 1), (3, 2), (1, 3), (2, 0)]
    step_b = [(0, 2), (3, 1), (1, 0), (2, 3)]

    def exchange(array, bits):
        return lax.ppermute(array, "row", [(i, i ^ bits) for i in range(rows)])

    def after(array, earlier):
        return lax.optimization_barrier((array, earlier))

    def over_x(send, keep):
        return keep + exchange(send, 2).astype(jnp.float32)

    own_rows = half_tensor.reshape(aux_local * occ_local, domain)
    other_rows = exchange(own_rows, 1)
    own_owner = batch_owner[:, 0]
    owners = own_owner, exchange(own_owner, 1)
    columns = block_columns(pair_list[0], live_pairs[0], domain // TILE)
    own_codes = jnp.concatenate([columns, orb_at[None]])
    far_codes = lax.ppermute(own_codes, "orb", [(i, i ^ 3) for i in range(4)])
    a_codes = lax.ppermute(own_codes, "orb", [(to, at) for at, to in step_a])
    b_codes = lax.ppermute(own_codes, "orb", [(to, at) for at, to in step_b])
    far_codes, a_codes, b_codes = lax.optimization_barrier((far_codes, a_codes, b_codes))

    def chunk(codes, other_rows):
        return tile_chunk(owners, codes, own_rows, other_rows, occ_local, share)

    far_send, far_keep = chunk(far_codes, other_rows)
    a_send, a_keep = chunk(a_codes, other_rows)
    far = over_x(far_send, far_keep).astype(jnp.bfloat16)
    other_rows, far = after(other_rows, far)
    far = lax.ppermute(far, "orb", swap).astype(jnp.float32)
    b_send, b_keep = chunk(b_codes, other_rows)
    a_term = over_x(a_send, a_keep) + jnp.where(inner, far, 0.0)
    other_rows, a_term = after(other_rows, a_term.astype(jnp.bfloat16))
    a_term = lax.ppermute(a_term, "orb", step_a)
    own_send, own_keep = chunk(own_codes, other_rows)
    b_keep, own_send = after(b_keep, own_send)
    b_term = over_x(b_send, b_keep) + jnp.where(inner, 0.0, far)
    b_term = lax.ppermute(b_term.astype(jnp.bfloat16), "orb", step_b)
    own_other = exchange(own_send, 2)
    part = own_keep + a_term.astype(jnp.float32)
    part, own_other, b_term = lax.optimization_barrier((part, own_other, b_term))
    total = part + own_other.astype(jnp.float32) + b_term.astype(jnp.float32)
    return total.astype(jnp.bfloat16)[None]


def per_device(half_tensor, batch_owner, pair_list, live_pairs):
    batches = lax.axis_size("orb")
    rows = lax.axis_size("row")
    aux_local, occ_local, domain = half_tensor.shape
    pair_total = pair_list.shape[1]
    tile_elements = batches * pair_total * TILE * TILE
    slab_elements = batches * CAP * aux_local * domain
    fits = (
        rows == ROWS
        and batches == 4
        and pair_total % rows == 0
        and occ_local & (occ_local - 1) == 0
        and GROUP % occ_local == 0
        and domain % GROUP == 0
        and aux_local * occ_local % GROUP == 0
        and tile_elements <= slab_elements
    )
    plan = tile_plan if fits else slab_plan
    return plan(half_tensor, batch_owner, pair_list, live_pairs)


def solution(mesh):
    return jax.shard_map(
        per_device,
        mesh=mesh,
        in_specs=(
            P(("grp", "orb"), "row", None),
            P(("grp", "row"), None),
            P(("grp", "orb"), None),
            P(("grp", "orb")),
        ),
        out_specs=P(("grp", "orb"), "row", None, None),
        check_vma=False,
    )
```

```python
import functools
import math

import jax
import jax.numpy as jnp
from jax import lax
from jax.experimental import pallas as pl
from jax.experimental.pallas import tpu as pltpu
from jax.sharding import PartitionSpec as P

TILE = 128
CAP = 8
GROUP = 256
PART = 512
ROWS = 4
SHIFT = 16


def block_pairs(pair_codes, blocks):
    row_grid = lax.broadcasted_iota(jnp.int32, (blocks, blocks), 0)
    col_grid = lax.broadcasted_iota(jnp.int32, (blocks, blocks), 1)
    code_grid = row_grid * blocks - row_grid * (row_grid - 1) // 2 + (col_grid - row_grid)
    upper_part = col_grid >= row_grid
    matches = (code_grid[None, :, :] == pair_codes[:, None, None]) & upper_part[None, :, :]
    first_blocks = jnp.sum(jnp.where(matches, row_grid[None], 0), axis=(1, 2))
    second_blocks = jnp.sum(jnp.where(matches, col_grid[None], 0), axis=(1, 2))
    return (first_blocks, second_blocks)


def slot_sources(owner_local, batches, capacity):
    local_count = owner_local.shape[0]
    batch_ids = lax.broadcasted_iota(jnp.int32, (local_count, batches), 1)
    onehot = (owner_local[:, None] == batch_ids).astype(jnp.int32)
    ranking = jnp.cumsum(onehot, axis=0) - 1
    slot_of = jnp.sum(ranking * onehot, axis=1)
    target = owner_local * capacity + slot_of
    slot_ids = lax.broadcasted_iota(jnp.int32, (local_count, batches * capacity), 1)
    orbital_ids = lax.broadcasted_iota(jnp.int32, (local_count, batches * capacity), 0)
    slot_hits = target[:, None] == slot_ids
    source_row = jnp.sum(jnp.where(slot_hits, orbital_ids, 0), axis=0)
    filled = jnp.any(slot_hits, axis=0)
    return jnp.where(filled, source_row, local_count)


def slab_plan(half_tensor, batch_owner, pair_list, live_pairs):
    batches = lax.axis_size("orb")
    aux_local, occ_local, domain = half_tensor.shape
    blocks = domain // TILE
    sources = slot_sources(batch_owner[:, 0], batches, CAP)
    block_major = half_tensor.reshape(aux_local, occ_local, blocks, TILE).transpose(2, 1, 0, 3)
    outgoing = jnp.take(block_major, sources, axis=1, mode="fill", fill_value=0)
    arrived = lax.all_to_all(outgoing, "orb", split_axis=1, concat_axis=2, tiled=True)
    stacked_rows = arrived.reshape(blocks, -1, TILE)
    first_blocks, second_blocks = block_pairs(pair_list[0], blocks)
    live_count = live_pairs[0]
    pair_total = pair_list.shape[1]
    contract = (((0,), (0,)), ((), ()))
    group_size = math.gcd(4, pair_total)

    def one_group(group_index):
        pair_start = group_index * group_size
        tiles = []
        for offset in range(group_size):
            left = lax.dynamic_index_in_dim(
                stacked_rows, first_blocks[pair_start + offset], 0, keepdims=False
            )
            right = lax.dynamic_index_in_dim(
                stacked_rows, second_blocks[pair_start + offset], 0, keepdims=False
            )
            tiles.append(
                lax.dot_general(left, right, contract, preferred_element_type=jnp.float32)
            )
        keep_mask = pair_start + lax.iota(jnp.int32, group_size) < live_count
        return jnp.where(keep_mask[:, None, None], jnp.stack(tiles, axis=0), jnp.float32(0.0))

    grouped = lax.map(one_group, jnp.arange(pair_total // group_size, dtype=jnp.int32))
    terms = grouped.reshape(pair_total, TILE, TILE)
    mine = lax.psum_scatter(terms.astype(jnp.bfloat16), "row", scatter_dimension=0, tiled=True)
    return mine[None]


def chunk_kernel(occ_local, share, halves, own_owner, other_owner, codes, own_rows, other_rows, *refs):
    send_outs, keep_outs = refs[:halves], refs[halves:2 * halves]
    stage, packed_rows, turned, pick, sums, send_ref, arrived, left_off = refs[2 * halves:]
    rows_total, domain = own_rows.shape
    groups = rows_total // GROUP
    per_group = GROUP // occ_local
    held = per_group * CAP
    batch = codes[share * ROWS]

    def slab_copy(place):
        slab = own_rows if place < groups else other_rows
        return pltpu.make_async_copy(
            slab.at[pl.ds(place % groups * GROUP, GROUP), :],
            stage.at[pl.ds(place * GROUP, GROUP), :],
            arrived.at[place],
        )

    for place in range(2 * groups):
        slab_copy(place).start()

    lane = lax.broadcasted_iota(jnp.int32, (1, GROUP), 1)
    orbital_of = lane & (occ_local - 1)
    turn_of = lane >> (occ_local.bit_length() - 1)
    slot = lax.broadcasted_iota(jnp.int32, (held, GROUP), 0)
    counts = []
    for source, owner in enumerate((own_owner, other_owner)):
        count = jnp.int32(0)
        rank = jnp.full((1, GROUP), -GROUP * CAP, jnp.int32)
        for orbital in range(occ_local):
            mine = owner[orbital] == batch
            rank = jnp.where(orbital_of == orbital, jnp.where(mine, count, -GROUP * CAP), rank)
            count = count + mine.astype(jnp.int32)
        pick[source] = (slot == turn_of * count + rank).astype(jnp.bfloat16)
        counts.append(count)
    turned[domain:, :] = jnp.zeros((TILE, PART), jnp.bfloat16)

    def pack(place, carry):
        rows = pl.ds(pl.multiple_of(place * GROUP, GROUP), GROUP)
        pltpu.make_async_copy(
            own_rows.at[pl.ds(0, GROUP), :], stage.at[rows, :], arrived.at[place]
        ).wait()
        source = (place >= groups).astype(jnp.int32)
        before = jnp.minimum(place, groups) * counts[0]
        before = before + jnp.maximum(place - groups, 0) * counts[1]
        start = pl.multiple_of(before * per_group, per_group)
        for column in range(0, domain, 2 * TILE):
            columns = slice(column, column + 2 * TILE)
            packed = jnp.dot(
                pick[source], stage[rows, columns], preferred_element_type=jnp.float32
            )
            packed_rows[pl.ds(start, held), columns] = packed.astype(jnp.bfloat16)
        return carry

    lax.fori_loop(0, 2 * groups, pack, 0)
    filled = pl.multiple_of((counts[0] + counts[1]) * groups * per_group, per_group)
    packed_rows[pl.ds(filled, PART), :] = jnp.zeros((PART, domain), jnp.bfloat16)
    parts = jnp.maximum((filled + PART - 1) // PART, 1)

    row_at = lax.axis_index("row")
    send_first = (row_at ^ 2) * share
    keep_first = row_at * share
    width = math.gcd(4, share)

    turns = share // width // halves

    def out_copies(half, turn_at):
        sends = pl.ds((half * turns + turn_at) * width, width)
        keeps = pl.ds(share + (half * turns + turn_at) * width, width)
        to = pl.ds(turn_at * width, width)
        return (
            pltpu.make_async_copy(
                send_ref.at[sends], send_outs[half].at[to], left_off.at[half, 0, turn_at]
            ),
            pltpu.make_async_copy(
                sums.at[keeps], keep_outs[half].at[to], left_off.at[half, 1, turn_at]
            ),
        )

    def add_part(part, fresh):
        rows = pl.ds(pl.multiple_of(part * PART, PART), PART)
        for column in range(0, domain, TILE):
            columns = slice(column, column + TILE)
            turned[columns, :] = packed_rows[rows, columns].T

        def several(half, turn_at, carry):
            for offset in range(width):
                at = (half * turns + turn_at) * width + offset
                for pair, to in ((send_first + at, at), (keep_first + at, share + at)):
                    code = codes[pair]
                    left = pl.multiple_of(code >> SHIFT, TILE)
                    right = pl.multiple_of(code & ((1 << SHIFT) - 1), TILE)
                    product = jnp.dot(
                        turned[pl.ds(left, TILE), :],
                        packed_rows[rows, pl.ds(right, TILE)],
                        preferred_element_type=jnp.float32,
                    )
                    sums[to] = product if fresh else sums[to] + product

            @pl.when(part == parts - 1)
            def _():
                sends = pl.ds((half * turns + turn_at) * width, width)
                send_ref[sends] = sums[sends].astype(send_ref.dtype)
                for copy in out_copies(half, turn_at):
                    copy.start()

            return carry

        for half in range(halves):
            lax.fori_loop(0, turns, functools.partial(several, half), 0)

    add_part(jnp.int32(0), True)

    def more(part, carry):
        add_part(part, False)
        return carry

    lax.fori_loop(1, parts, more, 0)
    for half in range(halves):
        for turn_at in range(turns):
            for copy in out_copies(half, turn_at):
                copy.wait()


def tile_chunk(owners, codes, own_rows, other_rows, occ_local, share, halves):
    rows_total, domain = own_rows.shape
    groups = rows_total // GROUP
    held = GROUP // occ_local * CAP
    depth = 2 * groups * held
    tiles = (share, TILE, TILE)
    anywhere = pl.BlockSpec(memory_space=pl.ANY)
    in_smem = pl.BlockSpec(memory_space=pltpu.SMEM)
    return pl.pallas_call(
        functools.partial(chunk_kernel, occ_local, share, halves),
        in_specs=[in_smem] * 3 + [anywhere] * 2,
        out_specs=[anywhere] * (2 * halves),
        scratch_shapes=[
            pltpu.VMEM((2 * rows_total, domain), jnp.bfloat16),
            pltpu.VMEM((depth + PART, domain), jnp.bfloat16),
            pltpu.VMEM((domain + TILE, PART), jnp.bfloat16),
            pltpu.VMEM((2, held, GROUP), jnp.bfloat16),
            pltpu.VMEM((2 * share, TILE, TILE), jnp.float32),
            pltpu.VMEM(tiles, jnp.bfloat16),
            pltpu.SemaphoreType.DMA((2 * groups,)),
            pltpu.SemaphoreType.DMA((halves, 2, share)),
        ],
        out_shape=[
            jax.ShapeDtypeStruct((share // halves, TILE, TILE), kind)
            for kind in (jnp.bfloat16, jnp.float32)
            for _ in range(halves)
        ],
        compiler_params=pltpu.CompilerParams(vmem_limit_bytes=56 * 1024 * 1024),
        cost_estimate=pl.CostEstimate(
            flops=4 * share * TILE * TILE * depth + 2 * depth * GROUP * domain,
            bytes_accessed=4 * rows_total * domain + 6 * share * TILE * TILE,
            transcendentals=0,
        ),
        name="tile_chunk",
    )(*owners, codes, own_rows, other_rows)


def block_columns(pair_codes, live, blocks):
    left = jnp.zeros_like(pair_codes)
    start = jnp.zeros_like(pair_codes)
    for block in range(1, blocks):
        first = block * blocks - block * (block - 1) // 2
        left = jnp.where(pair_codes >= first, block, left)
        start = jnp.where(pair_codes >= first, first, start)
    right = pair_codes - start + left
    left = jnp.where(lax.iota(jnp.int32, pair_codes.shape[0]) < live, left, blocks)
    return ((left << SHIFT) + right) * TILE


def tile_plan(half_tensor, batch_owner, pair_list, live_pairs):
    rows = lax.axis_size("row")
    aux_local, occ_local, domain = half_tensor.shape
    share = pair_list.shape[1] // rows
    orb_at = lax.axis_index("orb")
    inner = (orb_at == 1) | (orb_at == 2)
    swap = [(i, i ^ 1) for i in range(4)]
    step_a = [(0, 1), (3, 2), (1, 3), (2, 0)]
    step_b = [(0, 2), (3, 1), (1, 0), (2, 3)]

    def exchange(array, bits):
        return lax.ppermute(array, "row", [(i, i ^ bits) for i in range(rows)])

    def after(array, earlier):
        return lax.optimization_barrier((array, earlier))

    def over_x(send, keep):
        return keep + exchange(send, 2).astype(jnp.float32)

    own_rows = half_tensor.reshape(aux_local * occ_local, domain)
    other_rows = exchange(own_rows, 1)
    own_owner = batch_owner[:, 0]
    owners = own_owner, exchange(own_owner, 1)
    columns = block_columns(pair_list[0], live_pairs[0], domain // TILE)
    own_codes = jnp.concatenate([columns, orb_at[None]])
    far_codes = lax.ppermute(own_codes, "orb", [(i, i ^ 3) for i in range(4)])
    a_codes = lax.ppermute(own_codes, "orb", [(to, at) for at, to in step_a])
    b_codes = lax.ppermute(own_codes, "orb", [(to, at) for at, to in step_b])
    b_codes, a_codes, far_codes = lax.optimization_barrier((b_codes, a_codes, far_codes))

    def chunk(codes, halves=1):
        return tile_chunk(owners, codes, own_rows, other_rows, occ_local, share, halves)

    send_1, send_2, keep_1, keep_2 = chunk(far_codes, 2)
    a_send, a_keep = chunk(a_codes)
    far_1, a_send = after(exchange(send_1, 2), a_send)
    far_1 = (keep_1 + far_1.astype(jnp.float32)).astype(jnp.bfloat16)
    b_codes, far_1 = after(b_codes, far_1)
    far_1 = lax.ppermute(far_1, "orb", swap)
    b_send, b_keep = chunk(b_codes)
    far_2 = exchange(send_2, 2)
    far_2, far_1, b_send = lax.optimization_barrier((far_2, far_1, b_send))
    far_2 = (keep_2 + far_2.astype(jnp.float32)).astype(jnp.bfloat16)
    far_2 = lax.ppermute(far_2, "orb", swap)
    far = jnp.concatenate([far_1, far_2]).astype(jnp.float32)
    a_term = over_x(a_send, a_keep) + jnp.where(inner, far, 0.0)
    own_codes, a_term = after(own_codes, a_term.astype(jnp.bfloat16))
    a_term = lax.ppermute(a_term, "orb", step_a)
    own_send, own_keep = chunk(own_codes)
    b_keep, own_send = after(b_keep, own_send)
    b_term = over_x(b_send, b_keep) + jnp.where(inner, 0.0, far)
    b_term = lax.ppermute(b_term.astype(jnp.bfloat16), "orb", step_b)
    own_other = exchange(own_send, 2)
    part = own_keep + a_term.astype(jnp.float32)
    part, own_other, b_term = lax.optimization_barrier((part, own_other, b_term))
    total = part + own_other.astype(jnp.float32) + b_term.astype(jnp.float32)
    return total.astype(jnp.bfloat16)[None]


def per_device(half_tensor, batch_owner, pair_list, live_pairs):
    batches = lax.axis_size("orb")
    rows = lax.axis_size("row")
    aux_local, occ_local, domain = half_tensor.shape
    pair_total = pair_list.shape[1]
    tile_elements = batches * pair_total * TILE * TILE
    slab_elements = batches * CAP * aux_local * domain
    fits = (
        rows == ROWS
        and batches == 4
        and pair_total % (8 * rows) == 0
        and occ_local & (occ_local - 1) == 0
        and GROUP % occ_local == 0
        and aux_local * occ_local % GROUP == 0
        and tile_elements <= slab_elements
    )
    plan = tile_plan if fits else slab_plan
    return plan(half_tensor, batch_owner, pair_list, live_pairs)


def solution(mesh):
    return jax.shard_map(
        per_device,
        mesh=mesh,
        in_specs=(
            P(("grp", "orb"), "row", None),
            P(("grp", "row"), None),
            P(("grp", "orb"), None),
            P(("grp", "orb")),
        ),
        out_specs=P(("grp", "orb"), "row", None, None),
        check_vma=False,
    )
```

```python
import functools
import math

import jax
import jax.numpy as jnp
from jax import lax
from jax.experimental import pallas as pl
from jax.experimental.pallas import tpu as pltpu
from jax.sharding import PartitionSpec as P

TILE = 128
CAP = 8
GROUP = 256
PART = 512
ROWS = 4
SHIFT = 16


def block_pairs(pair_codes, blocks):
    row_grid = lax.broadcasted_iota(jnp.int32, (blocks, blocks), 0)
    col_grid = lax.broadcasted_iota(jnp.int32, (blocks, blocks), 1)
    code_grid = row_grid * blocks - row_grid * (row_grid - 1) // 2 + (col_grid - row_grid)
    upper_part = col_grid >= row_grid
    matches = (code_grid[None, :, :] == pair_codes[:, None, None]) & upper_part[None, :, :]
    first_blocks = jnp.sum(jnp.where(matches, row_grid[None], 0), axis=(1, 2))
    second_blocks = jnp.sum(jnp.where(matches, col_grid[None], 0), axis=(1, 2))
    return (first_blocks, second_blocks)


def slot_sources(owner_local, batches, capacity):
    local_count = owner_local.shape[0]
    batch_ids = lax.broadcasted_iota(jnp.int32, (local_count, batches), 1)
    onehot = (owner_local[:, None] == batch_ids).astype(jnp.int32)
    ranking = jnp.cumsum(onehot, axis=0) - 1
    slot_of = jnp.sum(ranking * onehot, axis=1)
    target = owner_local * capacity + slot_of
    slot_ids = lax.broadcasted_iota(jnp.int32, (local_count, batches * capacity), 1)
    orbital_ids = lax.broadcasted_iota(jnp.int32, (local_count, batches * capacity), 0)
    slot_hits = target[:, None] == slot_ids
    source_row = jnp.sum(jnp.where(slot_hits, orbital_ids, 0), axis=0)
    filled = jnp.any(slot_hits, axis=0)
    return jnp.where(filled, source_row, local_count)


def slab_plan(half_tensor, batch_owner, pair_list, live_pairs):
    batches = lax.axis_size("orb")
    aux_local, occ_local, domain = half_tensor.shape
    blocks = domain // TILE
    sources = slot_sources(batch_owner[:, 0], batches, CAP)
    block_major = half_tensor.reshape(aux_local, occ_local, blocks, TILE).transpose(2, 1, 0, 3)
    outgoing = jnp.take(block_major, sources, axis=1, mode="fill", fill_value=0)
    arrived = lax.all_to_all(outgoing, "orb", split_axis=1, concat_axis=2, tiled=True)
    stacked_rows = arrived.reshape(blocks, -1, TILE)
    first_blocks, second_blocks = block_pairs(pair_list[0], blocks)
    live_count = live_pairs[0]
    pair_total = pair_list.shape[1]
    contract = (((0,), (0,)), ((), ()))
    group_size = math.gcd(4, pair_total)

    def one_group(group_index):
        pair_start = group_index * group_size
        tiles = []
        for offset in range(group_size):
            left = lax.dynamic_index_in_dim(
                stacked_rows, first_blocks[pair_start + offset], 0, keepdims=False
            )
            right = lax.dynamic_index_in_dim(
                stacked_rows, second_blocks[pair_start + offset], 0, keepdims=False
            )
            tiles.append(
                lax.dot_general(left, right, contract, preferred_element_type=jnp.float32)
            )
        keep_mask = pair_start + lax.iota(jnp.int32, group_size) < live_count
        return jnp.where(keep_mask[:, None, None], jnp.stack(tiles, axis=0), jnp.float32(0.0))

    grouped = lax.map(one_group, jnp.arange(pair_total // group_size, dtype=jnp.int32))
    terms = grouped.reshape(pair_total, TILE, TILE)
    mine = lax.psum_scatter(terms.astype(jnp.bfloat16), "row", scatter_dimension=0, tiled=True)
    return mine[None]


def chunk_kernel(occ_local, share, own_owner, other_owner, codes, own_rows, other_rows, *refs):
    send_out, keep_out = refs[:2]
    stage, packed_rows, turned, pick, sums, send_ref, arrived, left_off = refs[2:]
    rows_total, domain = own_rows.shape
    groups = rows_total // GROUP
    per_group = GROUP // occ_local
    held = per_group * CAP
    batch = codes[share * ROWS]

    def slab_copy(place):
        slab = own_rows if place < groups else other_rows
        return pltpu.make_async_copy(
            slab.at[pl.ds(place % groups * GROUP, GROUP), :],
            stage.at[pl.ds(place * GROUP, GROUP), :],
            arrived.at[place],
        )

    for place in range(2 * groups):
        slab_copy(place).start()

    lane = lax.broadcasted_iota(jnp.int32, (1, GROUP), 1)
    orbital_of = lane & (occ_local - 1)
    turn_of = lane >> (occ_local.bit_length() - 1)
    slot = lax.broadcasted_iota(jnp.int32, (held, GROUP), 0)
    counts = []
    for source, owner in enumerate((own_owner, other_owner)):
        count = jnp.int32(0)
        rank = jnp.full((1, GROUP), -GROUP * CAP, jnp.int32)
        for orbital in range(occ_local):
            mine = owner[orbital] == batch
            rank = jnp.where(orbital_of == orbital, jnp.where(mine, count, -GROUP * CAP), rank)
            count = count + mine.astype(jnp.int32)
        pick[source] = (slot == turn_of * count + rank).astype(jnp.bfloat16)
        counts.append(count)
    turned[domain:, :] = jnp.zeros((TILE, PART), jnp.bfloat16)

    def pack(place, carry):
        rows = pl.ds(pl.multiple_of(place * GROUP, GROUP), GROUP)
        pltpu.make_async_copy(
            own_rows.at[pl.ds(0, GROUP), :], stage.at[rows, :], arrived.at[place]
        ).wait()
        source = (place >= groups).astype(jnp.int32)
        before = jnp.minimum(place, groups) * counts[0]
        before = before + jnp.maximum(place - groups, 0) * counts[1]
        start = pl.multiple_of(before * per_group, per_group)
        for column in range(0, domain, 2 * TILE):
            columns = slice(column, column + 2 * TILE)
            packed = jnp.dot(
                pick[source], stage[rows, columns], preferred_element_type=jnp.float32
            )
            packed_rows[pl.ds(start, held), columns] = packed.astype(jnp.bfloat16)
        return carry

    lax.fori_loop(0, 2 * groups, pack, 0)
    filled = pl.multiple_of((counts[0] + counts[1]) * groups * per_group, per_group)
    packed_rows[pl.ds(filled, PART), :] = jnp.zeros((PART, domain), jnp.bfloat16)
    more_parts = jnp.maximum(filled - PART + GROUP - 1, 0) // GROUP

    row_at = lax.axis_index("row")
    send_first = (row_at ^ 2) * share
    keep_first = row_at * share
    width = math.gcd(4, share)

    def out_copies(turn_at):
        sends = pl.ds(turn_at * width, width)
        keeps = pl.ds(share + turn_at * width, width)
        return (
            pltpu.make_async_copy(send_ref.at[sends], send_out.at[sends], left_off.at[0, turn_at]),
            pltpu.make_async_copy(sums.at[keeps], keep_out.at[sends], left_off.at[1, turn_at]),
        )

    def add_part(first_row, depth, fresh, last):
        rows = pl.ds(first_row, depth)
        for column in range(0, domain, TILE):
            columns = slice(column, column + TILE)
            turned[columns, :depth] = packed_rows[rows, columns].T

        def several(turn_at, carry):
            for offset in range(width):
                at = turn_at * width + offset
                for pair, to in ((send_first + at, at), (keep_first + at, share + at)):
                    code = codes[pair]
                    left = pl.multiple_of(code >> SHIFT, TILE)
                    right = pl.multiple_of(code & ((1 << SHIFT) - 1), TILE)
                    product = jnp.dot(
                        turned[pl.ds(left, TILE), :depth],
                        packed_rows[rows, pl.ds(right, TILE)],
                        preferred_element_type=jnp.float32,
                    )
                    sums[to] = product if fresh else sums[to] + product

            @pl.when(last)
            def _():
                sends = pl.ds(turn_at * width, width)
                send_ref[sends] = sums[sends].astype(send_ref.dtype)
                for copy in out_copies(turn_at):
                    copy.start()

            return carry

        lax.fori_loop(0, share // width, several, 0)

    add_part(0, PART, True, more_parts == 0)

    def more(part, carry):
        first_row = pl.multiple_of(PART + part * GROUP, GROUP)
        add_part(first_row, GROUP, False, part == more_parts - 1)
        return carry

    lax.fori_loop(0, more_parts, more, 0)
    for turn_at in range(share // width):
        for copy in out_copies(turn_at):
            copy.wait()


def tile_chunk(owners, codes, own_rows, other_rows, occ_local, share):
    rows_total, domain = own_rows.shape
    groups = rows_total // GROUP
    held = GROUP // occ_local * CAP
    depth = 2 * groups * held
    tiles = (share, TILE, TILE)
    anywhere = pl.BlockSpec(memory_space=pl.ANY)
    in_smem = pl.BlockSpec(memory_space=pltpu.SMEM)
    return pl.pallas_call(
        functools.partial(chunk_kernel, occ_local, share),
        in_specs=[in_smem] * 3 + [anywhere] * 2,
        out_specs=[anywhere, anywhere],
        scratch_shapes=[
            pltpu.VMEM((2 * rows_total, domain), jnp.bfloat16),
            pltpu.VMEM((depth + PART, domain), jnp.bfloat16),
            pltpu.VMEM((domain + TILE, PART), jnp.bfloat16),
            pltpu.VMEM((2, held, GROUP), jnp.bfloat16),
            pltpu.VMEM((2 * share, TILE, TILE), jnp.float32),
            pltpu.VMEM(tiles, jnp.bfloat16),
            pltpu.SemaphoreType.DMA((2 * groups,)),
            pltpu.SemaphoreType.DMA((2, share)),
        ],
        out_shape=[
            jax.ShapeDtypeStruct(tiles, jnp.bfloat16),
            jax.ShapeDtypeStruct(tiles, jnp.float32),
        ],
        compiler_params=pltpu.CompilerParams(vmem_limit_bytes=56 * 1024 * 1024),
        cost_estimate=pl.CostEstimate(
            flops=4 * share * TILE * TILE * depth + 2 * depth * GROUP * domain,
            bytes_accessed=4 * rows_total * domain + 6 * share * TILE * TILE,
            transcendentals=0,
        ),
        name="tile_chunk",
    )(*owners, codes, own_rows, other_rows)


def block_columns(pair_codes, live, blocks):
    left = jnp.zeros_like(pair_codes)
    start = jnp.zeros_like(pair_codes)
    for block in range(1, blocks):
        first = block * blocks - block * (block - 1) // 2
        left = jnp.where(pair_codes >= first, block, left)
        start = jnp.where(pair_codes >= first, first, start)
    right = pair_codes - start + left
    left = jnp.where(lax.iota(jnp.int32, pair_codes.shape[0]) < live, left, blocks)
    return ((left << SHIFT) + right) * TILE


def tile_plan(half_tensor, batch_owner, pair_list, live_pairs):
    rows = lax.axis_size("row")
    aux_local, occ_local, domain = half_tensor.shape
    share = pair_list.shape[1] // rows
    orb_at = lax.axis_index("orb")
    inner = (orb_at == 1) | (orb_at == 2)
    swap = [(i, i ^ 1) for i in range(4)]
    step_a = [(0, 1), (3, 2), (1, 3), (2, 0)]
    step_b = [(0, 2), (3, 1), (1, 0), (2, 3)]

    def exchange(array, bits):
        return lax.ppermute(array, "row", [(i, i ^ bits) for i in range(rows)])

    def after(array, earlier):
        return lax.optimization_barrier((array, earlier))

    def over_x(send, keep):
        return keep + exchange(send, 2).astype(jnp.float32)

    own_rows = half_tensor.reshape(aux_local * occ_local, domain)
    other_rows = exchange(own_rows, 1)
    own_owner = batch_owner[:, 0]
    owners = own_owner, exchange(own_owner, 1)
    columns = block_columns(pair_list[0], live_pairs[0], domain // TILE)
    own_codes = jnp.concatenate([columns, orb_at[None]])
    far_codes = lax.ppermute(own_codes, "orb", [(i, i ^ 3) for i in range(4)])
    a_codes = lax.ppermute(own_codes, "orb", [(to, at) for at, to in step_a])
    b_codes = lax.ppermute(own_codes, "orb", [(to, at) for at, to in step_b])
    far_codes, a_codes, b_codes = lax.optimization_barrier((far_codes, a_codes, b_codes))

    def chunk(codes, other_rows):
        return tile_chunk(owners, codes, own_rows, other_rows, occ_local, share)

    far_send, far_keep = chunk(far_codes, other_rows)
    a_send, a_keep = chunk(a_codes, other_rows)
    far = over_x(far_send, far_keep).astype(jnp.bfloat16)
    other_rows, far = after(other_rows, far)
    far = lax.ppermute(far, "orb", swap).astype(jnp.float32)
    b_send, b_keep = chunk(b_codes, other_rows)
    a_term = over_x(a_send, a_keep) + jnp.where(inner, far, 0.0)
    other_rows, a_term = after(other_rows, a_term.astype(jnp.bfloat16))
    a_term = lax.ppermute(a_term, "orb", step_a)
    own_send, own_keep = chunk(own_codes, other_rows)
    b_keep, own_send = after(b_keep, own_send)
    b_term = over_x(b_send, b_keep) + jnp.where(inner, 0.0, far)
    b_term = lax.ppermute(b_term.astype(jnp.bfloat16), "orb", step_b)
    own_other = exchange(own_send, 2)
    part = own_keep + a_term.astype(jnp.float32)
    part, own_other, b_term = lax.optimization_barrier((part, own_other, b_term))
    total = part + own_other.astype(jnp.float32) + b_term.astype(jnp.float32)
    return total.astype(jnp.bfloat16)[None]


def per_device(half_tensor, batch_owner, pair_list, live_pairs):
    batches = lax.axis_size("orb")
    rows = lax.axis_size("row")
    aux_local, occ_local, domain = half_tensor.shape
    pair_total = pair_list.shape[1]
    tile_elements = batches * pair_total * TILE * TILE
    slab_elements = batches * CAP * aux_local * domain
    fits = (
        rows == ROWS
        and batches == 4
        and pair_total % rows == 0
        and occ_local & (occ_local - 1) == 0
        and GROUP % occ_local == 0
        and aux_local * occ_local % GROUP == 0
        and tile_elements <= slab_elements
    )
    plan = tile_plan if fits else slab_plan
    return plan(half_tensor, batch_owner, pair_list, live_pairs)


def solution(mesh):
    return jax.shard_map(
        per_device,
        mesh=mesh,
        in_specs=(
            P(("grp", "orb"), "row", None),
            P(("grp", "row"), None),
            P(("grp", "orb"), None),
            P(("grp", "orb")),
        ),
        out_specs=P(("grp", "orb"), "row", None, None),
        check_vma=False,
    )
```

```python
import functools
import math

import jax
import jax.numpy as jnp
from jax import lax
from jax.experimental import pallas as pl
from jax.experimental.pallas import tpu as pltpu
from jax.sharding import PartitionSpec as P

TILE = 128
CAP = 8
GROUP = 256
PART = 512
ROWS = 4
SHIFT = 16


def block_pairs(pair_codes, blocks):
    row_grid = lax.broadcasted_iota(jnp.int32, (blocks, blocks), 0)
    col_grid = lax.broadcasted_iota(jnp.int32, (blocks, blocks), 1)
    code_grid = row_grid * blocks - row_grid * (row_grid - 1) // 2 + (col_grid - row_grid)
    upper_part = col_grid >= row_grid
    matches = (code_grid[None, :, :] == pair_codes[:, None, None]) & upper_part[None, :, :]
    first_blocks = jnp.sum(jnp.where(matches, row_grid[None], 0), axis=(1, 2))
    second_blocks = jnp.sum(jnp.where(matches, col_grid[None], 0), axis=(1, 2))
    return (first_blocks, second_blocks)


def slot_sources(owner_local, batches, capacity):
    local_count = owner_local.shape[0]
    batch_ids = lax.broadcasted_iota(jnp.int32, (local_count, batches), 1)
    onehot = (owner_local[:, None] == batch_ids).astype(jnp.int32)
    ranking = jnp.cumsum(onehot, axis=0) - 1
    slot_of = jnp.sum(ranking * onehot, axis=1)
    target = owner_local * capacity + slot_of
    slot_ids = lax.broadcasted_iota(jnp.int32, (local_count, batches * capacity), 1)
    orbital_ids = lax.broadcasted_iota(jnp.int32, (local_count, batches * capacity), 0)
    slot_hits = target[:, None] == slot_ids
    source_row = jnp.sum(jnp.where(slot_hits, orbital_ids, 0), axis=0)
    filled = jnp.any(slot_hits, axis=0)
    return jnp.where(filled, source_row, local_count)


def slab_plan(half_tensor, batch_owner, pair_list, live_pairs):
    batches = lax.axis_size("orb")
    aux_local, occ_local, domain = half_tensor.shape
    blocks = domain // TILE
    sources = slot_sources(batch_owner[:, 0], batches, CAP)
    block_major = half_tensor.reshape(aux_local, occ_local, blocks, TILE).transpose(2, 1, 0, 3)
    outgoing = jnp.take(block_major, sources, axis=1, mode="fill", fill_value=0)
    arrived = lax.all_to_all(outgoing, "orb", split_axis=1, concat_axis=2, tiled=True)
    stacked_rows = arrived.reshape(blocks, -1, TILE)
    first_blocks, second_blocks = block_pairs(pair_list[0], blocks)
    live_count = live_pairs[0]
    pair_total = pair_list.shape[1]
    contract = (((0,), (0,)), ((), ()))
    group_size = math.gcd(4, pair_total)

    def one_group(group_index):
        pair_start = group_index * group_size
        tiles = []
        for offset in range(group_size):
            left = lax.dynamic_index_in_dim(
                stacked_rows, first_blocks[pair_start + offset], 0, keepdims=False
            )
            right = lax.dynamic_index_in_dim(
                stacked_rows, second_blocks[pair_start + offset], 0, keepdims=False
            )
            tiles.append(
                lax.dot_general(left, right, contract, preferred_element_type=jnp.float32)
            )
        keep_mask = pair_start + lax.iota(jnp.int32, group_size) < live_count
        return jnp.where(keep_mask[:, None, None], jnp.stack(tiles, axis=0), jnp.float32(0.0))

    grouped = lax.map(one_group, jnp.arange(pair_total // group_size, dtype=jnp.int32))
    terms = grouped.reshape(pair_total, TILE, TILE)
    mine = lax.psum_scatter(terms.astype(jnp.bfloat16), "row", scatter_dimension=0, tiled=True)
    return mine[None]


def chunk_kernel(occ_local, share, own_owner, other_owner, codes, own_rows, other_rows, *refs):
    send_out, keep_out = refs[:2]
    stage, packed_rows, turned, pick, sums, send_ref, arrived, left_off = refs[2:]
    rows_total, domain = own_rows.shape
    groups = rows_total // GROUP
    per_group = GROUP // occ_local
    held = per_group * CAP
    batch = codes[share * ROWS]

    def slab_copy(place):
        slab = own_rows if place < groups else other_rows
        return pltpu.make_async_copy(
            slab.at[pl.ds(place % groups * GROUP, GROUP), :],
            stage.at[pl.ds(place * GROUP, GROUP), :],
            arrived.at[place],
        )

    for place in range(2 * groups):
        slab_copy(place).start()

    lane = lax.broadcasted_iota(jnp.int32, (1, GROUP), 1)
    orbital_of = lane & (occ_local - 1)
    turn_of = lane >> (occ_local.bit_length() - 1)
    slot = lax.broadcasted_iota(jnp.int32, (held, GROUP), 0)
    counts = []
    for source, owner in enumerate((own_owner, other_owner)):
        count = jnp.int32(0)
        rank = jnp.full((1, GROUP), -GROUP * CAP, jnp.int32)
        for orbital in range(occ_local):
            mine = owner[orbital] == batch
            rank = jnp.where(orbital_of == orbital, jnp.where(mine, count, -GROUP * CAP), rank)
            count = count + mine.astype(jnp.int32)
        pick[source] = (slot == turn_of * count + rank).astype(jnp.bfloat16)
        counts.append(count)
    turned[domain:, :] = jnp.zeros((TILE, PART), jnp.bfloat16)

    def pack(place, carry):
        rows = pl.ds(pl.multiple_of(place * GROUP, GROUP), GROUP)
        pltpu.make_async_copy(
            own_rows.at[pl.ds(0, GROUP), :], stage.at[rows, :], arrived.at[place]
        ).wait()
        source = (place >= groups).astype(jnp.int32)
        before = jnp.minimum(place, groups) * counts[0]
        before = before + jnp.maximum(place - groups, 0) * counts[1]
        start = pl.multiple_of(before * per_group, per_group)
        for column in range(0, domain, 2 * TILE):
            columns = slice(column, column + 2 * TILE)
            packed = jnp.dot(
                pick[source], stage[rows, columns], preferred_element_type=jnp.float32
            )
            packed_rows[pl.ds(start, held), columns] = packed.astype(jnp.bfloat16)
        return carry

    lax.fori_loop(0, 2 * groups, pack, 0)
    filled = pl.multiple_of((counts[0] + counts[1]) * groups * per_group, per_group)
    packed_rows[pl.ds(filled, PART), :] = jnp.zeros((PART, domain), jnp.bfloat16)
    parts = jnp.maximum((filled + PART - 1) // PART, 1)

    row_at = lax.axis_index("row")
    send_first = (row_at ^ 2) * share
    keep_first = row_at * share
    width = math.gcd(4, share)

    def out_copies(turn_at):
        sends = pl.ds(turn_at * width, width)
        keeps = pl.ds(share + turn_at * width, width)
        return (
            pltpu.make_async_copy(send_ref.at[sends], send_out.at[sends], left_off.at[0, turn_at]),
            pltpu.make_async_copy(sums.at[keeps], keep_out.at[sends], left_off.at[1, turn_at]),
        )

    def add_part(part, fresh):
        rows = pl.ds(pl.multiple_of(part * PART, PART), PART)
        for column in range(0, domain, TILE):
            columns = slice(column, column + TILE)
            turned[columns, :] = packed_rows[rows, columns].T

        def several(turn_at, carry):
            for offset in range(width):
                at = turn_at * width + offset
                for pair, to in ((send_first + at, at), (keep_first + at, share + at)):
                    code = codes[pair]
                    left = pl.multiple_of(code >> SHIFT, TILE)
                    right = pl.multiple_of(code & ((1 << SHIFT) - 1), TILE)
                    product = jnp.dot(
                        turned[pl.ds(left, TILE), :],
                        packed_rows[rows, pl.ds(right, TILE)],
                        preferred_element_type=jnp.float32,
                    )
                    sums[to] = product if fresh else sums[to] + product

            @pl.when(part == parts - 1)
            def _():
                sends = pl.ds(turn_at * width, width)
                send_ref[sends] = sums[sends].astype(send_ref.dtype)
                for copy in out_copies(turn_at):
                    copy.start()

            return carry

        lax.fori_loop(0, share // width, several, 0)

    add_part(jnp.int32(0), True)

    def more(part, carry):
        add_part(part, False)
        return carry

    lax.fori_loop(1, parts, more, 0)
    for turn_at in range(share // width):
        for copy in out_copies(turn_at):
            copy.wait()


def tile_chunk(owners, codes, own_rows, other_rows, occ_local, share):
    rows_total, domain = own_rows.shape
    groups = rows_total // GROUP
    held = GROUP // occ_local * CAP
    depth = 2 * groups * held
    tiles = (share, TILE, TILE)
    anywhere = pl.BlockSpec(memory_space=pl.ANY)
    in_smem = pl.BlockSpec(memory_space=pltpu.SMEM)
    return pl.pallas_call(
        functools.partial(chunk_kernel, occ_local, share),
        in_specs=[in_smem] * 3 + [anywhere] * 2,
        out_specs=[anywhere, anywhere],
        scratch_shapes=[
            pltpu.VMEM((2 * rows_total, domain), jnp.bfloat16),
            pltpu.VMEM((depth + PART, domain), jnp.bfloat16),
            pltpu.VMEM((domain + TILE, PART), jnp.bfloat16),
            pltpu.VMEM((2, held, GROUP), jnp.bfloat16),
            pltpu.VMEM((2 * share, TILE, TILE), jnp.float32),
            pltpu.VMEM(tiles, jnp.bfloat16),
            pltpu.SemaphoreType.DMA((2 * groups,)),
            pltpu.SemaphoreType.DMA((2, share)),
        ],
        out_shape=[
            jax.ShapeDtypeStruct(tiles, jnp.bfloat16),
            jax.ShapeDtypeStruct(tiles, jnp.float32),
        ],
        compiler_params=pltpu.CompilerParams(vmem_limit_bytes=56 * 1024 * 1024),
        cost_estimate=pl.CostEstimate(
            flops=4 * share * TILE * TILE * depth + 2 * depth * GROUP * domain,
            bytes_accessed=4 * rows_total * domain + 6 * share * TILE * TILE,
            transcendentals=0,
        ),
        name="tile_chunk",
    )(*owners, codes, own_rows, other_rows)


def block_columns(pair_codes, live, blocks):
    left = jnp.zeros_like(pair_codes)
    start = jnp.zeros_like(pair_codes)
    for block in range(1, blocks):
        first = block * blocks - block * (block - 1) // 2
        left = jnp.where(pair_codes >= first, block, left)
        start = jnp.where(pair_codes >= first, first, start)
    right = pair_codes - start + left
    left = jnp.where(lax.iota(jnp.int32, pair_codes.shape[0]) < live, left, blocks)
    return ((left << SHIFT) + right) * TILE


def tile_plan(half_tensor, batch_owner, pair_list, live_pairs):
    rows = lax.axis_size("row")
    aux_local, occ_local, domain = half_tensor.shape
    share = pair_list.shape[1] // rows
    orb_at = lax.axis_index("orb")
    inner = (orb_at == 1) | (orb_at == 2)
    swap = [(i, i ^ 1) for i in range(4)]
    step_a = [(0, 1), (3, 2), (1, 3), (2, 0)]
    step_b = [(0, 2), (3, 1), (1, 0), (2, 3)]

    def exchange(array, bits):
        return lax.ppermute(array, "row", [(i, i ^ bits) for i in range(rows)])

    def after(array, earlier):
        return lax.optimization_barrier((array, earlier))

    def over_x(send, keep):
        return keep + exchange(send, 2).astype(jnp.float32)

    own_rows = half_tensor.reshape(aux_local * occ_local, domain)
    other_rows = exchange(own_rows, 1)
    own_owner = batch_owner[:, 0]
    owners = own_owner, exchange(own_owner, 1)
    columns = block_columns(pair_list[0], live_pairs[0], domain // TILE)
    own_codes = jnp.concatenate([columns, orb_at[None]])
    far_codes = lax.ppermute(own_codes, "orb", [(i, i ^ 3) for i in range(4)])
    a_codes = lax.ppermute(own_codes, "orb", [(to, at) for at, to in step_a])
    b_codes = lax.ppermute(own_codes, "orb", [(to, at) for at, to in step_b])
    b_codes, a_codes, far_codes = lax.optimization_barrier((b_codes, a_codes, far_codes))

    def chunk(codes, other_rows):
        return tile_chunk(owners, codes, own_rows, other_rows, occ_local, share)

    far_send, far_keep = chunk(far_codes, other_rows)
    a_send, a_keep = chunk(a_codes, other_rows)
    far = over_x(far_send, far_keep).astype(jnp.bfloat16)
    other_rows, far = after(other_rows, far)
    far = lax.ppermute(far, "orb", swap).astype(jnp.float32)
    b_send, b_keep = chunk(b_codes, other_rows)
    a_term = over_x(a_send, a_keep) + jnp.where(inner, far, 0.0)
    other_rows, a_term = after(other_rows, a_term.astype(jnp.bfloat16))
    a_term = lax.ppermute(a_term, "orb", step_a)
    own_send, own_keep = chunk(own_codes, other_rows)
    b_keep, own_send = after(b_keep, own_send)
    b_term = over_x(b_send, b_keep) + jnp.where(inner, 0.0, far)
    b_term = lax.ppermute(b_term.astype(jnp.bfloat16), "orb", step_b)
    beside = a_term.astype(jnp.float32) + b_term.astype(jnp.float32)
    beside, own_keep = after(beside, own_keep)
    total = over_x(own_send, own_keep) + beside
    return total.astype(jnp.bfloat16)[None]


def per_device(half_tensor, batch_owner, pair_list, live_pairs):
    batches = lax.axis_size("orb")
    rows = lax.axis_size("row")
    aux_local, occ_local, domain = half_tensor.shape
    pair_total = pair_list.shape[1]
    tile_elements = batches * pair_total * TILE * TILE
    slab_elements = batches * CAP * aux_local * domain
    fits = (
        rows == ROWS
        and batches == 4
        and pair_total % rows == 0
        and occ_local & (occ_local - 1) == 0
        and GROUP % occ_local == 0
        and aux_local * occ_local % GROUP == 0
        and tile_elements <= slab_elements
    )
    plan = tile_plan if fits else slab_plan
    return plan(half_tensor, batch_owner, pair_list, live_pairs)


def solution(mesh):
    return jax.shard_map(
        per_device,
        mesh=mesh,
        in_specs=(
            P(("grp", "orb"), "row", None),
            P(("grp", "row"), None),
            P(("grp", "orb"), None),
            P(("grp", "orb")),
        ),
        out_specs=P(("grp", "orb"), "row", None, None),
        check_vma=False,
    )
```
